32 devices in a mesh: gy: 16 (over z, x, core), gz: 2 (over y).
Axes of the slice: x: 2, y: 2, z: 4, core: 2. Of those that a mesh axis runs over, the one named last changes fastest.
Arguments:
- velocity: float32 [3, 384, 1024], P(None, ('gy', 'gz')), may hold values from -6 to 6
- explicit: float32 [3, 384, 1024], P(None, ('gy', 'gz')), may hold values from -6 to 6
- bands: float32 [2, 5, 384], P(None, None, 'gy'), may hold values from -0.6 to 0.6
- inverse: float32 [384, 24, 512], P('gy', None, 'gz'), may hold values from -1.25 to 1.25
- spikes: float32 [2, 2, 384, 512], P(None, None, 'gy', 'gz'), may hold values from -1.4 to 1.4
Outputs:
- updated: float32 [3, 384, 1024], P(None, 'gy', 'gz')
The draws below stay inside these ranges and needn't reach their ends.
All inputs are finite; a program needn't handle non-finite values.
Results may differ from the reference program's by a relative error of at most 0.00024.
Values sent between devices are 32-bit elements; how exact they have to be, the bound alone decides.
No kernel may reach another device: no remote copies, remote signals or barrier semaphores. Data moves between devices by JAX's collectives and lax.ppermute only.
A program may use at most 64 MiB of HBM per device.

```python
import math
import jax
import jax.numpy as jnp
from jax import lax

NYD = 24
NY = 384
MODES = 512


def draw_spikes(key, part):
    base_key = jax.random.fold_in(key, 11)
    angle_key = jax.random.fold_in(key, 12)
    decay_key = jax.random.fold_in(key, 13)
    blocks = NY // NYD
    filler = jnp.clip(0.35 * jax.random.normal(base_key, (2, 2, NY, MODES), jnp.float32), -1.4, 1.4)
    low_rate = -1.0 / 10.0
    high_rate = -1.0 / 32.0
    angles = jax.random.uniform(angle_key, (2, blocks, MODES), jnp.float32, -math.pi, math.pi)
    radius = jnp.exp(jax.random.uniform(decay_key, (2, blocks, MODES), jnp.float32, low_rate, high_rate))
    cosine = jnp.repeat(radius * jnp.cos(angles), NYD, axis=1)
    sine_part = jnp.repeat(radius * jnp.sin(angles), NYD, axis=1)
    within = jnp.arange(NY) % NYD
    first_row = jnp.stack([within == NYD - 2, within == 0])
    second_row = jnp.stack([within == NYD - 1, within == 1])
    at_first = jnp.stack([cosine, -sine_part], axis=1)
    at_second = jnp.stack([sine_part, cosine], axis=1)
    result = jnp.where(first_row[:, None, :, None], at_first, filler)
    result = jnp.where(second_row[:, None, :, None], at_second, result)
    return result.astype(jnp.float32)


def shard_levels(key, extent, split, low, top_value):
    level, own = 1.0, jax.random.fold_in(key, 6)
    for position, blocks in split:
        draws = jnp.exp(jax.random.uniform(jax.random.fold_in(own, position), (blocks,), jnp.float32, low / len(split), top_value / len(split)))
        level = level * jnp.repeat(draws, extent[position] // blocks).reshape([-1 if axis == position else 1 for axis in range(len(extent))])
    return level


def scatter_about(rng, shape, width, reach, cuts=(), dtype=jnp.bfloat16):
    array = width * jax.random.normal(rng, shape, jnp.float32)
    if cuts:
        array = array * shard_levels(rng, shape, cuts, -0.22, 0.18)
    return jnp.clip(array, -reach, reach).astype(dtype)


def setup_inputs(seed: int = 0) -> dict:
    keys = jax.random.split(jax.random.key(seed), 6)
    velocity = scatter_about(keys[0], (3, NY, 2 * MODES), 1.0, 6.0, ((1, 32),), jnp.float32)
    explicit = scatter_about(keys[1], (3, NY, 2 * MODES), 1.0, 6.0, ((1, 32),), jnp.float32)
    bands = jnp.clip(jax.random.uniform(keys[2], (2, 5, NY), jnp.float32, -0.6, 0.6) * shard_levels(keys[2], (2, 5, NY), ((2, 16),), -0.4, 0.0), -0.6, 0.6)
    inverse = scatter_about(keys[3], (NY, NYD, MODES), NYD ** -0.5, 1.25, ((0, 16), (2, 2)), jnp.float32)
    spikes = draw_spikes(jax.random.fold_in(keys[5], 71), 0)
    return {"velocity": velocity, "explicit": explicit, "bands": bands, "inverse": inverse, "spikes": spikes}


def couple(spike, state):
    first = spike[..., 0, :, :][..., None, :, :, None] * state[..., :, 0, :, :][..., :, None, :, :]
    second = spike[..., 1, :, :][..., None, :, :, None] * state[..., :, 1, :, :][..., :, None, :, :]
    return first + second


def reference(velocity, explicit, bands, inverse, spikes):
    rows = velocity.shape[1]
    blocks = rows // NYD
    modes = inverse.shape[2]
    total = velocity + explicit
    pad_total = jnp.pad(total, ((0, 0), (2, 2), (0, 0)))
    pad_vel = jnp.pad(velocity, ((0, 0), (2, 2), (0, 0)))
    rhs = jnp.zeros(velocity.shape, jnp.float32)
    for offset in range(5):
        rhs = rhs + bands[0, offset][None, :, None] * pad_total[:, offset:offset + rows]
        rhs = rhs + bands[1, offset][None, :, None] * pad_vel[:, offset:offset + rows]
    rhs_blocks = rhs.reshape(3, blocks, NYD, modes, 2).transpose(1, 0, 2, 3, 4)
    inv_blocks = inverse.reshape(blocks, NYD, NYD, modes)
    lower = spikes[0].reshape(2, blocks, NYD, modes).transpose(1, 0, 2, 3)
    upper = spikes[1].reshape(2, blocks, NYD, modes).transpose(1, 0, 2, 3)

    def solve_block(pair):
        return jnp.einsum("rcm,fcmp->frmp", pair[0], pair[1], precision=lax.Precision.HIGHEST)

    local = lax.map(solve_block, (inv_blocks, rhs_blocks))

    def forward(state, pieces):
        zval = pieces[1] - couple(pieces[0], state)
        return zval[:, NYD - 2:], zval

    start = jnp.zeros((3, 2, modes, 2), jnp.float32)
    _, zvals = lax.scan(forward, start, (lower, local))

    def backward(state, pieces):
        xval = pieces[1] - couple(pieces[0], state)
        return xval[:, 0:2], xval

    _, xvals = lax.scan(backward, start, (upper, zvals), reverse=True)
    return xvals.transpose(1, 0, 2, 3, 4).reshape(3, rows, 2 * modes)
```

```python
import functools

import jax
import jax.numpy as jnp
from jax import lax
from jax.experimental import pallas as pl
from jax.experimental.pallas import tpu as pltpu
from jax.sharding import PartitionSpec as P

F32 = jnp.float32
BF16 = jnp.bfloat16
LANES = 128
HALO = 2


def vmem_call(body, out_shapes, args, scratch=(), flops=0, name=None):
    spec = pl.BlockSpec(memory_space=pltpu.VMEM)
    nbytes = sum(a.size * 4 for a in args)
    return pl.pallas_call(
        body,
        out_shape=[jax.ShapeDtypeStruct(s, F32) for s in out_shapes],
        in_specs=[spec] * len(args),
        out_specs=[spec] * len(out_shapes),
        scratch_shapes=list(scratch),
        compiler_params=pltpu.CompilerParams(vmem_limit_bytes=16 * 2**20),
        cost_estimate=pl.CostEstimate(flops=flops, bytes_accessed=nbytes, transcendentals=0),
        name=name,
    )(*args)


def window(rows, own, groups):
    for wide in range(8, rows + 1, 8):
        firsts = []
        for g in range(groups):
            low = max(g * own - HALO, 0)
            first = min(low // 8 * 8, rows - wide)
            if min(g * own + own + HALO, rows) > first + wide:
                break
            firsts.append(first)
        if len(firsts) == groups:
            return wide, firsts
    return rows, [0] * groups


def pick(values, index):
    result = jnp.int32(values[0])
    for i, value in enumerate(values[1:], 1):
        result = jnp.where(index == i, jnp.int32(value), result)
    return result


def exact_parts(x):
    high = x.astype(BF16)
    rest = x - high.astype(F32)
    mid = rest.astype(BF16)
    low = (rest - mid.astype(F32)).astype(BF16)
    return high, mid, low


def by_ones(x, ones):
    high, mid, low = exact_parts(x)
    dot = functools.partial(jnp.dot, preferred_element_type=F32)
    return dot(high, ones) + (dot(mid, ones) + dot(low, ones))


def doubled(x):
    row = lax.broadcasted_iota(jnp.int32, (LANES, 2 * LANES), 0)
    col = lax.broadcasted_iota(jnp.int32, (LANES, 2 * LANES), 1)
    ones = (row == lax.shift_right_logical(col, 1)).astype(F32).astype(BF16)
    parts = [by_ones(x[:, i : i + LANES], ones) for i in range(0, x.shape[1], LANES)]
    return jnp.concatenate(parts, axis=1)


def interleave_ones(back):
    a = lax.broadcasted_iota(jnp.int32, (2 * LANES, 2 * LANES), 1 if back else 0)
    b = lax.broadcasted_iota(jnp.int32, (2 * LANES, 2 * LANES), 0 if back else 1)
    place = 2 * (b % LANES) + b // LANES
    return (a == place).astype(F32).astype(BF16)


def edges_kernel(groups, velocity, explicit, out):
    g = lax.axis_index("gz")
    own = velocity.shape[1]
    head = pl.ds(0, HALO)
    tail = pl.ds(own - HALO, HALO)
    for f in range(3):
        for row, which in ((f, None), (f + 3, explicit)):
            top, bottom = velocity[f, head], velocity[f, tail]
            if which is not None:
                top, bottom = top + which[f, head], bottom + which[f, tail]
            out[row] = jnp.where(g == 0, top, bottom)


def prepare_kernel(bands, spikes, inverse, maps, lu, inv4, coef, square):
    rows = inverse.shape[1]
    lu2 = doubled(spikes[...].reshape(4 * rows, -1))
    lu[...] = lu2.reshape(lu.shape)
    for k in range(2):
        for j in range(2):
            maps[2 * k + j : 2 * k + j + 1] = -lu[0, j, rows - 2 + k : rows - 1 + k]
            maps[4 + 2 * k + j : 5 + 2 * k + j] = -lu[0, j, k : k + 1]
            maps[8 + 2 * k + j : 9 + 2 * k + j] = -lu[1, j, k : k + 1]
    near = jnp.concatenate([inverse[0:2], inverse[rows - 2 : rows]], axis=0)
    inv4[...] = doubled(near.reshape(4 * rows, -1)).reshape(inv4.shape)
    square[...] = jnp.zeros_like(square)
    square[0:5, 0:rows] = bands[0]
    square[8:13, 0:rows] = bands[1]
    turned = jnp.transpose(square[...])
    for a in range(2):
        for d in range(5):
            column = turned[0:rows, 8 * a + d : 8 * a + d + 1]
            coef[5 * a + d] = jnp.broadcast_to(column, (rows, LANES))


def stencil_kernel(wide, firsts, velocity, explicit, halo, coef, *refs):
    outs, (vel, tot) = refs[:-2], refs[-2:]
    groups = len(firsts)
    own, lanes = velocity.shape[1:]
    rows = coef.shape[1]
    part = lanes // groups
    g = lax.axis_index("gz")
    gy, count = lax.axis_index("gy"), lax.axis_size("gy")
    vel[...] = jnp.zeros_like(vel)
    tot[...] = jnp.zeros_like(tot)
    for k in range(groups):
        base = 8 + k * own - firsts[k]

        @pl.when(g == k)
        def _(base=base):
            for f in range(3):
                vel[f, base : base + own] = velocity[f]
                tot[f, base : base + own] = velocity[f] + explicit[f]

    first = pl.multiple_of(pick(firsts, g), 8)
    weights = [coef[i, pl.ds(first, wide)] for i in range(10)]
    below = (g == 0) & (gy < count - 1)
    above = (g == groups - 1) & (gy > 0)

    def beside(low, high):
        chosen = []
        for kind in (5, 0):
            one = 0.0 if high is None else coef[kind + high[0], high[1] : high[1] + 1]
            two = 0.0 if low is None else coef[kind + low[0], low[1] : low[1] + 1]
            chosen.append(jnp.where(below, one, jnp.where(above, two, jnp.zeros((1, LANES), F32))))
        return chosen

    sides = [
        [beside((0, 0), (4, rows - 2)), beside((1, 0), None)],
        [beside(None, (3, rows - 1)), beside((0, 1), (4, rows - 1))],
    ]
    for shift, out in enumerate(outs):
        begin = lax.rem(g + shift, groups) * part
        for lane in range(0, part, LANES):
            at = pl.ds(pl.multiple_of(begin + lane, LANES), LANES)
            to = pl.ds(lane, LANES)
            for f in range(3):
                total = None
                for d in range(5):
                    low = pl.ds(8 + d - 2, wide)
                    term = weights[d] * tot[f, low, at] + weights[5 + d] * vel[f, low, at]
                    total = term if total is None else total + term
                out[f * wide : f * wide + wide, to] = total
                for i in range(2):
                    total = None
                    for j in range(2):
                        term = sides[i][j][0] * halo[f, j : j + 1, at] + sides[i][j][1] * halo[f + 3, j : j + 1, at]
                        total = term if total is None else total + term
                    row = 3 * wide + 2 * f + i
                    out[row : row + 1, to] = total


def interface_kernel(wide, firsts, inv4, maps, *refs):
    groups = len(firsts)
    pieces, (rhs, message) = refs[:groups], refs[groups:]
    rows = rhs.shape[1]
    g = lax.axis_index("gz")
    rhs[...] = jnp.zeros_like(rhs)
    for shift, piece in enumerate(pieces):
        source = lax.rem(g - shift + groups, groups)
        at = pl.ds(pl.multiple_of(pick(firsts, source), 8), wide)
        for f in range(3):
            rhs[f, at] += piece[f * wide : f * wide + wide]
            side = piece[3 * wide + 2 * f : 3 * wide + 2 * f + 2]
            rhs[f, 0:2] += jnp.where(source == groups - 1, side, 0.0)
            rhs[f, rows - 2 : rows] += jnp.where(source == 0, side, 0.0)
    for f in range(3):
        for r in range(4):
            value = jnp.sum(inv4[r] * rhs[f], axis=0, keepdims=True)
            row = (6 if r < 2 else 0) + 3 * (r % 2) + f
            message[row : row + 1] = value
    message[12:24] = maps[...]


class Piece:
    def __init__(self, ref):
        self.p = [ref[0:3], ref[3:6]]
        self.q = [ref[6:9], ref[9:12]]
        grid = lambda at: [[ref[at + 2 * k + j : at + 2 * k + j + 1] for j in range(2)] for k in range(2)]
        self.F, self.H, self.G = grid(12), grid(16), grid(20)


def act(matrix, vector, plus=None):
    out = [matrix[k][0] * vector[0] + matrix[k][1] * vector[1] for k in range(2)]
    return out if plus is None else [plus[k] + out[k] for k in range(2)]


def times(a, b, plus=None):
    out = [[a[k][0] * b[0][j] + a[k][1] * b[1][j] for j in range(2)] for k in range(2)]
    return out if plus is None else [[plus[k][j] + out[k][j] for j in range(2)] for k in range(2)]


def after(state, piece):
    if state is None:
        return piece.p, piece.F
    return act(piece.F, state[0], piece.p), times(piece.F, state[1])


def before(piece, state):
    if state is None:
        return piece.q, piece.H, piece.G
    q, H, G = state
    q = act(piece.G, act(H, piece.p, q), piece.q)
    H = times(piece.G, times(H, piece.F), piece.H)
    return q, H, times(piece.G, G)


def choose(flag, new, old):
    return jax.tree.map(lambda a, b: jnp.where(flag, a, b), new, old)


def store_vector(ref, at, vector):
    ref[at : at + 3] = vector[0]
    ref[at + 3 : at + 6] = vector[1]


def store_matrix(ref, at, matrix):
    for k in range(2):
        for j in range(2):
            ref[at + 2 * k + j : at + 2 * k + j + 1] = matrix[k][j]


def sorted_pieces(base, pieces, board):
    size = len(pieces)
    position = lax.rem(lax.div(lax.axis_index("gy"), base), size)
    for x, piece in enumerate(pieces):
        board[jnp.bitwise_xor(position, x)] = piece[...]
    return position, [Piece(board.at[i]) for i in range(size)]


def compose_kernel(base, *refs):
    *pieces, out, board = refs
    _, run = sorted_pieces(base, pieces, board)
    up = down = None
    for piece in run:
        up = after(up, piece)
    for piece in run[::-1]:
        down = before(piece, down)
    store_vector(out, 0, up[0])
    store_vector(out, 6, down[0])
    store_matrix(out, 12, up[1])
    store_matrix(out, 16, down[1])
    store_matrix(out, 20, down[2])


def around(base, pieces, board):
    position, run = sorted_pieces(base, pieces, board)
    mine = Piece(pieces[0])
    one, none = jnp.ones_like(mine.F[0][0]), jnp.zeros_like(mine.F[0][0])
    zero = jnp.zeros_like(mine.p[0])
    unit = [[one, none], [none, one]]
    blank = [[none, none], [none, none]]
    up = ([zero, zero], unit)
    for i, piece in enumerate(run[:-1]):
        up = choose(i < position, after(up, piece), up)
    down = ([zero, zero], blank, unit)
    for i in range(len(run) - 1, 0, -1):
        down = choose(i > position, before(run[i], down), down)
    return mine, up, down


def widen(base, pieces, board, known):
    mine, (pl_, Fl), (q, H, G) = around(base, pieces, board)
    top = act(mine.F, pl_, mine.p)
    e = act(H, top, q)
    E = times(H, times(mine.F, Fl))
    if known is None:
        return pl_, Fl, e, E, G
    a, A, b, B, D = known
    return (
        act(A, pl_, a),
        times(A, Fl),
        act(D, e, act(B, pl_, b)),
        times(D, E, times(B, Fl)),
        times(D, G),
    )


def read_known(ref):
    piece = Piece(ref)
    return piece.p, piece.F, piece.q, piece.H, piece.G


def widen_kernel(base, start, *refs):
    *pieces, out, board = refs
    known = None
    if not start:
        known = read_known(pieces.pop())
    a, A, b, B, D = widen(base, pieces, board, known)
    store_vector(out, 0, a)
    store_vector(out, 6, b)
    store_matrix(out, 12, A)
    store_matrix(out, 16, B)
    store_matrix(out, 20, D)


def block_kernel(inverse, rhs, local, split, solved):
    fields, rows, lanes = rhs.shape
    apart, together = interleave_ones(False), interleave_ones(True)
    flat = rhs[...].reshape(fields * rows, lanes)
    for at in range(0, lanes, 2 * LANES):
        turned = by_ones(flat[:, at : at + 2 * LANES], apart)
        split[:, :, at : at + 2 * LANES] = turned.reshape(fields, rows, 2 * LANES)
    for tile in range(lanes // (2 * LANES)):
        modes = pl.ds(tile * LANES, LANES)
        for f in range(fields):
            for p in range(2):
                at = pl.ds((2 * tile + p) * LANES, LANES)
                value = split[f, :, at]
                solved[f, :, at] = jnp.sum(inverse[:, :, modes] * value[None], axis=1)
    flat = solved[...].reshape(fields * rows, lanes)
    for at in range(0, lanes, 2 * LANES):
        turned = by_ones(flat[:, at : at + 2 * LANES], together)
        local[:, :, at : at + 2 * LANES] = turned.reshape(fields, rows, 2 * LANES)


def final_kernel(base, start, local, lu, *refs):
    *pieces, out, board = refs
    known = None
    if not start:
        known = read_known(pieces.pop())
    t, _, s, _, _ = widen(base, pieces, board, known)
    for f in range(3):
        value = local[f]
        for k in range(2):
            value = value - lu[0, k] * t[k][f : f + 1] - lu[1, k] * s[k][f : f + 1]
        out[f] = value


def ring_halo(gy, gz):
    at = lambda y, z: y * gz + z
    pairs = []
    for y in range(gy):
        for z in range(gz):
            if gz == 1:
                continue
            if z == gz - 1:
                pairs.append((at(y, z), at(y + 1, z) if y < gy - 1 else at(y, 0)))
            elif z == 0:
                pairs.append((at(y, z), at(y - 1, z) if y > 0 else at(y, gz - 1)))
    return pairs


def groups_of(count):
    steps, base = [], 1
    while base < count:
        size = 4 if base > 1 and base * 4 <= count else 2
        steps.append((base, size))
        base *= size
    return steps


def per_device(velocity, explicit, bands, inverse, spikes):
    gy, gz = lax.axis_size("gy"), lax.axis_size("gz")
    own, columns = velocity.shape[1:]
    rows, modes = inverse.shape[0], inverse.shape[2]
    lanes = 2 * modes
    wide, firsts = window(rows, own, gz)

    (edges,) = vmem_call(
        functools.partial(edges_kernel, gz), [(6, HALO, columns)], [velocity, explicit], name="edges"
    )
    halo = lax.ppermute(edges, ("gy", "gz"), ring_halo(gy, gz))
    maps, lu, inv4, coef = vmem_call(
        prepare_kernel,
        [(12, lanes), (2, 2, rows, lanes), (4, rows, lanes), (10, rows, LANES)],
        [bands, spikes, inverse],
        scratch=[pltpu.VMEM((LANES, LANES), F32)],
        flops=2 * 10**8,
        name="prepare",
    )
    padded = pltpu.VMEM((3, wide + 24, columns), F32)
    shares = vmem_call(
        functools.partial(stencil_kernel, wide, firsts),
        [(3 * wide + 8, lanes)] * gz,
        [velocity, explicit, halo, coef],
        scratch=[padded, padded],
        name="stencil",
    )
    pieces = [shares[0]]
    for shift in range(1, gz):
        ring = [(i, (i + shift) % gz) for i in range(gz)]
        pieces.append(lax.ppermute(shares[shift], "gz", ring))
    rhs, message = vmem_call(
        functools.partial(interface_kernel, wide, firsts),
        [(3, rows, lanes), (24, lanes)],
        [inv4, maps, *pieces],
        name="interface",
    )

    known, local = None, None
    steps = groups_of(gy)
    for number, (base, size) in enumerate(steps):
        gathered = [message]
        for x in range(1, size):
            mask = x * base if number == 0 else (x * base) | 1
            gathered.append(lax.ppermute(message, "gy", [(i, i ^ mask) for i in range(gy)]))
        board = [pltpu.VMEM((size, 24, lanes), F32)]
        have = [] if known is None else [known]
        if number == 1 or len(steps) == 1:
            (local,) = vmem_call(
                block_kernel,
                [(3, rows, lanes)],
                [inverse, rhs],
                scratch=[pltpu.VMEM((3, rows, lanes), F32)] * 2,
                flops=2 * 10**8,
                name="block",
            )
        if number == len(steps) - 1:
            (out,) = vmem_call(
                functools.partial(final_kernel, base, known is None),
                [(3, rows, lanes)],
                [local, lu, *gathered, *have],
                scratch=board,
                name="final",
            )
            return out
        (message,) = vmem_call(
            functools.partial(compose_kernel, base), [(24, lanes)], gathered, scratch=board, name="compose"
        )
        (known,) = vmem_call(
            functools.partial(widen_kernel, base, known is None),
            [(24, lanes)],
            [*gathered, *have],
            scratch=board,
            flops=10**7,
            name="widen",
        )


def solution(mesh):
    placed = (
        P(None, ("gy", "gz"), None),
        P(None, ("gy", "gz"), None),
        P(None, None, "gy"),
        P("gy", None, "gz"),
        P(None, None, "gy", "gz"),
    )
    return jax.shard_map(
        per_device, mesh=mesh, in_specs=placed, out_specs=P(None, "gy", "gz"), check_vma=False
    )
```

```python
import functools

import jax
import jax.numpy as jnp
from jax import lax
from jax.experimental import pallas as pl
from jax.experimental.pallas import tpu as pltpu
from jax.sharding import PartitionSpec as P

F32 = jnp.float32
BF16 = jnp.bfloat16
LANES = 128
HALO = 2


def vmem_call(body, out_shapes, args, scratch=(), flops=0, name=None, far=0, far_out=False):
    near, away = pl.BlockSpec(memory_space=pltpu.VMEM), pl.BlockSpec(memory_space=pltpu.HBM)
    nbytes = sum(a.size * 4 for a in args)
    args = [pltpu.with_memory_space_constraint(a, pltpu.HBM) for a in args[:far]] + args[far:]
    return pl.pallas_call(
        body,
        out_shape=[jax.ShapeDtypeStruct(s, F32) for s in out_shapes],
        in_specs=[away] * far + [near] * (len(args) - far),
        out_specs=[away if far_out else near] * len(out_shapes),
        scratch_shapes=list(scratch),
        compiler_params=pltpu.CompilerParams(vmem_limit_bytes=16 * 2**20),
        cost_estimate=pl.CostEstimate(flops=flops, bytes_accessed=nbytes, transcendentals=0),
        name=name,
    )(*args)


def window(rows, own, groups):
    spans = [(max(g * own - HALO, 0), min(g * own + own + HALO, rows)) for g in range(groups)]
    wide = max(high - low for low, high in spans)
    return wide, [min(low, rows - wide) for low, _ in spans]


def exact_parts(x):
    high = x.astype(BF16)
    rest = x - high.astype(F32)
    mid = rest.astype(BF16)
    low = (rest - mid.astype(F32)).astype(BF16)
    return high, mid, low


def by_ones(x, ones):
    high, mid, low = exact_parts(x)
    dot = functools.partial(jnp.dot, preferred_element_type=F32)
    return dot(high, ones) + (dot(mid, ones) + dot(low, ones))


def doubled(x):
    row = lax.broadcasted_iota(jnp.int32, (LANES, 2 * LANES), 0)
    col = lax.broadcasted_iota(jnp.int32, (LANES, 2 * LANES), 1)
    ones = (row == lax.shift_right_logical(col, 1)).astype(F32).astype(BF16)
    parts = [by_ones(x[:, i : i + LANES], ones) for i in range(0, x.shape[1], LANES)]
    return jnp.concatenate(parts, axis=1)


def interleave_ones(back):
    a = lax.broadcasted_iota(jnp.int32, (2 * LANES, 2 * LANES), 1 if back else 0)
    b = lax.broadcasted_iota(jnp.int32, (2 * LANES, 2 * LANES), 0 if back else 1)
    place = 2 * (b % LANES) + b // LANES
    return (a == place).astype(F32).astype(BF16)


def side_weights(coef, upper):
    rows = coef.shape[1]
    if upper:
        taps = [[(4, rows - 2), None], [(3, rows - 1), (4, rows - 1)]]
    else:
        taps = [[(0, 0), (1, 0)], [None, (0, 1)]]
    none = jnp.zeros((1, LANES), F32)
    get = lambda tap, kind: none if tap is None else coef[2 * tap[0] + kind, tap[1] : tap[1] + 1]
    return [[[get(tap, kind) for kind in range(2)] for tap in row] for row in taps]


def beside(weights, planes):
    return [
        sum(weights[i][j][kind] * planes(kind, j) for j in range(2) for kind in range(2)) for i in range(2)
    ]


def planes_of(ref, at):
    return lambda kind, j: ref[at + 6 * kind + 3 * j : at + 6 * kind + 3 * j + 3]


def stencil_kernel(wide, firsts, velocity, explicit, bands, *refs):
    groups = len(firsts)
    outs, (edges, coef, here, there, taps, square, weight, vel, tot, sems) = refs[:groups], refs[groups:]
    own, lanes = velocity.shape[1:]
    rows = coef.shape[1]
    part = lanes // groups
    g = lax.axis_index("gz")
    copies = [
        pltpu.make_async_copy(source, target, sems.at[i])
        for i, (source, target) in enumerate(((bands, taps), (velocity, here), (explicit, there)))
    ]
    for copy in copies:
        copy.start()
    square[...] = jnp.zeros_like(square)
    vel[...] = jnp.zeros_like(vel)
    tot[...] = jnp.zeros_like(tot)
    copies[0].wait()
    for d in range(5):
        square[2 * d : 2 * d + 2, 0:rows] = taps[d]
    turned = jnp.transpose(square[...])
    for i in range(10):
        coef[i] = jnp.broadcast_to(turned[0:rows, i : i + 1], (rows, LANES))
    copies[1].wait()
    copies[2].wait()
    for k in range(groups):
        base = 8 + k * own - firsts[k]

        @pl.when(g == k)
        def _(base=base, first=firsts[k]):
            for i in range(10):
                weight[i] = coef[i, first : first + wide]
            for f in range(3):
                vel[f, base : base + own] = here[f]
                tot[f, base : base + own] = here[f] + there[f]

    for f in range(3):
        for j in range(HALO):
            top, bottom = here[f, j : j + 1], here[f, own - HALO + j : own - HALO + j + 1]
            edges[6 + 3 * j + f : 7 + 3 * j + f] = jnp.where(g == 0, top, bottom)
            top += there[f, j : j + 1]
            bottom += there[f, own - HALO + j : own - HALO + j + 1]
            edges[3 * j + f : 3 * j + f + 1] = jnp.where(g == 0, top, bottom)
    weights = [weight[i] for i in range(10)]
    for shift in range(groups - 1, -1, -1):
        out = outs[shift]
        begin = lax.rem(g + shift, groups) * part
        for lane in range(0, part, LANES):
            at = pl.ds(pl.multiple_of(begin + lane, LANES), LANES)
            to = pl.ds(lane, LANES)
            for f in range(3):
                total = None
                for d in range(5):
                    low = pl.ds(8 + d - 2, wide)
                    term = weights[2 * d] * tot[f, low, at] + weights[2 * d + 1] * vel[f, low, at]
                    total = term if total is None else total + term
                out[f * wide : f * wide + wide, to] = total
            out[3 * wide : 3 * wide + 12, to] = edges[0:12, at]


def relay_kernel(groups, edges, beside_edges, *outs):
    core = lax.rem(lax.axis_index("gy"), 2)
    mine = jnp.where(lax.axis_index("gz") == 0, core == 0, core == 1)
    part = edges.shape[1] // groups
    for step, out in enumerate(outs):
        begin = (2 * step + 1 - core) * part
        for lane in range(0, part, LANES):
            at = pl.ds(pl.multiple_of(begin + lane, LANES), LANES)
            out[:, lane : lane + LANES] = jnp.where(mine, edges[:, at], beside_edges[:, at])


def prepare_kernel(spikes, inverse, coef, lu, inv4, fixed, outer, inside, near, sems):
    rows = inverse.shape[1]
    lanes = lu.shape[3]
    core = lax.rem(lax.axis_index("gy"), 2)
    gy, count = lax.axis_index("gy"), lax.axis_size("gy")
    copies = [
        pltpu.make_async_copy(spikes, near, sems.at[0]),
        pltpu.make_async_copy(inverse, inside, sems.at[1]),
    ]
    for copy in copies:
        copy.start()
    wide = lambda row: jnp.concatenate([row] * (lanes // LANES), axis=1)
    lower, upper = side_weights(coef, False), side_weights(coef, True)
    used = jnp.where(core == 0, gy > 0, gy < count - 1)
    for i in range(2):
        for j in range(2):
            for kind in range(2):
                at = 4 * i + 2 * j + kind
                low, high = lower[i][j][kind], upper[i][j][kind]
                fixed[20 + at : 21 + at] = wide(jnp.where(core == 0, high, low))
                outer[at : at + 1] = wide(jnp.where(used, jnp.where(core == 0, low, high), 0.0))
    copies[0].wait()
    lu[...] = doubled(near[...].reshape(4 * rows, -1)).reshape(lu.shape)
    for k in range(2):
        for j in range(2):
            fixed[2 * k + j : 2 * k + j + 1] = -lu[0, j, rows - 2 + k : rows - 1 + k]
            fixed[4 + 2 * k + j : 5 + 2 * k + j] = -lu[0, j, k : k + 1]
            fixed[8 + 2 * k + j : 9 + 2 * k + j] = -lu[1, j, k : k + 1]
    copies[1].wait()
    ends = jnp.concatenate([inside[0:2], inside[rows - 2 : rows]], axis=0)
    inv4[...] = doubled(ends.reshape(4 * rows, -1)).reshape(inv4.shape)
    for k in range(4):
        for i in range(2):
            low, high = inv4[k, i : i + 1], inv4[k, rows - 2 + i : rows - 1 + i]
            at = 12 + 2 * ((k + 2) % 4) + i
            fixed[at : at + 1] = jnp.where(core == 0, high, low)


def rows_of(ref, at):
    return [[[ref[at + 4 * i + 2 * j + kind : at + 4 * i + 2 * j + kind + 1] for kind in range(2)] for j in range(2)] for i in range(2)]


def interface_kernel(wide, firsts, inv4, fixed, outer, *refs):
    groups = len(firsts)
    pieces, ends, (rhs, message) = refs[:groups], refs[groups:-2], refs[-2:]
    rows = rhs.shape[1]
    g = lax.axis_index("gz")
    core = lax.rem(lax.axis_index("gy"), 2)
    rhs[...] = jnp.zeros_like(rhs)
    for shift, piece in enumerate(pieces):
        source = lax.rem(g - shift + groups, groups)
        for k in range(groups):

            @pl.when(source == k)
            def _(piece=piece, k=k):
                for f in range(3):
                    rhs[f, firsts[k] : firsts[k] + wide] += piece[f * wide : f * wide + wide]
                if k in (0, groups - 1):

                    @pl.when(core == (1 if k == 0 else 0))
                    def _():
                        message[24:36] = piece[3 * wide : 3 * wide + 12]

    end = ends[0][...]
    for step in range(1, len(ends)):
        end = jnp.where(g // 2 == step, ends[step][...], end)
    side = beside(rows_of(outer, 0), lambda kind, j: end[6 * kind + 3 * j : 6 * kind + 3 * j + 3])
    low = [jnp.where(core == 0, side[i], 0.0) for i in range(2)]
    high = [jnp.where(core == 0, 0.0, side[i]) for i in range(2)]
    for f in range(3):
        for i in range(2):
            rhs[f, i : i + 1] += low[i][f : f + 1]
            rhs[f, rows - 2 + i : rows - 1 + i] += high[i][f : f + 1]
    for f in range(3):
        for r in range(4):
            value = jnp.sum(inv4[r] * rhs[f], axis=0, keepdims=True)
            row = (6 if r < 2 else 0) + 3 * (r % 2) + f
            message[row : row + 1] = value
    message[12:24] = fixed[0:12]
    message[36:52] = fixed[12:28]


class Piece:
    def __init__(self, ref):
        self.p = [ref[0:3], ref[3:6]]
        self.q = [ref[6:9], ref[9:12]]
        grid = lambda at: [[ref[at + 2 * k + j : at + 2 * k + j + 1] for j in range(2)] for k in range(2)]
        self.F, self.H, self.G = grid(12), grid(16), grid(20)


def act(matrix, vector, plus=None):
    out = [matrix[k][0] * vector[0] + matrix[k][1] * vector[1] for k in range(2)]
    return out if plus is None else [plus[k] + out[k] for k in range(2)]


def times(a, b, plus=None):
    out = [[a[k][0] * b[0][j] + a[k][1] * b[1][j] for j in range(2)] for k in range(2)]
    return out if plus is None else [[plus[k][j] + out[k][j] for j in range(2)] for k in range(2)]


def after(state, piece):
    if state is None:
        return piece.p, piece.F
    return act(piece.F, state[0], piece.p), times(piece.F, state[1])


def before(piece, state):
    if state is None:
        return piece.q, piece.H, piece.G
    q, H, G = state
    q = act(piece.G, act(H, piece.p, q), piece.q)
    H = times(piece.G, times(H, piece.F), piece.H)
    return q, H, times(piece.G, G)


def choose(flag, new, old):
    return jax.tree.map(lambda a, b: jnp.where(flag, a, b), new, old)


def store_vector(ref, at, vector):
    ref[at : at + 3] = vector[0]
    ref[at + 3 : at + 6] = vector[1]


def store_matrix(ref, at, matrix):
    for k in range(2):
        for j in range(2):
            ref[at + 2 * k + j : at + 2 * k + j + 1] = matrix[k][j]


def sorted_pieces(base, pieces, board):
    size = len(pieces)
    position = lax.rem(lax.div(lax.axis_index("gy"), base), size)
    for x, piece in enumerate(pieces):
        board[jnp.bitwise_xor(position, x)] = piece[...]
    return position, [Piece(board.at[i]) for i in range(size)]


def compose_kernel(base, *refs):
    *pieces, out, board = refs
    _, run = sorted_pieces(base, pieces, board)
    up = down = None
    for piece in run:
        up = after(up, piece)
    for piece in run[::-1]:
        down = before(piece, down)
    store_vector(out, 0, up[0])
    store_vector(out, 6, down[0])
    store_matrix(out, 12, up[1])
    store_matrix(out, 16, down[1])
    store_matrix(out, 20, down[2])


def pair_kernel(mine, other, out, fixed_mine, fixed_other):
    core = lax.rem(lax.axis_index("gy"), 2)
    both = []
    for ref, near, target in ((mine, other, fixed_mine), (other, mine, fixed_other)):
        side = beside(rows_of(ref, 44), planes_of(near, 24))
        target[12:24] = ref[12:24]
        for k in range(4):
            value = ref[3 * k : 3 * k + 3]
            for i in range(2):
                value = value + ref[36 + 2 * k + i : 37 + 2 * k + i] * side[i]
            target[3 * k : 3 * k + 3] = value
    low, high = (
        [jnp.where(core == i, fixed_mine[...], fixed_other[...])] for i in range(2)
    )
    low, high = Piece(low[0]), Piece(high[0])
    up, down = after(after(None, low), high), before(low, before(high, None))
    store_vector(out, 0, up[0])
    store_vector(out, 6, down[0])
    store_matrix(out, 12, up[1])
    store_matrix(out, 16, down[1])
    store_matrix(out, 20, down[2])


def around(base, pieces, board):
    position, run = sorted_pieces(base, pieces, board)
    mine = Piece(pieces[0])
    one, none = jnp.ones_like(mine.F[0][0]), jnp.zeros_like(mine.F[0][0])
    zero = jnp.zeros_like(mine.p[0])
    unit = [[one, none], [none, one]]
    blank = [[none, none], [none, none]]
    up = ([zero, zero], unit)
    for i, piece in enumerate(run[:-1]):
        up = choose(i < position, after(up, piece), up)
    down = ([zero, zero], blank, unit)
    for i in range(len(run) - 1, 0, -1):
        down = choose(i > position, before(run[i], down), down)
    return mine, up, down


def widen(base, pieces, board, known):
    mine, (pl_, Fl), (q, H, G) = around(base, pieces, board)
    top = act(mine.F, pl_, mine.p)
    e = act(H, top, q)
    E = times(H, times(mine.F, Fl))
    if known is None:
        return pl_, Fl, e, E, G
    a, A, b, B, D = known
    return (
        act(A, pl_, a),
        times(A, Fl),
        act(D, e, act(B, pl_, b)),
        times(D, E, times(B, Fl)),
        times(D, G),
    )


def read_known(ref):
    piece = Piece(ref)
    return piece.p, piece.F, piece.q, piece.H, piece.G


def widen_kernel(base, start, *refs):
    *pieces, out, board = refs
    known = None
    if not start:
        known = read_known(pieces.pop())
    a, A, b, B, D = widen(base, pieces, board, known)
    store_vector(out, 0, a)
    store_vector(out, 6, b)
    store_matrix(out, 12, A)
    store_matrix(out, 16, B)
    store_matrix(out, 20, D)


def block_kernel(inverse, rhs, mine, other, local, split, solved):
    fields, rows, lanes = rhs.shape
    core = lax.rem(lax.axis_index("gy"), 2)
    side = beside(rows_of(mine, 44), planes_of(other, 24))
    local[...] = rhs[...]
    for f in range(fields):
        for i in range(2):
            value = side[i][f : f + 1]
            local[f, i : i + 1] += jnp.where(core == 0, 0.0, value)
            local[f, rows - 2 + i : rows - 1 + i] += jnp.where(core == 0, value, 0.0)
    apart, together = interleave_ones(False), interleave_ones(True)
    flat = local[...].reshape(fields * rows, lanes)
    for at in range(0, lanes, 2 * LANES):
        turned = by_ones(flat[:, at : at + 2 * LANES], apart)
        split[:, :, at : at + 2 * LANES] = turned.reshape(fields, rows, 2 * LANES)
    for tile in range(lanes // (2 * LANES)):
        modes = pl.ds(tile * LANES, LANES)
        for f in range(fields):
            for p in range(2):
                at = pl.ds((2 * tile + p) * LANES, LANES)
                value = split[f, :, at]
                solved[f, :, at] = jnp.sum(inverse[:, :, modes] * value[None], axis=1)
    flat = solved[...].reshape(fields * rows, lanes)
    for at in range(0, lanes, 2 * LANES):
        turned = by_ones(flat[:, at : at + 2 * LANES], together)
        local[:, :, at : at + 2 * LANES] = turned.reshape(fields, rows, 2 * LANES)


def last_message_kernel(base, composed, out):
    upper = lax.rem(lax.div(lax.axis_index("gy"), base), 2) == 1
    out[0:6] = jnp.where(upper, composed[6:12], composed[0:6])
    out[6:10] = composed[16:20]


def ready_kernel(base, local, lu, known, ready, lift):
    upper = lax.rem(lax.div(lax.axis_index("gy"), base), 2) == 1
    a, A, b, B, D = read_known(known)
    for f in range(3):
        value = local[f]
        for k in range(2):
            value = value - lu[0, k] * a[k][f : f + 1] - lu[1, k] * b[k][f : f + 1]
        ready[f] = value
    for j in range(2):
        value = jnp.zeros_like(lift[j])
        for k in range(2):
            through_t = lu[0, k] * A[k][j] + lu[1, k] * B[k][j]
            value = value - jnp.where(upper, through_t, lu[1, k] * D[k][j])
        lift[j] = value


def final_kernel(base, ready, lift, composed, received, out, held, sems):
    upper = lax.rem(lax.div(lax.axis_index("gy"), base), 2) == 1
    mine = [composed[0:3], composed[3:6]]
    theirs = [received[0:3], received[3:6]]
    H = [[received[6 + 2 * k + j : 7 + 2 * k + j] for j in range(2)] for k in range(2)]
    state = choose(upper, theirs, act(H, mine, theirs))
    copies = []
    for f in range(3):
        held[f] = ready[f] + lift[0] * state[0][f : f + 1] + lift[1] * state[1][f : f + 1]
        copies.append(pltpu.make_async_copy(held.at[f], out.at[f], sems.at[f]))
        copies[-1].start()
    for copy in copies:
        copy.wait()


def end_pairs(gy, gz, step):
    at = lambda y, z: y * gz + z
    pairs = []
    for y in range(1, gy - 1, 2):
        pairs.append((at(y, gz - 1), at(y + 1, 2 * step)))
        pairs.append((at(y - 1, gz - 1), at(y + 1, 2 * step + 1)))
        pairs.append((at(y + 1, 0), at(y, 2 * step + 1)))
        pairs.append((at(y + 2, 0), at(y, 2 * step)))
    sources = sorted(set(range(gy * gz)) - {s for s, _ in pairs})
    targets = sorted(set(range(gy * gz)) - {t for _, t in pairs})
    if gz == 2:
        for i in range(0, len(sources), 2):
            pairs += [(sources[i], targets[i + 1]), (sources[i + 1], targets[i])]
    return pairs


def groups_of(count):
    steps, base = [(1, 2)], 2
    while 2 * base < count:
        size = 4 if base * 8 <= count else 2
        steps.append((base, size))
        base *= size
    return steps + [(base, 2)]


def per_device(velocity, explicit, bands, inverse, spikes):
    gy, gz = lax.axis_size("gy"), lax.axis_size("gz")
    own, columns = velocity.shape[1:]
    rows, modes = inverse.shape[0], inverse.shape[2]
    lanes = 2 * modes
    wide, firsts = window(rows, own, gz)
    vmem = lambda *shape: pltpu.VMEM(shape, F32)
    dma = lambda n: pltpu.SemaphoreType.DMA((n,))

    high = -(-(3 * wide + 12) // 8) * 8
    *shares, edges, coef = vmem_call(
        functools.partial(stencil_kernel, wide, firsts),
        [(high, lanes)] * gz + [(12, columns), (10, rows, LANES)],
        [velocity, explicit, jnp.transpose(bands, (1, 0, 2))],
        scratch=[vmem(3, own, columns)] * 2
        + [vmem(5, 2, rows), vmem(LANES, LANES), vmem(10, wide, LANES)]
        + [vmem(3, rows + 16, columns)] * 2
        + [dma(3)],
        name="stencil",
        far=3,
    )
    beside_edges = lax.ppermute(edges, "gy", [(i, i ^ 1) for i in range(gy)])
    pieces = [shares[0]]
    for shift in range(1, gz):
        ring = [(i, (i + shift) % gz) for i in range(gz)]
        pieces.append(lax.ppermute(shares[shift], "gz", ring))
    relays = vmem_call(
        functools.partial(relay_kernel, gz), [(12, lanes)] * (gz // 2), [edges, beside_edges], name="relay"
    )
    ends = [lax.ppermute(relay, ("gy", "gz"), end_pairs(gy, gz, step)) for step, relay in enumerate(relays)]
    lu, inv4, fixed, outer, inside = vmem_call(
        prepare_kernel,
        [(2, 2, rows, lanes), (4, rows, lanes), (28, lanes), (8, lanes), (rows, rows, modes)],
        [spikes, inverse, coef],
        scratch=[vmem(2, 2, rows, modes), dma(2)],
        flops=2 * 10**8,
        name="prepare",
        far=2,
    )
    rhs, message = vmem_call(
        functools.partial(interface_kernel, wide, firsts),
        [(3, rows, lanes), (56, lanes)],
        [inv4, fixed, outer, *pieces, *ends],
        name="interface",
    )
    other = lax.ppermute(message, "gy", [(i, i ^ 1) for i in range(gy)])
    composed, mine, theirs = vmem_call(pair_kernel, [(24, lanes)] * 3, [message, other], name="pair")

    steps = groups_of(gy)
    base, size = steps[0]
    (known,) = vmem_call(
        functools.partial(widen_kernel, base, True),
        [(24, lanes)],
        [mine, theirs],
        scratch=[vmem(size, 24, lanes)],
        flops=10**7,
        name="widen",
    )
    (local,) = vmem_call(
        block_kernel,
        [(3, rows, lanes)],
        [inside, rhs, message, other],
        scratch=[vmem(3, rows, lanes)] * 2,
        flops=2 * 10**8,
        name="block",
    )
    for base, size in steps[1:-1]:
        gathered = [composed]
        for x in range(1, size):
            gathered.append(lax.ppermute(composed, "gy", [(i, i ^ (x * base) ^ 1) for i in range(gy)]))
        board = [vmem(size, 24, lanes)]
        (composed,) = vmem_call(
            functools.partial(compose_kernel, base), [(24, lanes)], gathered, scratch=board, name="compose"
        )
        (known,) = vmem_call(
            functools.partial(widen_kernel, base, False),
            [(24, lanes)],
            [*gathered, known],
            scratch=board,
            flops=10**7,
            name="widen",
        )
    base, _ = steps[-1]
    (message,) = vmem_call(
        functools.partial(last_message_kernel, base), [(10, lanes)], [composed], name="last_message"
    )
    received = lax.ppermute(message, "gy", [(i, i ^ base ^ 1) for i in range(gy)])
    ready, lift = vmem_call(
        functools.partial(ready_kernel, base),
        [(3, rows, lanes), (2, rows, lanes)],
        [local, lu, known],
        flops=10**7,
        name="ready",
    )
    (out,) = vmem_call(
        functools.partial(final_kernel, base),
        [(3, rows, lanes)],
        [ready, lift, composed, received],
        scratch=[vmem(3, rows, lanes), dma(3)],
        name="final",
        far_out=True,
    )
    return out


def solution(mesh):
    placed = (
        P(None, ("gy", "gz"), None),
        P(None, ("gy", "gz"), None),
        P(None, None, "gy"),
        P("gy", None, "gz"),
        P(None, None, "gy", "gz"),
    )
    return jax.shard_map(
        per_device, mesh=mesh, in_specs=placed, out_specs=P(None, "gy", "gz"), check_vma=False
    )
```

```python
import functools

import jax
import jax.numpy as jnp
from jax import lax
from jax.experimental import pallas as pl
from jax.experimental.pallas import tpu as pltpu
from jax.sharding import PartitionSpec as P

F32 = jnp.float32
BF16 = jnp.bfloat16
LANES = 128
HALO = 2


def vmem_call(body, out_shapes, args, scratch=(), flops=0, name=None, far=0, far_out=False):
    near, away = pl.BlockSpec(memory_space=pltpu.VMEM), pl.BlockSpec(memory_space=pltpu.HBM)
    nbytes = sum(a.size * 4 for a in args)
    args = [pltpu.with_memory_space_constraint(a, pltpu.HBM) for a in args[:far]] + args[far:]
    return pl.pallas_call(
        body,
        out_shape=[jax.ShapeDtypeStruct(s, F32) for s in out_shapes],
        in_specs=[away] * far + [near] * (len(args) - far),
        out_specs=[away if far_out else near] * len(out_shapes),
        scratch_shapes=list(scratch),
        compiler_params=pltpu.CompilerParams(vmem_limit_bytes=16 * 2**20),
        cost_estimate=pl.CostEstimate(flops=flops, bytes_accessed=nbytes, transcendentals=0),
        name=name,
    )(*args)


def window(rows, own, groups):
    spans = [(max(g * own - HALO, 0), min(g * own + own + HALO, rows)) for g in range(groups)]
    wide = max(high - low for low, high in spans)
    return wide, [min(low, rows - wide) for low, _ in spans]


def exact_parts(x):
    high = x.astype(BF16)
    rest = x - high.astype(F32)
    mid = rest.astype(BF16)
    low = (rest - mid.astype(F32)).astype(BF16)
    return high, mid, low


def by_ones(x, ones):
    high, mid, low = exact_parts(x)
    dot = functools.partial(jnp.dot, preferred_element_type=F32)
    return dot(high, ones) + (dot(mid, ones) + dot(low, ones))


def doubled(x):
    row = lax.broadcasted_iota(jnp.int32, (LANES, 2 * LANES), 0)
    col = lax.broadcasted_iota(jnp.int32, (LANES, 2 * LANES), 1)
    ones = (row == lax.shift_right_logical(col, 1)).astype(F32).astype(BF16)
    parts = [by_ones(x[:, i : i + LANES], ones) for i in range(0, x.shape[1], LANES)]
    return jnp.concatenate(parts, axis=1)


def interleave_ones(back):
    a = lax.broadcasted_iota(jnp.int32, (2 * LANES, 2 * LANES), 1 if back else 0)
    b = lax.broadcasted_iota(jnp.int32, (2 * LANES, 2 * LANES), 0 if back else 1)
    place = 2 * (b % LANES) + b // LANES
    return (a == place).astype(F32).astype(BF16)


def side_weights(coef, upper):
    rows = coef.shape[1]
    if upper:
        taps = [[(4, rows - 2), None], [(3, rows - 1), (4, rows - 1)]]
    else:
        taps = [[(0, 0), (1, 0)], [None, (0, 1)]]
    none = jnp.zeros((1, LANES), F32)
    get = lambda tap, kind: none if tap is None else coef[2 * tap[0] + kind, tap[1] : tap[1] + 1]
    return [[[get(tap, kind) for kind in range(2)] for tap in row] for row in taps]


def beside(weights, planes):
    return [
        sum(weights[i][j][kind] * planes(kind, j) for j in range(2) for kind in range(2)) for i in range(2)
    ]


def planes_of(ref, at):
    return lambda kind, j: ref[at + 6 * kind + 3 * j : at + 6 * kind + 3 * j + 3]


def load_kernel(wide, firsts, velocity, explicit, bands, edges, coef, weight, vel, tot, here, there, taps, square, sems):
    groups = len(firsts)
    own = velocity.shape[1]
    rows = coef.shape[1]
    g = lax.axis_index("gz")
    copies = [
        pltpu.make_async_copy(source, target, sems.at[i])
        for i, (source, target) in enumerate(((bands, taps), (velocity, here), (explicit, there)))
    ]
    for copy in copies:
        copy.start()
    square[...] = jnp.zeros_like(square)
    vel[...] = jnp.zeros_like(vel)
    tot[...] = jnp.zeros_like(tot)
    copies[0].wait()
    for d in range(5):
        square[2 * d : 2 * d + 2, 0:rows] = taps[d]
    turned = jnp.transpose(square[...])
    for i in range(10):
        coef[i] = jnp.broadcast_to(turned[0:rows, i : i + 1], (rows, LANES))
    for k in range(groups):

        @pl.when(g == k)
        def _(first=firsts[k]):
            for i in range(10):
                weight[i] = coef[i, first : first + wide]

    copies[1].wait()
    copies[2].wait()
    for k in range(groups):

        @pl.when(g == k)
        def _(base=8 + k * own - firsts[k]):
            for f in range(3):
                vel[f, base : base + own] = here[f]
                tot[f, base : base + own] = here[f] + there[f]

    for f in range(3):
        for j in range(HALO):
            top, bottom = here[f, j : j + 1], here[f, own - HALO + j : own - HALO + j + 1]
            edges[6 + 3 * j + f : 7 + 3 * j + f] = jnp.where(g == 0, top, bottom)
            top += there[f, j : j + 1]
            bottom += there[f, own - HALO + j : own - HALO + j + 1]
            edges[3 * j + f : 3 * j + f + 1] = jnp.where(g == 0, top, bottom)


def stencil_kernel(wide, groups, shifts, vel, tot, weight, edges, *outs):
    part = vel.shape[2] // groups
    g = lax.axis_index("gz")
    weights = [weight[i] for i in range(10)]
    for shift, out in zip(shifts, outs):
        begin = lax.rem(g + shift, groups) * part
        for lane in range(0, part, LANES):
            at = pl.ds(pl.multiple_of(begin + lane, LANES), LANES)
            to = pl.ds(lane, LANES)
            for f in range(3):
                total = None
                for d in range(5):
                    low = pl.ds(8 + d - 2, wide)
                    term = weights[2 * d] * tot[f, low, at] + weights[2 * d + 1] * vel[f, low, at]
                    total = term if total is None else total + term
                out[f * wide : f * wide + wide, to] = total
            out[3 * wide : 3 * wide + 12, to] = edges[0:12, at]


def relay_kernel(groups, edges, beside_edges, *outs):
    core = lax.rem(lax.axis_index("gy"), 2)
    mine = jnp.where(lax.axis_index("gz") == 0, core == 0, core == 1)
    part = edges.shape[1] // groups
    for step, out in enumerate(outs):
        begin = (2 * step + 1 - core) * part
        for lane in range(0, part, LANES):
            at = pl.ds(pl.multiple_of(begin + lane, LANES), LANES)
            out[:, lane : lane + LANES] = jnp.where(mine, edges[:, at], beside_edges[:, at])


def prepare_kernel(spikes, inverse, coef, lu, inv4, fixed, outer, inside, near, sems):
    rows = inverse.shape[1]
    lanes = lu.shape[3]
    core = lax.rem(lax.axis_index("gy"), 2)
    gy, count = lax.axis_index("gy"), lax.axis_size("gy")
    copies = [
        pltpu.make_async_copy(spikes, near, sems.at[0]),
        pltpu.make_async_copy(inverse, inside, sems.at[1]),
    ]
    for copy in copies:
        copy.start()
    wide = lambda row: jnp.concatenate([row] * (lanes // LANES), axis=1)
    lower, upper = side_weights(coef, False), side_weights(coef, True)
    used = jnp.where(core == 0, gy > 0, gy < count - 1)
    for i in range(2):
        for j in range(2):
            for kind in range(2):
                at = 4 * i + 2 * j + kind
                low, high = lower[i][j][kind], upper[i][j][kind]
                fixed[20 + at : 21 + at] = wide(jnp.where(core == 0, high, low))
                outer[at : at + 1] = wide(jnp.where(used, jnp.where(core == 0, low, high), 0.0))
    copies[0].wait()
    lu[...] = doubled(near[...].reshape(4 * rows, -1)).reshape(lu.shape)
    for k in range(2):
        for j in range(2):
            fixed[2 * k + j : 2 * k + j + 1] = -lu[0, j, rows - 2 + k : rows - 1 + k]
            fixed[4 + 2 * k + j : 5 + 2 * k + j] = -lu[0, j, k : k + 1]
            fixed[8 + 2 * k + j : 9 + 2 * k + j] = -lu[1, j, k : k + 1]
    copies[1].wait()
    ends = jnp.concatenate([inside[0:2], inside[rows - 2 : rows]], axis=0)
    inv4[...] = doubled(ends.reshape(4 * rows, -1)).reshape(inv4.shape)
    for k in range(4):
        for i in range(2):
            low, high = inv4[k, i : i + 1], inv4[k, rows - 2 + i : rows - 1 + i]
            at = 12 + 2 * ((k + 2) % 4) + i
            fixed[at : at + 1] = jnp.where(core == 0, high, low)


def rows_of(ref, at):
    return [[[ref[at + 4 * i + 2 * j + kind : at + 4 * i + 2 * j + kind + 1] for kind in range(2)] for j in range(2)] for i in range(2)]


def interface_kernel(wide, firsts, inv4, fixed, outer, *refs):
    groups = len(firsts)
    pieces, ends, (rhs, message) = refs[:groups], refs[groups:-2], refs[-2:]
    rows = rhs.shape[1]
    g = lax.axis_index("gz")
    core = lax.rem(lax.axis_index("gy"), 2)
    rhs[...] = jnp.zeros_like(rhs)
    for shift, piece in enumerate(pieces):
        source = lax.rem(g - shift + groups, groups)
        for k in range(groups):

            @pl.when(source == k)
            def _(piece=piece, k=k):
                for f in range(3):
                    rhs[f, firsts[k] : firsts[k] + wide] += piece[f * wide : f * wide + wide]
                if k in (0, groups - 1):

                    @pl.when(core == (1 if k == 0 else 0))
                    def _():
                        message[24:36] = piece[3 * wide : 3 * wide + 12]

    end = ends[0][...]
    for step in range(1, len(ends)):
        end = jnp.where(g // 2 == step, ends[step][...], end)
    side = beside(rows_of(outer, 0), lambda kind, j: end[6 * kind + 3 * j : 6 * kind + 3 * j + 3])
    low = [jnp.where(core == 0, side[i], 0.0) for i in range(2)]
    high = [jnp.where(core == 0, 0.0, side[i]) for i in range(2)]
    for f in range(3):
        for i in range(2):
            rhs[f, i : i + 1] += low[i][f : f + 1]
            rhs[f, rows - 2 + i : rows - 1 + i] += high[i][f : f + 1]
    for f in range(3):
        for r in range(4):
            value = jnp.sum(inv4[r] * rhs[f], axis=0, keepdims=True)
            row = (6 if r < 2 else 0) + 3 * (r % 2) + f
            message[row : row + 1] = value
    message[12:24] = fixed[0:12]
    message[36:52] = fixed[12:28]


class Piece:
    def __init__(self, ref):
        self.p = [ref[0:3], ref[3:6]]
        self.q = [ref[6:9], ref[9:12]]
        grid = lambda at: [[ref[at + 2 * k + j : at + 2 * k + j + 1] for j in range(2)] for k in range(2)]
        self.F, self.H, self.G = grid(12), grid(16), grid(20)


def act(matrix, vector, plus=None):
    out = [matrix[k][0] * vector[0] + matrix[k][1] * vector[1] for k in range(2)]
    return out if plus is None else [plus[k] + out[k] for k in range(2)]


def times(a, b, plus=None):
    out = [[a[k][0] * b[0][j] + a[k][1] * b[1][j] for j in range(2)] for k in range(2)]
    return out if plus is None else [[plus[k][j] + out[k][j] for j in range(2)] for k in range(2)]


def after(state, piece):
    if state is None:
        return piece.p, piece.F
    return act(piece.F, state[0], piece.p), times(piece.F, state[1])


def before(piece, state):
    if state is None:
        return piece.q, piece.H, piece.G
    q, H, G = state
    q = act(piece.G, act(H, piece.p, q), piece.q)
    H = times(piece.G, times(H, piece.F), piece.H)
    return q, H, times(piece.G, G)


def choose(flag, new, old):
    return jax.tree.map(lambda a, b: jnp.where(flag, a, b), new, old)


def store_vector(ref, at, vector):
    ref[at : at + 3] = vector[0]
    ref[at + 3 : at + 6] = vector[1]


def store_matrix(ref, at, matrix):
    for k in range(2):
        for j in range(2):
            ref[at + 2 * k + j : at + 2 * k + j + 1] = matrix[k][j]


def sorted_pieces(base, pieces, board):
    size = len(pieces)
    position = lax.rem(lax.div(lax.axis_index("gy"), base), size)
    for x, piece in enumerate(pieces):
        board[jnp.bitwise_xor(position, x)] = piece[...]
    return position, [Piece(board.at[i]) for i in range(size)]


def compose_kernel(base, *refs):
    *pieces, out, board = refs
    _, run = sorted_pieces(base, pieces, board)
    up = down = None
    for piece in run:
        up = after(up, piece)
    for piece in run[::-1]:
        down = before(piece, down)
    store_vector(out, 0, up[0])
    store_vector(out, 6, down[0])
    store_matrix(out, 12, up[1])
    store_matrix(out, 16, down[1])
    store_matrix(out, 20, down[2])


def pair_kernel(mine, other, out, fixed_mine, fixed_other):
    core = lax.rem(lax.axis_index("gy"), 2)
    both = []
    for ref, near, target in ((mine, other, fixed_mine), (other, mine, fixed_other)):
        side = beside(rows_of(ref, 44), planes_of(near, 24))
        target[12:24] = ref[12:24]
        for k in range(4):
            value = ref[3 * k : 3 * k + 3]
            for i in range(2):
                value = value + ref[36 + 2 * k + i : 37 + 2 * k + i] * side[i]
            target[3 * k : 3 * k + 3] = value
    low, high = (
        [jnp.where(core == i, fixed_mine[...], fixed_other[...])] for i in range(2)
    )
    low, high = Piece(low[0]), Piece(high[0])
    up, down = after(after(None, low), high), before(low, before(high, None))
    store_vector(out, 0, up[0])
    store_vector(out, 6, down[0])
    store_matrix(out, 12, up[1])
    store_matrix(out, 16, down[1])
    store_matrix(out, 20, down[2])


def around(base, pieces, board):
    position, run = sorted_pieces(base, pieces, board)
    mine = Piece(pieces[0])
    one, none = jnp.ones_like(mine.F[0][0]), jnp.zeros_like(mine.F[0][0])
    zero = jnp.zeros_like(mine.p[0])
    unit = [[one, none], [none, one]]
    blank = [[none, none], [none, none]]
    up = ([zero, zero], unit)
    for i, piece in enumerate(run[:-1]):
        up = choose(i < position, after(up, piece), up)
    down = ([zero, zero], blank, unit)
    for i in range(len(run) - 1, 0, -1):
        down = choose(i > position, before(run[i], down), down)
    return mine, up, down


def widen(base, pieces, board, known):
    mine, (pl_, Fl), (q, H, G) = around(base, pieces, board)
    top = act(mine.F, pl_, mine.p)
    e = act(H, top, q)
    E = times(H, times(mine.F, Fl))
    if known is None:
        return pl_, Fl, e, E, G
    a, A, b, B, D = known
    return (
        act(A, pl_, a),
        times(A, Fl),
        act(D, e, act(B, pl_, b)),
        times(D, E, times(B, Fl)),
        times(D, G),
    )


def read_known(ref):
    piece = Piece(ref)
    return piece.p, piece.F, piece.q, piece.H, piece.G


def widen_kernel(base, start, *refs):
    *pieces, out, board = refs
    known = None
    if not start:
        known = read_known(pieces.pop())
    a, A, b, B, D = widen(base, pieces, board, known)
    store_vector(out, 0, a)
    store_vector(out, 6, b)
    store_matrix(out, 12, A)
    store_matrix(out, 16, B)
    store_matrix(out, 20, D)


def block_kernel(inverse, rhs, mine, other, local, split, solved):
    fields, rows, lanes = rhs.shape
    core = lax.rem(lax.axis_index("gy"), 2)
    side = beside(rows_of(mine, 44), planes_of(other, 24))
    local[...] = rhs[...]
    for f in range(fields):
        for i in range(2):
            value = side[i][f : f + 1]
            local[f, i : i + 1] += jnp.where(core == 0, 0.0, value)
            local[f, rows - 2 + i : rows - 1 + i] += jnp.where(core == 0, value, 0.0)
    apart, together = interleave_ones(False), interleave_ones(True)
    flat = local[...].reshape(fields * rows, lanes)
    for at in range(0, lanes, 2 * LANES):
        turned = by_ones(flat[:, at : at + 2 * LANES], apart)
        split[:, :, at : at + 2 * LANES] = turned.reshape(fields, rows, 2 * LANES)
    for tile in range(lanes // (2 * LANES)):
        modes = pl.ds(tile * LANES, LANES)
        for f in range(fields):
            for p in range(2):
                at = pl.ds((2 * tile + p) * LANES, LANES)
                value = split[f, :, at]
                solved[f, :, at] = jnp.sum(inverse[:, :, modes] * value[None], axis=1)
    flat = solved[...].reshape(fields * rows, lanes)
    for at in range(0, lanes, 2 * LANES):
        turned = by_ones(flat[:, at : at + 2 * LANES], together)
        local[:, :, at : at + 2 * LANES] = turned.reshape(fields, rows, 2 * LANES)


def last_message_kernel(base, composed, out):
    upper = lax.rem(lax.div(lax.axis_index("gy"), base), 2) == 1
    out[0:6] = jnp.where(upper, composed[6:12], composed[0:6])
    out[6:10] = composed[16:20]


def ready_kernel(base, local, lu, known, ready, lift):
    upper = lax.rem(lax.div(lax.axis_index("gy"), base), 2) == 1
    a, A, b, B, D = read_known(known)
    for f in range(3):
        value = local[f]
        for k in range(2):
            value = value - lu[0, k] * a[k][f : f + 1] - lu[1, k] * b[k][f : f + 1]
        ready[f] = value
    for j in range(2):
        value = jnp.zeros_like(lift[j])
        for k in range(2):
            through_t = lu[0, k] * A[k][j] + lu[1, k] * B[k][j]
            value = value - jnp.where(upper, through_t, lu[1, k] * D[k][j])
        lift[j] = value


def final_kernel(base, ready, lift, composed, received, out, held, sems):
    upper = lax.rem(lax.div(lax.axis_index("gy"), base), 2) == 1
    mine = [composed[0:3], composed[3:6]]
    theirs = [received[0:3], received[3:6]]
    H = [[received[6 + 2 * k + j : 7 + 2 * k + j] for j in range(2)] for k in range(2)]
    state = choose(upper, theirs, act(H, mine, theirs))
    copies = []
    for f in range(3):
        held[f] = ready[f] + lift[0] * state[0][f : f + 1] + lift[1] * state[1][f : f + 1]
        copies.append(pltpu.make_async_copy(held.at[f], out.at[f], sems.at[f]))
        copies[-1].start()
    for copy in copies:
        copy.wait()


def end_pairs(gy, gz, step):
    at = lambda y, z: y * gz + z
    pairs = []
    for y in range(1, gy - 1, 2):
        pairs.append((at(y, gz - 1), at(y + 1, 2 * step)))
        pairs.append((at(y - 1, gz - 1), at(y + 1, 2 * step + 1)))
        pairs.append((at(y + 1, 0), at(y, 2 * step + 1)))
        pairs.append((at(y + 2, 0), at(y, 2 * step)))
    sources = sorted(set(range(gy * gz)) - {s for s, _ in pairs})
    targets = sorted(set(range(gy * gz)) - {t for _, t in pairs})
    if gz == 2:
        for i in range(0, len(sources), 2):
            pairs += [(sources[i], targets[i + 1]), (sources[i + 1], targets[i])]
    return pairs


def groups_of(count):
    steps, base = [(1, 2)], 2
    while 2 * base < count:
        size = 4 if base * 8 <= count else 2
        steps.append((base, size))
        base *= size
    return steps + [(base, 2)]


def per_device(velocity, explicit, bands, inverse, spikes):
    gy, gz = lax.axis_size("gy"), lax.axis_size("gz")
    own, columns = velocity.shape[1:]
    rows, modes = inverse.shape[0], inverse.shape[2]
    lanes = 2 * modes
    wide, firsts = window(rows, own, gz)
    vmem = lambda *shape: pltpu.VMEM(shape, F32)
    dma = lambda n: pltpu.SemaphoreType.DMA((n,))

    high = -(-(3 * wide + 12) // 8) * 8
    padded = (3, rows + 16, columns)
    edges, coef, weight, vel, tot = vmem_call(
        functools.partial(load_kernel, wide, firsts),
        [(12, columns), (10, rows, LANES), (10, wide, LANES), padded, padded],
        [velocity, explicit, jnp.transpose(bands, (1, 0, 2))],
        scratch=[vmem(3, own, columns)] * 2 + [vmem(5, 2, rows), vmem(LANES, LANES), dma(3)],
        name="load",
        far=3,
    )
    beside_edges = lax.ppermute(edges, "gy", [(i, i ^ 1) for i in range(gy)])

    def shares(*shifts):
        return vmem_call(
            functools.partial(stencil_kernel, wide, gz, shifts),
            [(high, lanes)] * len(shifts),
            [vel, tot, weight, edges],
            flops=2 * 10**8,
            name="stencil",
        )

    sent = shares(*range(1, gz))
    pieces = list(shares(0))
    for shift in range(1, gz):
        ring = [(i, (i + shift) % gz) for i in range(gz)]
        pieces.append(lax.ppermute(sent[shift - 1], "gz", ring))
    relays = vmem_call(
        functools.partial(relay_kernel, gz), [(12, lanes)] * (gz // 2), [edges, beside_edges], name="relay"
    )
    ends = [lax.ppermute(relay, ("gy", "gz"), end_pairs(gy, gz, step)) for step, relay in enumerate(relays)]
    lu, inv4, fixed, outer, inside = vmem_call(
        prepare_kernel,
        [(2, 2, rows, lanes), (4, rows, lanes), (28, lanes), (8, lanes), (rows, rows, modes)],
        [spikes, inverse, coef],
        scratch=[vmem(2, 2, rows, modes), dma(2)],
        flops=2 * 10**10,
        name="prepare",
        far=2,
    )
    rhs, message = vmem_call(
        functools.partial(interface_kernel, wide, firsts),
        [(3, rows, lanes), (56, lanes)],
        [inv4, fixed, outer, *pieces, *ends],
        name="interface",
    )
    other = lax.ppermute(message, "gy", [(i, i ^ 1) for i in range(gy)])
    composed, mine, theirs = vmem_call(pair_kernel, [(24, lanes)] * 3, [message, other], name="pair")

    steps = groups_of(gy)
    base, size = steps[0]
    (known,) = vmem_call(
        functools.partial(widen_kernel, base, True),
        [(24, lanes)],
        [mine, theirs],
        scratch=[vmem(size, 24, lanes)],
        flops=10**7,
        name="widen",
    )
    (local,) = vmem_call(
        block_kernel,
        [(3, rows, lanes)],
        [inside, rhs, message, other],
        scratch=[vmem(3, rows, lanes)] * 2,
        flops=2 * 10**8,
        name="block",
    )
    for base, size in steps[1:-1]:
        gathered = [composed]
        for x in range(1, size):
            gathered.append(lax.ppermute(composed, "gy", [(i, i ^ (x * base) ^ 1) for i in range(gy)]))
        board = [vmem(size, 24, lanes)]
        (composed,) = vmem_call(
            functools.partial(compose_kernel, base), [(24, lanes)], gathered, scratch=board, name="compose"
        )
        (known,) = vmem_call(
            functools.partial(widen_kernel, base, False),
            [(24, lanes)],
            [*gathered, known],
            scratch=board,
            flops=10**7,
            name="widen",
        )
    base, _ = steps[-1]
    (message,) = vmem_call(
        functools.partial(last_message_kernel, base), [(10, lanes)], [composed], name="last_message"
    )
    received = lax.ppermute(message, "gy", [(i, i ^ base ^ 1) for i in range(gy)])
    ready, lift = vmem_call(
        functools.partial(ready_kernel, base),
        [(3, rows, lanes), (2, rows, lanes)],
        [local, lu, known],
        flops=10**7,
        name="ready",
    )
    (out,) = vmem_call(
        functools.partial(final_kernel, base),
        [(3, rows, lanes)],
        [ready, lift, composed, received],
        scratch=[vmem(3, rows, lanes), dma(3)],
        name="final",
        far_out=True,
    )
    return out


def solution(mesh):
    placed = (
        P(None, ("gy", "gz"), None),
        P(None, ("gy", "gz"), None),
        P(None, None, "gy"),
        P("gy", None, "gz"),
        P(None, None, "gy", "gz"),
    )
    return jax.shard_map(
        per_device, mesh=mesh, in_specs=placed, out_specs=P(None, "gy", "gz"), check_vma=False
    )
```

```python
import functools

import jax
import jax.numpy as jnp
from jax import lax
from jax.experimental import pallas as pl
from jax.experimental.pallas import tpu as pltpu
from jax.sharding import PartitionSpec as P

F32 = jnp.float32
LANES = 128
HALO = 2


def vmem_call(body, out_shapes, args, scratch=(), flops=0, name=None, far=0, far_out=False):
    near, away = pl.BlockSpec(memory_space=pltpu.VMEM), pl.BlockSpec(memory_space=pltpu.HBM)
    nbytes = sum(a.size * 4 for a in args)
    args = [pltpu.with_memory_space_constraint(a, pltpu.HBM) for a in args[:far]] + args[far:]
    return pl.pallas_call(
        body,
        out_shape=[jax.ShapeDtypeStruct(s, F32) for s in out_shapes],
        in_specs=[away] * far + [near] * (len(args) - far),
        out_specs=[away if far_out else near] * len(out_shapes),
        scratch_shapes=list(scratch),
        compiler_params=pltpu.CompilerParams(vmem_limit_bytes=16 * 2**20),
        cost_estimate=pl.CostEstimate(flops=flops, bytes_accessed=nbytes, transcendentals=0),
        name=name,
    )(*args)


def window(rows, own, groups):
    spans = [(max(g * own - HALO, 0), min(g * own + own + HALO, rows)) for g in range(groups)]
    wide = max(high - low for low, high in spans)
    return wide, [min(low, rows - wide) for low, _ in spans]


def lane_of(x):
    return lax.broadcasted_iota(jnp.int32, (x.shape[0], LANES), 1)


def take(x, lanes):
    return jnp.take_along_axis(x, lanes, axis=1, mode="promise_in_bounds")


def apart(x):
    lane = lane_of(x)
    low = lane < LANES // 2
    even = jnp.where(low, 2 * lane, 2 * lane - (LANES - 1))
    odd = jnp.where(low, 2 * lane + 1, 2 * lane - LANES)
    a, b = x[:, :LANES], x[:, LANES:]
    return jnp.where(low, take(a, even), take(b, odd)), jnp.where(low, take(a, odd), take(b, even))


def together(real, imaginary):
    lane = lane_of(real)
    half, odd = lax.shift_right_logical(lane, 1), jnp.bitwise_and(lane, 1) == 1
    parts = [
        jnp.where(odd, take(imaginary, half + at), take(real, half + at)) for at in (0, LANES // 2)
    ]
    return jnp.concatenate(parts, axis=1)


def doubled(x):
    half = lax.shift_right_logical(lane_of(x), 1)
    return jnp.concatenate([take(x, half), take(x, half + LANES // 2)], axis=1)


STATE = 24
MAPS = 12
RUN = STATE + MAPS
FIRST = STATE + 24 + MAPS + 16
LAST = 16


def side_weights(coef, upper):
    rows = coef.shape[1]
    if upper:
        taps = [[(4, rows - 2), None], [(3, rows - 1), (4, rows - 1)]]
    else:
        taps = [[(0, 0), (1, 0)], [None, (0, 1)]]
    none = jnp.zeros((1, LANES), F32)
    get = lambda tap, kind: none if tap is None else coef[2 * tap[0] + kind, tap[1] : tap[1] + 1]
    return [[[get(tap, kind) for kind in range(2)] for tap in row] for row in taps]


def beside(weights, planes):
    return [
        sum(weights[i][j][kind] * planes(kind, j) for j in range(2) for kind in range(2)) for i in range(2)
    ]


def load_kernel(wide, firsts, velocity, explicit, bands, edges, coef, weight, vel, tot, here, there, taps, square, sems):
    groups = len(firsts)
    own = velocity.shape[1]
    rows = coef.shape[1]
    g = lax.axis_index("gz")
    copies = [
        pltpu.make_async_copy(source, target, sems.at[i])
        for i, (source, target) in enumerate(((bands, taps), (velocity, here), (explicit, there)))
    ]
    for copy in copies:
        copy.start()
    square[...] = jnp.zeros_like(square)
    vel[...] = jnp.zeros_like(vel)
    tot[...] = jnp.zeros_like(tot)
    copies[0].wait()
    for d in range(5):
        square[2 * d : 2 * d + 2, 0:rows] = taps[d]
    turned = jnp.transpose(square[...])
    for i in range(10):
        coef[i] = jnp.broadcast_to(turned[0:rows, i : i + 1], (rows, LANES))
    for k in range(groups):

        @pl.when(g == k)
        def _(first=firsts[k]):
            for i in range(10):
                weight[i] = coef[i, first : first + wide]

    copies[1].wait()
    copies[2].wait()
    for k in range(groups):

        @pl.when(g == k)
        def _(base=8 + k * own - firsts[k]):
            for f in range(3):
                vel[f, base : base + own] = here[f]
                tot[f, base : base + own] = here[f] + there[f]

    for f in range(3):
        for j in range(HALO):
            top, bottom = here[f, j : j + 1], here[f, own - HALO + j : own - HALO + j + 1]
            edges[6 + 3 * j + f : 7 + 3 * j + f] = jnp.where(g == 0, top, bottom)
            top += there[f, j : j + 1]
            bottom += there[f, own - HALO + j : own - HALO + j + 1]
            edges[3 * j + f : 3 * j + f + 1] = jnp.where(g == 0, top, bottom)


def stencil_kernel(wide, groups, shifts, vel, tot, weight, edges, *outs):
    part = vel.shape[2] // groups
    g = lax.axis_index("gz")
    weights = [weight[i] for i in range(10)]
    for shift, out in zip(shifts, outs):
        begin = lax.rem(g + shift, groups) * part
        for lane in range(0, part, LANES):
            at = pl.ds(pl.multiple_of(begin + lane, LANES), LANES)
            to = pl.ds(lane, LANES)
            for f in range(3):
                total = None
                for d in range(5):
                    low = pl.ds(8 + d - 2, wide)
                    term = weights[2 * d] * tot[f, low, at] + weights[2 * d + 1] * vel[f, low, at]
                    total = term if total is None else total + term
                out[f * wide : f * wide + wide, to] = total
            out[3 * wide : 3 * wide + 12, to] = edges[0:12, at]


def store_planes(ref, at, planes):
    real, imaginary = apart(planes)
    for i in range(4):
        ref[at + 6 * i : at + 6 * i + 3] = real[3 * i : 3 * i + 3]
        ref[at + 6 * i + 3 : at + 6 * i + 6] = imaginary[3 * i : 3 * i + 3]


def planes_of(ref, at):
    return lambda kind, j: ref[at + 12 * kind + 6 * j : at + 12 * kind + 6 * j + 6]


def relay_kernel(groups, edges, beside_edges, *outs):
    core = lax.rem(lax.axis_index("gy"), 2)
    mine = jnp.where(lax.axis_index("gz") == 0, core == 0, core == 1)
    part = edges.shape[1] // groups
    for step, out in enumerate(outs):
        begin = (2 * step + 1 - core) * part
        for b in range(part // (2 * LANES)):
            at = pl.ds(pl.multiple_of(begin + 2 * LANES * b, 2 * LANES), 2 * LANES)
            store_planes(out, 24 * b, jnp.where(mine, edges[:, at], beside_edges[:, at]))


def prepare_kernel(spikes, inverse, coef, inv4, fixed, inside, near, sems):
    rows, modes = inverse.shape[1:]
    core = lax.rem(lax.axis_index("gy"), 2)
    gy, count = lax.axis_index("gy"), lax.axis_size("gy")
    copies = [pltpu.make_async_copy(spikes, near, sems.at[0])]
    for i, (low, size) in enumerate(((0, 2), (rows - 2, 2), (2, rows - 4))):
        part = pl.ds(low, size)
        copies.append(pltpu.make_async_copy(inverse.at[part], inside.at[part], sems.at[1 + i]))
    for copy in copies:
        copy.start()
    lower, upper = side_weights(coef, False), side_weights(coef, True)
    used = jnp.where(core == 0, gy > 0, gy < count - 1)
    weights = (MAPS + 16) * (modes // LANES)
    for i in range(2):
        for j in range(2):
            for kind in range(2):
                at = weights + 4 * i + 2 * j + kind
                low, high = lower[i][j][kind], upper[i][j][kind]
                fixed[at : at + 1] = jnp.where(core == 0, high, low)
                fixed[at + 8 : at + 9] = jnp.where(used, jnp.where(core == 0, low, high), 0.0)
    copies[0].wait()
    for b in range(modes // LANES):
        at, lanes = (MAPS + 16) * b, pl.ds(LANES * b, LANES)
        for k in range(2):
            for j in range(2):
                row = at + 2 * k + j
                fixed[row : row + 1] = -near[0, j, rows - 2 + k : rows - 1 + k, lanes]
                fixed[row + 4 : row + 5] = -near[0, j, k : k + 1, lanes]
                fixed[row + 8 : row + 9] = -near[1, j, k : k + 1, lanes]
    copies[1].wait()
    copies[2].wait()
    for b in range(modes // LANES):
        at, lanes = (MAPS + 16) * b + MAPS, pl.ds(LANES * b, LANES)
        for r, row in enumerate((0, 1, rows - 2, rows - 1)):
            inv4[r, :, 2 * LANES * b : 2 * LANES * (b + 1)] = doubled(inside[row, :, lanes])
            for i in range(2):
                low, high = inside[row, i : i + 1, lanes], inside[row, rows - 2 + i : rows - 1 + i, lanes]
                to = at + 2 * ((r + 2) % 4) + i
                fixed[to : to + 1] = jnp.where(core == 0, high, low)
                fixed[to + 8 : to + 9] = jnp.where(core == 0, low, high)
    copies[3].wait()


def weights_of(ref, at):
    at += ref.shape[0] - 16
    return [
        [[ref[at + 4 * i + 2 * j + kind : at + 4 * i + 2 * j + kind + 1] for kind in range(2)] for j in range(2)]
        for i in range(2)
    ]


def interface_kernel(wide, firsts, inv4, fixed, *refs):
    groups = len(firsts)
    *pieces, rhs, message, planes, values = refs
    rows, lanes = rhs.shape[1:]
    blocks = lanes // (2 * LANES)
    g = lax.axis_index("gz")
    core = lax.rem(lax.axis_index("gy"), 2)
    rhs[...] = jnp.zeros_like(rhs)
    for shift, piece in enumerate(pieces):
        source = lax.rem(g - shift + groups, groups)
        for k in range(groups):

            @pl.when(source == k)
            def _(piece=piece, k=k):
                for f in range(3):
                    rhs[f, firsts[k] : firsts[k] + wide] += piece[f * wide : f * wide + wide]
                if k in (0, groups - 1):

                    @pl.when(core == (1 if k == 0 else 0))
                    def _():
                        planes[...] = piece[3 * wide : 3 * wide + 12]

    for f in range(3):
        for r in range(4):
            row = (6 if r < 2 else 0) + 3 * (r % 2) + f
            values[row : row + 1] = jnp.sum(inv4[r] * rhs[f], axis=0, keepdims=True)
    for b in range(blocks):
        at, columns = FIRST * b, pl.ds(2 * LANES * b, 2 * LANES)
        store_planes(message, at, values[:, columns])
        store_planes(message, at + STATE, planes[:, columns])
        message[at + 48 : at + FIRST] = fixed[(MAPS + 16) * b : (MAPS + 16) * (b + 1)]
    message[FIRST * blocks : FIRST * blocks + 16] = fixed[(MAPS + 16) * blocks : (MAPS + 16) * blocks + 16]


class Piece:
    def __init__(self, ref, at):
        self.p = [ref[at : at + 6], ref[at + 6 : at + 12]]
        self.q = [ref[at + 12 : at + 18], ref[at + 18 : at + 24]]
        self.F, self.H, self.G = (matrix_of(ref, at + STATE + 4 * i) for i in range(3))


def matrix_of(ref, at):
    return [[ref[at + 2 * k + j : at + 2 * k + j + 1] for j in range(2)] for k in range(2)]


def act(matrix, vector, plus=None):
    out = [matrix[k][0] * vector[0] + matrix[k][1] * vector[1] for k in range(2)]
    return out if plus is None else [plus[k] + out[k] for k in range(2)]


def times(a, b, plus=None):
    out = [[a[k][0] * b[0][j] + a[k][1] * b[1][j] for j in range(2)] for k in range(2)]
    return out if plus is None else [[plus[k][j] + out[k][j] for j in range(2)] for k in range(2)]


def after(state, piece):
    if state is None:
        return piece.p, piece.F
    return act(piece.F, state[0], piece.p), times(piece.F, state[1])


def before(piece, state):
    if state is None:
        return piece.q, piece.H, piece.G
    q, H, G = state
    q = act(piece.G, act(H, piece.p, q), piece.q)
    H = times(piece.G, times(H, piece.F), piece.H)
    return q, H, times(piece.G, G)


def choose(flag, new, old):
    return jax.tree.map(lambda a, b: jnp.where(flag, a, b), new, old)


def store_run(ref, at, p, q, F, H, G):
    for i, vector in enumerate((p, q)):
        for k in range(2):
            ref[at + 12 * i + 6 * k : at + 12 * i + 6 * k + 6] = vector[k]
    for i, matrix in enumerate((F, H, G)):
        for k in range(2):
            for j in range(2):
                row = at + STATE + 4 * i + 2 * k + j
                ref[row : row + 1] = matrix[k][j]


def sort_pieces(base, pieces, board):
    size = len(pieces)
    position = lax.rem(lax.div(lax.axis_index("gy"), base), size)
    for i, piece in enumerate(pieces):
        board[jnp.bitwise_xor(position, (size - i) % size)] = piece[...]
    return position


def compose_kernel(base, *refs):
    *pieces, out, board = refs
    sort_pieces(base, pieces, board)
    for at in range(0, out.shape[0], RUN):
        run = [Piece(board.at[i], at) for i in range(len(pieces))]
        up = down = None
        for piece in run:
            up = after(up, piece)
        for piece in run[::-1]:
            down = before(piece, down)
        store_run(out, at, up[0], down[0], up[1], down[1], down[2])


def ends_kernel(*refs):
    *ends, out = refs
    step = lax.div(lax.axis_index("gz"), 2)
    half, size = len(ends) // 2, ends[0].shape[0]
    for k in range(2):
        end = ends[k * half][...]
        for i in range(1, half):
            end = jnp.where(step == i, ends[k * half + i][...], end)
        out[size * k : size * (k + 1)] = end


def pair_kernel(mine, other, ends, out, fixed_mine, fixed_other):
    core = lax.rem(lax.axis_index("gy"), 2)
    blocks = out.shape[0] // RUN
    for ref, across, side, target in ((mine, other, 0, fixed_mine), (other, mine, 1, fixed_other)):
        inner_weights, outer_weights = weights_of(ref, 0), weights_of(ref, 8)
        for b in range(blocks):
            at, to = FIRST * b, RUN * b
            inner = beside(inner_weights, planes_of(across, at + STATE))
            outer = beside(outer_weights, planes_of(ends, 24 * (side * blocks + b)))
            target[to + STATE : to + RUN] = ref[at + 48 : at + 48 + MAPS]
            for k in range(4):
                value = ref[at + 6 * k : at + 6 * k + 6]
                for i in range(2):
                    row = at + 48 + MAPS + 2 * k + i
                    value = value + ref[row : row + 1] * inner[i] + ref[row + 8 : row + 9] * outer[i]
                target[to + 6 * k : to + 6 * k + 6] = value
    low = jnp.where(core == 0, fixed_mine[...], fixed_other[...])
    high = jnp.where(core == 0, fixed_other[...], fixed_mine[...])
    for at in range(0, out.shape[0], RUN):
        first, second = Piece(low, at), Piece(high, at)
        up, down = after(after(None, first), second), before(first, before(second, None))
        store_run(out, at, up[0], down[0], up[1], down[1], down[2])


def widen_kernel(base, start, *refs):
    *pieces, out, board = refs
    known_ref = None if start else pieces.pop()
    position = sort_pieces(base, pieces, board)
    for at in range(0, out.shape[0], RUN):
        run = [Piece(board.at[i], at) for i in range(len(pieces))]
        mine = Piece(pieces[0], at)
        one, none = jnp.ones_like(mine.F[0][0]), jnp.zeros_like(mine.F[0][0])
        zero = [jnp.zeros_like(mine.p[0])] * 2
        unit, blank = [[one, none], [none, one]], [[none, none], [none, none]]
        up, down = (zero, unit), (zero, blank, unit)
        for i, piece in enumerate(run[:-1]):
            up = choose(i < position, after(up, piece), up)
        for i in range(len(run) - 1, 0, -1):
            down = choose(i > position, before(run[i], down), down)
        (t, F), (q, H, G) = up, down
        e = act(H, act(mine.F, t, mine.p), q)
        E = times(H, times(mine.F, F))
        if start:
            store_run(out, at, t, e, F, E, G)
        else:
            known = Piece(known_ref, at)
            a, A, b, B, D = known.p, known.F, known.q, known.H, known.G
            store_run(
                out, at, act(A, t, a), act(D, e, act(B, t, b)), times(A, F), times(D, E, times(B, F)), times(D, G)
            )


def block_kernel(inverse, rhs, mine, other, ends, local, split):
    fields, rows, lanes = rhs.shape
    core = lax.rem(lax.axis_index("gy"), 2)
    inner_weights, outer_weights = weights_of(mine, 0), weights_of(mine, 8)
    flat = rhs[...].reshape(fields * rows, lanes)
    for b in range(lanes // (2 * LANES)):
        columns = pl.ds(2 * LANES * b, 2 * LANES)
        parts = apart(flat[:, 2 * LANES * b : 2 * LANES * (b + 1)])
        inner = beside(inner_weights, planes_of(other, FIRST * b + STATE))
        outer = beside(outer_weights, planes_of(ends, 24 * b))
        solved = []
        for p in range(2):
            split[...] = parts[p].reshape(fields, rows, LANES)
            for f in range(fields):
                for i in range(2):
                    one, two = inner[i][3 * p + f : 3 * p + f + 1], outer[i][3 * p + f : 3 * p + f + 1]
                    split[f, i : i + 1] += jnp.where(core == 0, two, one)
                    split[f, rows - 2 + i : rows - 1 + i] += jnp.where(core == 0, one, two)
            factors = inverse[:, :, LANES * b : LANES * (b + 1)]
            solved.append([jnp.sum(factors * split[f][None], axis=1) for f in range(fields)])
        for f in range(fields):
            local[f, :, columns] = together(solved[0][f], solved[1][f])


def last_message_kernel(base, composed, out):
    upper = lax.rem(lax.div(lax.axis_index("gy"), base), 2) == 1
    for b in range(out.shape[0] // LAST):
        at, to = RUN * b, LAST * b
        out[to : to + 12] = jnp.where(upper, composed[at + 12 : at + 24], composed[at : at + 12])
        out[to + 12 : to + 16] = composed[at + STATE + 4 : at + STATE + 8]


def ready_kernel(base, local, spikes, known, ready, lift):
    upper = lax.rem(lax.div(lax.axis_index("gy"), base), 2) == 1
    for b in range(known.shape[0] // RUN):
        columns = pl.ds(2 * LANES * b, 2 * LANES)
        factors = [[doubled(spikes[i, k, :, LANES * b : LANES * (b + 1)]) for k in range(2)] for i in range(2)]
        run = Piece(known, RUN * b)
        maps = doubled(known[RUN * b + STATE : RUN * (b + 1)])
        A, B, D = (matrix_of(maps, 4 * i) for i in range(3))
        t, s = ([together(v[k][0:3], v[k][3:6]) for k in range(2)] for v in (run.p, run.q))
        for f in range(3):
            value = local[f, :, columns]
            for k in range(2):
                value = value - factors[0][k] * t[k][f : f + 1] - factors[1][k] * s[k][f : f + 1]
            ready[f, :, columns] = value
        for j in range(2):
            value = jnp.zeros_like(factors[0][0])
            for k in range(2):
                through_t = factors[0][k] * A[k][j] + factors[1][k] * B[k][j]
                value = value - jnp.where(upper, through_t, factors[1][k] * D[k][j])
            lift[j, :, columns] = value


def final_kernel(base, ready, lift, composed, received, out, held, sems):
    upper = lax.rem(lax.div(lax.axis_index("gy"), base), 2) == 1
    states = []
    for b in range(composed.shape[0] // RUN):
        at, to = RUN * b, LAST * b
        mine = [composed[at : at + 6], composed[at + 6 : at + 12]]
        theirs = [received[to : to + 6], received[to + 6 : to + 12]]
        state = choose(upper, theirs, act(matrix_of(received, to + 12), mine, theirs))
        states.append([together(v[0:3], v[3:6]) for v in state])
    copies = []
    for f in range(3):
        for b, state in enumerate(states):
            columns = pl.ds(2 * LANES * b, 2 * LANES)
            value = ready[f, :, columns]
            for j in range(2):
                value = value + lift[j, :, columns] * state[j][f : f + 1]
            held[f, :, columns] = value
        copies.append(pltpu.make_async_copy(held.at[f], out.at[f], sems.at[f]))
        copies[-1].start()
    for copy in copies:
        copy.wait()


def end_pairs(gy, gz, step, flip):
    at = lambda y, z: y * gz + z
    pairs = []
    for y in range(1, gy - 1, 2):
        up, down = (y + 1) ^ flip, y ^ flip
        pairs.append((at(y, gz - 1), at(up, 2 * step)))
        pairs.append((at(y - 1, gz - 1), at(up, 2 * step + 1)))
        pairs.append((at(y + 1, 0), at(down, 2 * step + 1)))
        pairs.append((at(y + 2, 0), at(down, 2 * step)))
    sources = sorted(set(range(gy * gz)) - {s for s, _ in pairs})
    targets = sorted(set(range(gy * gz)) - {t for _, t in pairs})
    if gz == 2:
        for i in range(0, len(sources), 2):
            (a, b), (c, d) = sources[i : i + 2], targets[i : i + 2]
            pairs += [(a, d), (b, c)] if a != d and b != c else [(a, c), (b, d)]
    return pairs


def groups_of(count):
    steps, base = [(1, 2)], 2
    while 2 * base < count:
        size = 4 if base * 8 <= count else 2
        steps.append((base, size))
        base *= size
    return steps + [(base, 2)]


def per_device(velocity, explicit, bands, inverse, spikes):
    gy, gz = lax.axis_size("gy"), lax.axis_size("gz")
    own, columns = velocity.shape[1:]
    rows, modes = inverse.shape[0], inverse.shape[2]
    lanes = 2 * modes
    wide, firsts = window(rows, own, gz)
    vmem = lambda *shape: pltpu.VMEM(shape, F32)
    dma = lambda n: pltpu.SemaphoreType.DMA((n,))

    high = -(-(3 * wide + 12) // 8) * 8
    padded = (3, rows + 16, columns)
    edges, coef, weight, vel, tot = vmem_call(
        functools.partial(load_kernel, wide, firsts),
        [(12, columns), (10, rows, LANES), (10, wide, LANES), padded, padded],
        [velocity, explicit, jnp.transpose(bands, (1, 0, 2))],
        scratch=[vmem(3, own, columns)] * 2 + [vmem(5, 2, rows), vmem(LANES, LANES), dma(3)],
        name="load",
        far=3,
    )
    beside_edges = lax.ppermute(edges, "gy", [(i, i ^ 1) for i in range(gy)])

    def shares(*shifts):
        return vmem_call(
            functools.partial(stencil_kernel, wide, gz, shifts),
            [(high, lanes)] * len(shifts),
            [vel, tot, weight, edges],
            flops=2 * 10**8,
            name="stencil",
        )

    sent = shares(*range(1, gz))
    pieces = list(shares(0))
    for shift in range(1, gz):
        ring = [(i, (i + shift) % gz) for i in range(gz)]
        pieces.append(lax.ppermute(sent[shift - 1], "gz", ring))
    blocks = modes // LANES
    relays = vmem_call(
        functools.partial(relay_kernel, gz), [(24 * blocks, LANES)] * (gz // 2), [edges, beside_edges], name="relay"
    )
    near, far = (
        [lax.ppermute(relay, ("gy", "gz"), end_pairs(gy, gz, step, flip)) for step, relay in enumerate(relays)]
        for flip in (0, 1)
    )
    inv4, fixed, inside, held = vmem_call(
        prepare_kernel,
        [(4, rows, lanes), ((MAPS + 16) * blocks + 16, LANES), (rows, rows, modes), (2, 2, rows, modes)],
        [spikes, inverse, coef],
        scratch=[dma(4)],
        flops=2 * 10**10,
        name="prepare",
        far=2,
    )
    rhs, message = vmem_call(
        functools.partial(interface_kernel, wide, firsts),
        [(3, rows, lanes), (FIRST * blocks + 16, LANES)],
        [inv4, fixed, *pieces],
        scratch=[vmem(12, lanes)] * 2,
        name="interface",
    )
    other = lax.ppermute(message, "gy", [(i, i ^ 1) for i in range(gy)])
    (ends,) = vmem_call(ends_kernel, [(48 * blocks, LANES)], [*near, *far], flops=2 * 10**10, name="ends")
    run = (RUN * blocks, LANES)
    composed, mine, theirs = vmem_call(pair_kernel, [run] * 3, [message, other, ends], name="pair")

    steps = groups_of(gy)
    base, size = steps[0]
    (known,) = vmem_call(
        functools.partial(widen_kernel, base, True),
        [run],
        [mine, theirs],
        scratch=[vmem(size, *run)],
        flops=10**7,
        name="widen",
    )
    (local,) = vmem_call(
        block_kernel,
        [(3, rows, lanes)],
        [inside, rhs, message, other, ends],
        scratch=[vmem(3, rows, LANES)],
        flops=2 * 10**8,
        name="block",
    )
    for base, size in steps[1:-1]:
        gathered = [composed]
        for x in range(size - 1, 0, -1):
            gathered.append(lax.ppermute(composed, "gy", [(i, i ^ (x * base) ^ 1) for i in range(gy)]))
        board = [vmem(size, *run)]
        (composed,) = vmem_call(
            functools.partial(compose_kernel, base), [run], gathered, scratch=board, name="compose"
        )
        (known,) = vmem_call(
            functools.partial(widen_kernel, base, False),
            [run],
            [*gathered, known],
            scratch=board,
            flops=10**7,
            name="widen",
        )
    base, _ = steps[-1]
    (message,) = vmem_call(
        functools.partial(last_message_kernel, base), [(LAST * blocks, LANES)], [composed], name="last_message"
    )
    received = lax.ppermute(message, "gy", [(i, i ^ base ^ 1) for i in range(gy)])
    ready, lift = vmem_call(
        functools.partial(ready_kernel, base),
        [(3, rows, lanes), (2, rows, lanes)],
        [local, held, known],
        flops=10**7,
        name="ready",
    )
    (out,) = vmem_call(
        functools.partial(final_kernel, base),
        [(3, rows, lanes)],
        [ready, lift, composed, received],
        scratch=[vmem(3, rows, lanes), dma(3)],
        name="final",
        far_out=True,
    )
    return out


def solution(mesh):
    placed = (
        P(None, ("gy", "gz"), None),
        P(None, ("gy", "gz"), None),
        P(None, None, "gy"),
        P("gy", None, "gz"),
        P(None, None, "gy", "gz"),
    )
    return jax.shard_map(
        per_device, mesh=mesh, in_specs=placed, out_specs=P(None, "gy", "gz"), check_vma=False
    )
```

```python
import functools

import jax
import jax.numpy as jnp
from jax import lax
from jax.experimental import pallas as pl
from jax.experimental.pallas import tpu as pltpu
from jax.sharding import PartitionSpec as P

F32 = jnp.float32
LANES = 128
HALO = 2


def vmem_call(body, out_shapes, args, scratch=(), flops=0, name=None, far=0, far_out=False):
    near, away = pl.BlockSpec(memory_space=pltpu.VMEM), pl.BlockSpec(memory_space=pltpu.HBM)
    nbytes = sum(a.size * 4 for a in args)
    args = [pltpu.with_memory_space_constraint(a, pltpu.HBM) for a in args[:far]] + args[far:]
    return pl.pallas_call(
        body,
        out_shape=[jax.ShapeDtypeStruct(s, F32) for s in out_shapes],
        in_specs=[away] * far + [near] * (len(args) - far),
        out_specs=[away if far_out else near] * len(out_shapes),
        scratch_shapes=list(scratch),
        compiler_params=pltpu.CompilerParams(vmem_limit_bytes=16 * 2**20),
        cost_estimate=pl.CostEstimate(flops=flops, bytes_accessed=nbytes, transcendentals=0),
        name=name,
    )(*args)


def window(rows, own, groups):
    spans = [(max(g * own - HALO, 0), min(g * own + own + HALO, rows)) for g in range(groups)]
    wide = max(high - low for low, high in spans)
    return wide, [min(low, rows - wide) for low, _ in spans]


def lane_of(x):
    return lax.broadcasted_iota(jnp.int32, (x.shape[0], LANES), 1)


def take(x, lanes):
    return jnp.take_along_axis(x, lanes, axis=1, mode="promise_in_bounds")


def apart(x):
    lane = lane_of(x)
    low = lane < LANES // 2
    even = jnp.where(low, 2 * lane, 2 * lane - (LANES - 1))
    odd = jnp.where(low, 2 * lane + 1, 2 * lane - LANES)
    a, b = x[:, :LANES], x[:, LANES:]
    return jnp.where(low, take(a, even), take(b, odd)), jnp.where(low, take(a, odd), take(b, even))


def together(real, imaginary):
    lane = lane_of(real)
    half, odd = lax.shift_right_logical(lane, 1), jnp.bitwise_and(lane, 1) == 1
    parts = [
        jnp.where(odd, take(imaginary, half + at), take(real, half + at)) for at in (0, LANES // 2)
    ]
    return jnp.concatenate(parts, axis=1)


def doubled(x):
    half = lax.shift_right_logical(lane_of(x), 1)
    return jnp.concatenate([take(x, half), take(x, half + LANES // 2)], axis=1)


STATE = 24
MAPS = 12
RUN = STATE + MAPS
FIRST = STATE + 12 + MAPS + 16
LAST = 16


def side_weights(coef, upper):
    rows = coef.shape[1]
    if upper:
        taps = [[(4, rows - 2), None], [(3, rows - 1), (4, rows - 1)]]
    else:
        taps = [[(0, 0), (1, 0)], [None, (0, 1)]]
    none = jnp.zeros((1, LANES), F32)
    get = lambda tap, kind: none if tap is None else coef[2 * tap[0] + kind, tap[1] : tap[1] + 1]
    return [[[get(tap, kind) for kind in range(2)] for tap in row] for row in taps]


def beside(weights, planes):
    return [
        sum(weights[i][j][kind] * planes(kind, j) for j in range(2) for kind in range(2)) for i in range(2)
    ]


def load_kernel(wide, firsts, velocity, explicit, bands, inverse, spikes, *refs):
    edges, coef, weight, vel, tot, inverse_ends, spike_ends, here, there, taps, square, sems = refs
    groups = len(firsts)
    own = velocity.shape[1]
    rows = coef.shape[1]
    g = lax.axis_index("gz")
    moves = [(bands, taps), (velocity, here), (explicit, there)]
    for i, (low, tiles) in enumerate(((0, 0), (rows - 2, rows - 8))):
        moves.append((inverse.at[pl.ds(low, 2)], inverse_ends.at[pl.ds(2 * i, 2)]))
        moves.append((spikes.at[:, :, pl.ds(tiles, 8)], spike_ends.at[:, :, pl.ds(8 * i, 8)]))
    copies = [pltpu.make_async_copy(source, target, sems.at[i]) for i, (source, target) in enumerate(moves)]
    for copy in copies:
        copy.start()
    square[...] = jnp.zeros_like(square)
    vel[...] = jnp.zeros_like(vel)
    tot[...] = jnp.zeros_like(tot)
    copies[0].wait()
    for d in range(5):
        square[2 * d : 2 * d + 2, 0:rows] = taps[d]
    turned = jnp.transpose(square[...])
    for i in range(10):
        coef[i] = jnp.broadcast_to(turned[0:rows, i : i + 1], (rows, LANES))
    for k in range(groups):

        @pl.when(g == k)
        def _(first=firsts[k]):
            for i in range(10):
                weight[i] = coef[i, first : first + wide]

    copies[1].wait()
    copies[2].wait()
    for k in range(groups):

        @pl.when(g == k)
        def _(base=8 + k * own - firsts[k]):
            for f in range(3):
                vel[f, base : base + own] = here[f]
                tot[f, base : base + own] = here[f] + there[f]

    for f in range(3):
        for j in range(HALO):
            top, bottom = here[f, j : j + 1], here[f, own - HALO + j : own - HALO + j + 1]
            edges[6 + 3 * j + f : 7 + 3 * j + f] = jnp.where(g == 0, top, bottom)
            top += there[f, j : j + 1]
            bottom += there[f, own - HALO + j : own - HALO + j + 1]
            edges[3 * j + f : 3 * j + f + 1] = jnp.where(g == 0, top, bottom)
    for copy in copies[3:]:
        copy.wait()


def stencil(vel, tot, weights, f, wide, at):
    total = None
    for d in range(5):
        low = pl.ds(8 + d - 2, wide)
        term = weights[2 * d] * tot[f, low, at] + weights[2 * d + 1] * vel[f, low, at]
        total = term if total is None else total + term
    return total


def across_weights(bands):
    rows = bands.shape[2]
    core = lax.rem(lax.axis_index("gy"), 2)
    get = lambda tap, kind, row: jnp.broadcast_to(bands[tap, kind : kind + 1, row : row + 1], (1, LANES))
    none = jnp.zeros((1, LANES), F32)
    low = [[(0, 0), (1, 0)], [None, (0, 1)]]
    high = [[(4, rows - 2), None], [(3, rows - 1), (4, rows - 1)]]
    pick = lambda tap, kind: none if tap is None else get(tap[0], kind, tap[1])
    return [
        [[jnp.where(core == 0, pick(low[i][j], kind), pick(high[i][j], kind)) for kind in range(2)] for j in range(2)]
        for i in range(2)
    ]


def store_share(out, wide, tile, at, vel, tot, weights, edges, across):
    base = (3 * wide + 6) * tile
    for f in range(3):
        total = None
        for d in range(5):
            low = pl.ds(8 + d - 2, wide)
            term = weights[2 * d] * tot[f, low, at] + weights[2 * d + 1] * vel[f, low, at]
            total = term if total is None else total + term
        out[base + wide * f : base + wide * (f + 1)] = total
    side = beside(across, lambda kind, j: edges[6 * kind + 3 * j : 6 * kind + 3 * j + 3, at])
    for i in range(2):
        out[base + 3 * wide + 3 * i : base + 3 * wide + 3 * i + 3] = side[i]


def shares_kernel(wide, vel, tot, weight, edges, bands, *outs):
    groups = len(outs) + 1
    part = vel.shape[2] // groups
    g = lax.axis_index("gz")
    weights, across = [weight[i] for i in range(10)], across_weights(bands)
    for shift, out in enumerate(outs, 1):
        begin = lax.rem(g + shift, groups) * part
        for tile in range(part // LANES):
            at = pl.ds(pl.multiple_of(begin + LANES * tile, LANES), LANES)
            store_share(out, wide, tile, at, vel, tot, weights, edges, across)


def add_share(rhs, wide, firsts, source, piece):
    for k, first in enumerate(firsts):

        @pl.when(source == k)
        def _(first=first):
            for tile in range(rhs.shape[2] // LANES):
                for f in range(3):
                    row = (3 * wide + 6) * tile + wide * f
                    rhs[f, first : first + wide, LANES * tile : LANES * (tile + 1)] += piece[row : row + wide]


def own_kernel(wide, firsts, vel, tot, weight, edges, bands, inv4, fixed, rhs, values, side, started, share):
    lanes = rhs.shape[2]
    blocks = lanes // (2 * LANES)
    g = lax.axis_index("gz")
    weights, across = [weight[i] for i in range(10)], across_weights(bands)
    for tile in range(lanes // LANES):
        at = pl.ds(pl.multiple_of(g * lanes + LANES * tile, LANES), LANES)
        store_share(share, wide, tile, at, vel, tot, weights, edges, across)
        row = (3 * wide + 6) * tile + 3 * wide
        side[:, LANES * tile : LANES * (tile + 1)] = share[row : row + 6]
    rhs[...] = jnp.zeros_like(rhs)
    add_share(rhs, wide, firsts, g, share)
    for f in range(3):
        for r in range(4):
            row = (6 if r < 2 else 0) + 3 * (r % 2) + f
            values[row : row + 1] = jnp.sum(inv4[r] * rhs[f], axis=0, keepdims=True)
    started[...] = jnp.zeros_like(started)
    for b in range(blocks):
        at = FIRST * b
        started[at + STATE + 12 : at + FIRST] = fixed[(MAPS + 16) * b : (MAPS + 16) * (b + 1)]
    started[FIRST * blocks : FIRST * blocks + 8] = fixed[(MAPS + 16) * blocks : (MAPS + 16) * blocks + 8]


def store_planes(ref, at, planes):
    real, imaginary = apart(planes)
    for i in range(planes.shape[0] // 3):
        ref[at + 6 * i : at + 6 * i + 3] = real[3 * i : 3 * i + 3]
        ref[at + 6 * i + 3 : at + 6 * i + 6] = imaginary[3 * i : 3 * i + 3]


def planes_of(ref, at):
    return lambda kind, j: ref[at + 12 * kind + 6 * j : at + 12 * kind + 6 * j + 6]


def relay_kernel(groups, edges, beside_edges, *outs):
    core = lax.rem(lax.axis_index("gy"), 2)
    mine = jnp.where(lax.axis_index("gz") == 0, core == 0, core == 1)
    part = edges.shape[1] // groups
    for step, out in enumerate(outs):
        begin = (2 * step + 1 - core) * part
        for b in range(part // (2 * LANES)):
            at = pl.ds(pl.multiple_of(begin + 2 * LANES * b, 2 * LANES), 2 * LANES)
            store_planes(out, 24 * b, jnp.where(mine, edges[:, at], beside_edges[:, at]))


def prepare_kernel(inverse_ends, spike_ends, coef, inv4, fixed):
    rows, modes = inverse_ends.shape[1:]
    core = lax.rem(lax.axis_index("gy"), 2)
    gy, count = lax.axis_index("gy"), lax.axis_size("gy")
    lower, upper = side_weights(coef, False), side_weights(coef, True)
    used = jnp.where(core == 0, gy > 0, gy < count - 1)
    weights = (MAPS + 16) * (modes // LANES)
    for i in range(2):
        for j in range(2):
            for kind in range(2):
                at = weights + 4 * i + 2 * j + kind
                low, high = lower[i][j][kind], upper[i][j][kind]
                fixed[at : at + 1] = jnp.where(used, jnp.where(core == 0, low, high), 0.0)
    for b in range(modes // LANES):
        at, lanes = (MAPS + 16) * b, pl.ds(LANES * b, LANES)
        for k in range(2):
            for j in range(2):
                row = at + 2 * k + j
                fixed[row : row + 1] = -spike_ends[0, j, 14 + k : 15 + k, lanes]
                fixed[row + 4 : row + 5] = -spike_ends[0, j, k : k + 1, lanes]
                fixed[row + 8 : row + 9] = -spike_ends[1, j, k : k + 1, lanes]
        for r in range(4):
            inv4[r, :, 2 * LANES * b : 2 * LANES * (b + 1)] = doubled(inverse_ends[r, :, lanes])
            for i in range(2):
                low, high = inverse_ends[r, i : i + 1, lanes], inverse_ends[r, rows - 2 + i : rows - 1 + i, lanes]
                to = at + MAPS + 2 * ((r + 2) % 4) + i
                fixed[to : to + 1] = jnp.where(core == 0, high, low)
                fixed[to + 8 : to + 9] = jnp.where(core == 0, low, high)


def fetch_kernel(inverse, spikes, after, inside, held, sems):
    copies = [pltpu.make_async_copy(inverse, inside, sems.at[0]), pltpu.make_async_copy(spikes, held, sems.at[1])]
    for copy in copies:
        copy.start()
    for copy in copies:
        copy.wait()


def weights_of(ref):
    at = ref.shape[0] - 8
    return [
        [[ref[at + 4 * i + 2 * j + kind : at + 4 * i + 2 * j + kind + 1] for kind in range(2)] for j in range(2)]
        for i in range(2)
    ]


def interface_kernel(wide, firsts, inv4, started, own_values, own_side, *refs):
    groups = len(firsts)
    *pieces, message, values, side = refs
    tiles = values.shape[1] // LANES
    g = lax.axis_index("gz")
    core = lax.rem(lax.axis_index("gy"), 2)
    message[...] = started[...]
    values[...] = own_values[...]
    side[...] = own_side[...]
    for shift, piece in enumerate(pieces, 1):
        source = lax.rem(g - shift + groups, groups)
        for k, first in enumerate(firsts):

            @pl.when(source == k)
            def _(piece=piece, first=first):
                for tile in range(tiles):
                    to = pl.ds(LANES * tile, LANES)
                    for f in range(3):
                        row = (3 * wide + 6) * tile + wide * f
                        share = piece[row : row + wide]
                        for r in range(4):
                            row = (6 if r < 2 else 0) + 3 * (r % 2) + f
                            values[row : row + 1, to] += jnp.sum(
                                inv4[r, first : first + wide, to] * share, axis=0, keepdims=True
                            )

        @pl.when(source == jnp.where(core == 0, groups - 1, 0))
        def _(piece=piece):
            for tile in range(tiles):
                row = (3 * wide + 6) * tile + 3 * wide
                side[:, LANES * tile : LANES * (tile + 1)] = piece[row : row + 6]

    for b in range(tiles // 2):
        store_planes(message, FIRST * b, values[:, 2 * LANES * b : 2 * LANES * (b + 1)])
        store_planes(message, FIRST * b + STATE, side[:, 2 * LANES * b : 2 * LANES * (b + 1)])


class Piece:
    def __init__(self, ref, at):
        self.p = [ref[at : at + 6], ref[at + 6 : at + 12]]
        self.q = [ref[at + 12 : at + 18], ref[at + 18 : at + 24]]
        self.F, self.H, self.G = (matrix_of(ref, at + STATE + 4 * i) for i in range(3))


def matrix_of(ref, at):
    return [[ref[at + 2 * k + j : at + 2 * k + j + 1] for j in range(2)] for k in range(2)]


def act(matrix, vector, plus=None):
    out = [matrix[k][0] * vector[0] + matrix[k][1] * vector[1] for k in range(2)]
    return out if plus is None else [plus[k] + out[k] for k in range(2)]


def times(a, b, plus=None):
    out = [[a[k][0] * b[0][j] + a[k][1] * b[1][j] for j in range(2)] for k in range(2)]
    return out if plus is None else [[plus[k][j] + out[k][j] for j in range(2)] for k in range(2)]


def after(state, piece):
    if state is None:
        return piece.p, piece.F
    return act(piece.F, state[0], piece.p), times(piece.F, state[1])


def before(piece, state):
    if state is None:
        return piece.q, piece.H, piece.G
    q, H, G = state
    q = act(piece.G, act(H, piece.p, q), piece.q)
    H = times(piece.G, times(H, piece.F), piece.H)
    return q, H, times(piece.G, G)


def choose(flag, new, old):
    return jax.tree.map(lambda a, b: jnp.where(flag, a, b), new, old)


def store_run(ref, at, p, q, F, H, G):
    for i, vector in enumerate((p, q)):
        for k in range(2):
            ref[at + 12 * i + 6 * k : at + 12 * i + 6 * k + 6] = vector[k]
    for i, matrix in enumerate((F, H, G)):
        for k in range(2):
            for j in range(2):
                row = at + STATE + 4 * i + 2 * k + j
                ref[row : row + 1] = matrix[k][j]


def sort_pieces(base, pieces, board):
    size = len(pieces)
    position = lax.rem(lax.div(lax.axis_index("gy"), base), size)
    for i, piece in enumerate(pieces):
        board[jnp.bitwise_xor(position, (size - i) % size)] = piece[...]
    return position


def compose_kernel(base, *refs):
    *pieces, out, board = refs
    sort_pieces(base, pieces, board)
    for at in range(0, out.shape[0], RUN):
        run = [Piece(board.at[i], at) for i in range(len(pieces))]
        up = down = None
        for piece in run:
            up = after(up, piece)
        for piece in run[::-1]:
            down = before(piece, down)
        store_run(out, at, up[0], down[0], up[1], down[1], down[2])


def ends_kernel(*refs):
    *ends, out = refs
    step = lax.div(lax.axis_index("gz"), 2)
    end = ends[0][...]
    for i in range(1, len(ends)):
        end = jnp.where(step == i, ends[i][...], end)
    out[...] = end


def pair_kernel(mine, other, end_mine, end_other, out, fixed_mine, fixed_other):
    core = lax.rem(lax.axis_index("gy"), 2)
    blocks = out.shape[0] // RUN
    for ref, across, end, target in ((mine, other, end_mine, fixed_mine), (other, mine, end_other, fixed_other)):
        outer_weights = weights_of(ref)
        for b in range(blocks):
            at, to = FIRST * b, RUN * b
            inner = [across[at + STATE + 6 * i : at + STATE + 6 * i + 6] for i in range(2)]
            outer = beside(outer_weights, planes_of(end, 24 * b))
            target[to + STATE : to + RUN] = ref[at + 36 : at + 36 + MAPS]
            for k in range(4):
                value = ref[at + 6 * k : at + 6 * k + 6]
                for i in range(2):
                    row = at + 36 + MAPS + 2 * k + i
                    value = value + ref[row : row + 1] * inner[i] + ref[row + 8 : row + 9] * outer[i]
                target[to + 6 * k : to + 6 * k + 6] = value
    low = jnp.where(core == 0, fixed_mine[...], fixed_other[...])
    high = jnp.where(core == 0, fixed_other[...], fixed_mine[...])
    for at in range(0, out.shape[0], RUN):
        first, second = Piece(low, at), Piece(high, at)
        up, down = after(after(None, first), second), before(first, before(second, None))
        store_run(out, at, up[0], down[0], up[1], down[1], down[2])


def widen_kernel(base, start, *refs):
    *pieces, out, board = refs
    known_ref = None if start else pieces.pop()
    position = sort_pieces(base, pieces, board)
    for at in range(0, out.shape[0], RUN):
        run = [Piece(board.at[i], at) for i in range(len(pieces))]
        mine = Piece(pieces[0], at)
        one, none = jnp.ones_like(mine.F[0][0]), jnp.zeros_like(mine.F[0][0])
        zero = [jnp.zeros_like(mine.p[0])] * 2
        unit, blank = [[one, none], [none, one]], [[none, none], [none, none]]
        up, down = (zero, unit), (zero, blank, unit)
        for i, piece in enumerate(run[:-1]):
            up = choose(i < position, after(up, piece), up)
        for i in range(len(run) - 1, 0, -1):
            down = choose(i > position, before(run[i], down), down)
        (t, F), (q, H, G) = up, down
        e = act(H, act(mine.F, t, mine.p), q)
        E = times(H, times(mine.F, F))
        if start:
            store_run(out, at, t, e, F, E, G)
        else:
            known = Piece(known_ref, at)
            a, A, b, B, D = known.p, known.F, known.q, known.H, known.G
            store_run(
                out, at, act(A, t, a), act(D, e, act(B, t, b)), times(A, F), times(D, E, times(B, F)), times(D, G)
            )


def block_kernel(wide, firsts, inverse, own_rhs, mine, other, end, *refs):
    *pieces, local, rhs, split = refs
    fields, rows, lanes = rhs.shape
    g = lax.axis_index("gz")
    rhs[...] = own_rhs[...]
    for shift, piece in enumerate(pieces, 1):
        add_share(rhs, wide, firsts, lax.rem(g - shift + len(firsts), len(firsts)), piece)
    core = lax.rem(lax.axis_index("gy"), 2)
    outer_weights = weights_of(mine)
    flat = rhs[...].reshape(fields * rows, lanes)
    for b in range(lanes // (2 * LANES)):
        columns = pl.ds(2 * LANES * b, 2 * LANES)
        parts = apart(flat[:, 2 * LANES * b : 2 * LANES * (b + 1)])
        inner = [other[FIRST * b + STATE + 6 * i : FIRST * b + STATE + 6 * i + 6] for i in range(2)]
        outer = beside(outer_weights, planes_of(end, 24 * b))
        solved = []
        for p in range(2):
            split[...] = parts[p].reshape(fields, rows, LANES)
            for f in range(fields):
                for i in range(2):
                    one, two = inner[i][3 * p + f : 3 * p + f + 1], outer[i][3 * p + f : 3 * p + f + 1]
                    split[f, i : i + 1] += jnp.where(core == 0, two, one)
                    split[f, rows - 2 + i : rows - 1 + i] += jnp.where(core == 0, one, two)
            factors = inverse[:, :, LANES * b : LANES * (b + 1)]
            solved.append([jnp.sum(factors * split[f][None], axis=1) for f in range(fields)])
        for f in range(fields):
            local[f, :, columns] = together(solved[0][f], solved[1][f])


def last_message_kernel(base, composed, out):
    upper = lax.rem(lax.div(lax.axis_index("gy"), base), 2) == 1
    for b in range(out.shape[0] // LAST):
        at, to = RUN * b, LAST * b
        out[to : to + 12] = jnp.where(upper, composed[at + 12 : at + 24], composed[at : at + 12])
        out[to + 12 : to + 16] = composed[at + STATE + 4 : at + STATE + 8]


def ready_kernel(base, local, spikes, known, ready, lift):
    upper = lax.rem(lax.div(lax.axis_index("gy"), base), 2) == 1
    for b in range(known.shape[0] // RUN):
        columns = pl.ds(2 * LANES * b, 2 * LANES)
        factors = [[doubled(spikes[i, k, :, LANES * b : LANES * (b + 1)]) for k in range(2)] for i in range(2)]
        run = Piece(known, RUN * b)
        maps = doubled(known[RUN * b + STATE : RUN * (b + 1)])
        A, B, D = (matrix_of(maps, 4 * i) for i in range(3))
        t, s = ([together(v[k][0:3], v[k][3:6]) for k in range(2)] for v in (run.p, run.q))
        for f in range(3):
            value = local[f, :, columns]
            for k in range(2):
                value = value - factors[0][k] * t[k][f : f + 1] - factors[1][k] * s[k][f : f + 1]
            ready[f, :, columns] = value
        for j in range(2):
            value = jnp.zeros_like(factors[0][0])
            for k in range(2):
                through_t = factors[0][k] * A[k][j] + factors[1][k] * B[k][j]
                value = value - jnp.where(upper, through_t, factors[1][k] * D[k][j])
            lift[j, :, columns] = value


def final_kernel(base, ready, lift, composed, received, out, held, sems):
    upper = lax.rem(lax.div(lax.axis_index("gy"), base), 2) == 1
    states = []
    for b in range(composed.shape[0] // RUN):
        at, to = RUN * b, LAST * b
        mine = [composed[at : at + 6], composed[at + 6 : at + 12]]
        theirs = [received[to : to + 6], received[to + 6 : to + 12]]
        state = choose(upper, theirs, act(matrix_of(received, to + 12), mine, theirs))
        states.append([together(v[0:3], v[3:6]) for v in state])
    copies = []
    for f in range(3):
        for b, state in enumerate(states):
            columns = pl.ds(2 * LANES * b, 2 * LANES)
            value = ready[f, :, columns]
            for j in range(2):
                value = value + lift[j, :, columns] * state[j][f : f + 1]
            held[f, :, columns] = value
        copies.append(pltpu.make_async_copy(held.at[f], out.at[f], sems.at[f]))
        copies[-1].start()
    for copy in copies:
        copy.wait()


def end_pairs(gy, gz, step):
    at = lambda y, z: y * gz + z
    pairs = []
    for y in range(1, gy - 1, 2):
        for core in range(2):
            column = 2 * step + 1 - core
            pairs.append((at(y - 1 + core, gz - 1), at(y + 1, column)))
            pairs.append((at(y + 1 + core, 0), at(y, column)))
    sources = sorted(set(range(gy * gz)) - {s for s, _ in pairs})
    targets = sorted(set(range(gy * gz)) - {t for _, t in pairs})
    if gz == 2:
        for i in range(0, len(sources), 2):
            (a, b), (c, d) = sources[i : i + 2], targets[i : i + 2]
            pairs += [(a, d), (b, c)] if a != d and b != c else [(a, c), (b, d)]
    return pairs


def groups_of(count):
    steps, base = [(1, 2)], 2
    while 2 * base < count:
        size = 4 if base * 8 <= count else 2
        steps.append((base, size))
        base *= size
    return steps + [(base, 2)]


def per_device(velocity, explicit, bands, inverse, spikes):
    gy, gz = lax.axis_size("gy"), lax.axis_size("gz")
    own, columns = velocity.shape[1:]
    rows, modes = inverse.shape[0], inverse.shape[2]
    lanes = 2 * modes
    wide, firsts = window(rows, own, gz)
    vmem = lambda *shape: pltpu.VMEM(shape, F32)
    dma = lambda n: pltpu.SemaphoreType.DMA((n,))

    blocks = modes // LANES
    taps = jnp.transpose(bands, (1, 0, 2))
    to_core = lambda x: lax.ppermute(x, "gy", [(i, i ^ 1) for i in range(gy)])
    beside_taps = to_core(taps)
    padded = (3, rows + 16, columns)
    edges, coef, weight, vel, tot, inverse_ends, spike_ends = vmem_call(
        functools.partial(load_kernel, wide, firsts),
        [(12, columns), (10, rows, LANES), (10, wide, LANES), padded, padded, (4, rows, modes), (2, 2, 16, modes)],
        [velocity, explicit, taps, inverse, spikes],
        scratch=[vmem(3, own, columns)] * 2 + [vmem(5, 2, rows), vmem(LANES, LANES), dma(7)],
        flops=2 * 10**10,
        name="load",
        far=5,
    )
    beside_edges = to_core(edges)
    share = ((3 * wide + 6) * 2 * blocks, LANES)
    shares = vmem_call(
        functools.partial(shares_kernel, wide),
        [share] * (gz - 1),
        [vel, tot, weight, edges, beside_taps],
        flops=2 * 10**10,
        name="shares",
    )
    pieces = [
        lax.ppermute(x, "gz", [(i, (i + shift) % gz) for i in range(gz)]) for shift, x in enumerate(shares, 1)
    ]
    relays = vmem_call(
        functools.partial(relay_kernel, gz), [(24 * blocks, LANES)] * (gz // 2), [edges, beside_edges], name="relay"
    )
    ends = [lax.ppermute(x, ("gy", "gz"), end_pairs(gy, gz, step)) for step, x in enumerate(relays)]
    inv4, fixed = vmem_call(
        prepare_kernel,
        [(4, rows, lanes), ((MAPS + 16) * blocks + 8, LANES)],
        [inverse_ends, spike_ends, coef],
        flops=2 * 10**10,
        name="prepare",
    )
    first = (FIRST * blocks + 8, LANES)
    rhs, values, side, started = vmem_call(
        functools.partial(own_kernel, wide, firsts),
        [(3, rows, lanes), (12, lanes), (6, lanes), first],
        [vel, tot, weight, edges, beside_taps, inv4, fixed],
        scratch=[vmem(*share)],
        flops=2 * 10**8,
        name="own",
    )
    (message,) = vmem_call(
        functools.partial(interface_kernel, wide, firsts),
        [first],
        [inv4, started, values, side, *pieces],
        scratch=[vmem(12, lanes), vmem(6, lanes)],
        name="interface",
    )
    other = to_core(message)
    (end,) = vmem_call(ends_kernel, [(24 * blocks, LANES)], ends, flops=2 * 10**10, name="ends")
    other_end = to_core(end)
    run = (RUN * blocks, LANES)
    composed, mine, theirs = vmem_call(pair_kernel, [run] * 3, [message, other, end, other_end], name="pair")

    inside, held = vmem_call(
        fetch_kernel,
        [(rows, rows, modes), (2, 2, rows, modes)],
        [inverse, spikes, composed],
        scratch=[dma(2)],
        flops=2 * 10**10,
        name="fetch",
        far=2,
    )
    steps = groups_of(gy)
    base, size = steps[0]
    (known,) = vmem_call(
        functools.partial(widen_kernel, base, True),
        [run],
        [mine, theirs],
        scratch=[vmem(size, *run)],
        flops=10**7,
        name="widen",
    )
    (local,) = vmem_call(
        functools.partial(block_kernel, wide, firsts),
        [(3, rows, lanes)],
        [inside, rhs, message, other, end, *pieces],
        scratch=[vmem(3, rows, lanes), vmem(3, rows, LANES)],
        flops=2 * 10**8,
        name="block",
    )
    for base, size in steps[1:-1]:
        gathered = [composed]
        for x in range(size - 1, 0, -1):
            gathered.append(lax.ppermute(composed, "gy", [(i, i ^ (x * base) ^ 1) for i in range(gy)]))
        board = [vmem(size, *run)]
        (composed,) = vmem_call(
            functools.partial(compose_kernel, base), [run], gathered, scratch=board, name="compose"
        )
        (known,) = vmem_call(
            functools.partial(widen_kernel, base, False),
            [run],
            [*gathered, known],
            scratch=board,
            flops=10**7,
            name="widen",
        )
    base, _ = steps[-1]
    (message,) = vmem_call(
        functools.partial(last_message_kernel, base), [(LAST * blocks, LANES)], [composed], name="last_message"
    )
    received = lax.ppermute(message, "gy", [(i, i ^ base ^ 1) for i in range(gy)])
    ready, lift = vmem_call(
        functools.partial(ready_kernel, base),
        [(3, rows, lanes), (2, rows, lanes)],
        [local, held, known],
        flops=10**7,
        name="ready",
    )
    (out,) = vmem_call(
        functools.partial(final_kernel, base),
        [(3, rows, lanes)],
        [ready, lift, composed, received],
        scratch=[vmem(3, rows, lanes), dma(3)],
        name="final",
        far_out=True,
    )
    return out


def solution(mesh):
    placed = (
        P(None, ("gy", "gz"), None),
        P(None, ("gy", "gz"), None),
        P(None, None, "gy"),
        P("gy", None, "gz"),
        P(None, None, "gy", "gz"),
    )
    return jax.shard_map(
        per_device, mesh=mesh, in_specs=placed, out_specs=P(None, "gy", "gz"), check_vma=False
    )
```

```python
import functools

import jax
import jax.numpy as jnp
from jax import lax
from jax.experimental import pallas as pl
from jax.experimental.pallas import tpu as pltpu
from jax.sharding import PartitionSpec as P

F32 = jnp.float32
LANES = 128
HALO = 2


def vmem_call(body, out_shapes, args, scratch=(), flops=0, name=None, far=0, far_out=False):
    near, away = pl.BlockSpec(memory_space=pltpu.VMEM), pl.BlockSpec(memory_space=pltpu.HBM)
    nbytes = sum(a.size * 4 for a in args)
    args = [pltpu.with_memory_space_constraint(a, pltpu.HBM) for a in args[:far]] + args[far:]
    return pl.pallas_call(
        body,
        out_shape=[jax.ShapeDtypeStruct(s, F32) for s in out_shapes],
        in_specs=[away] * far + [near] * (len(args) - far),
        out_specs=[away if far_out else near] * len(out_shapes),
        scratch_shapes=list(scratch),
        compiler_params=pltpu.CompilerParams(vmem_limit_bytes=16 * 2**20),
        cost_estimate=pl.CostEstimate(flops=flops, bytes_accessed=nbytes, transcendentals=0),
        name=name,
    )(*args)


def window(rows, own, groups):
    spans = [(max(g * own - HALO, 0), min(g * own + own + HALO, rows)) for g in range(groups)]
    wide = max(high - low for low, high in spans)
    return wide, [min(low, rows - wide) for low, _ in spans]


def lane_of(x):
    return lax.broadcasted_iota(jnp.int32, (x.shape[0], LANES), 1)


def take(x, lanes):
    return jnp.take_along_axis(x, lanes, axis=1, mode="promise_in_bounds")


def apart(x):
    lane = lane_of(x)
    low = lane < LANES // 2
    even = jnp.where(low, 2 * lane, 2 * lane - (LANES - 1))
    odd = jnp.where(low, 2 * lane + 1, 2 * lane - LANES)
    a, b = x[:, :LANES], x[:, LANES:]
    return jnp.where(low, take(a, even), take(b, odd)), jnp.where(low, take(a, odd), take(b, even))


def together(real, imaginary):
    lane = lane_of(real)
    half, odd = lax.shift_right_logical(lane, 1), jnp.bitwise_and(lane, 1) == 1
    parts = [
        jnp.where(odd, take(imaginary, half + at), take(real, half + at)) for at in (0, LANES // 2)
    ]
    return jnp.concatenate(parts, axis=1)


def doubled(x):
    half = lax.shift_right_logical(lane_of(x), 1)
    return jnp.concatenate([take(x, half), take(x, half + LANES // 2)], axis=1)


STATE = 24
MAPS = 12
RUN = STATE + MAPS
FIRST = STATE + 24 + MAPS + 16
LAST = 16


def side_weights(coef, upper):
    rows = coef.shape[1]
    if upper:
        taps = [[(4, rows - 2), None], [(3, rows - 1), (4, rows - 1)]]
    else:
        taps = [[(0, 0), (1, 0)], [None, (0, 1)]]
    none = jnp.zeros((1, LANES), F32)
    get = lambda tap, kind: none if tap is None else coef[2 * tap[0] + kind, tap[1] : tap[1] + 1]
    return [[[get(tap, kind) for kind in range(2)] for tap in row] for row in taps]


def beside(weights, planes):
    return [
        sum(weights[i][j][kind] * planes(kind, j) for j in range(2) for kind in range(2)) for i in range(2)
    ]


def load_kernel(wide, firsts, velocity, explicit, bands, inverse, spikes, *refs):
    edges, coef, weight, vel, tot, inverse_ends, spike_ends, here, there, taps, square, sems = refs
    groups = len(firsts)
    own = velocity.shape[1]
    rows = coef.shape[1]
    g = lax.axis_index("gz")
    moves = [(bands, taps), (velocity, here), (explicit, there)]
    for i, (low, tiles) in enumerate(((0, 0), (rows - 2, rows - 8))):
        moves.append((inverse.at[pl.ds(low, 2)], inverse_ends.at[pl.ds(2 * i, 2)]))
        moves.append((spikes.at[:, :, pl.ds(tiles, 8)], spike_ends.at[:, :, pl.ds(8 * i, 8)]))
    copies = [pltpu.make_async_copy(source, target, sems.at[i]) for i, (source, target) in enumerate(moves)]
    for copy in copies:
        copy.start()
    square[...] = jnp.zeros_like(square)
    vel[...] = jnp.zeros_like(vel)
    tot[...] = jnp.zeros_like(tot)
    copies[0].wait()
    for d in range(5):
        square[2 * d : 2 * d + 2, 0:rows] = taps[d]
    turned = jnp.transpose(square[...])
    for i in range(10):
        coef[i] = jnp.broadcast_to(turned[0:rows, i : i + 1], (rows, LANES))
    for k in range(groups):

        @pl.when(g == k)
        def _(first=firsts[k]):
            for i in range(10):
                weight[i] = coef[i, first : first + wide]

    copies[1].wait()
    copies[2].wait()
    for k in range(groups):

        @pl.when(g == k)
        def _(base=8 + k * own - firsts[k]):
            for f in range(3):
                vel[f, base : base + own] = here[f]
                tot[f, base : base + own] = here[f] + there[f]

    for f in range(3):
        for j in range(HALO):
            top, bottom = here[f, j : j + 1], here[f, own - HALO + j : own - HALO + j + 1]
            edges[6 + 3 * j + f : 7 + 3 * j + f] = jnp.where(g == 0, top, bottom)
            top += there[f, j : j + 1]
            bottom += there[f, own - HALO + j : own - HALO + j + 1]
            edges[3 * j + f : 3 * j + f + 1] = jnp.where(g == 0, top, bottom)
    for copy in copies[3:]:
        copy.wait()


def stencil(vel, tot, weights, f, wide, at):
    total = None
    for d in range(5):
        low = pl.ds(8 + d - 2, wide)
        term = weights[2 * d] * tot[f, low, at] + weights[2 * d + 1] * vel[f, low, at]
        total = term if total is None else total + term
    return total


def store_share(out, wide, tile, at, vel, tot, weights, edges):
    base = (3 * wide + 12) * tile
    for f in range(3):
        total = None
        for d in range(5):
            low = pl.ds(8 + d - 2, wide)
            term = weights[2 * d] * tot[f, low, at] + weights[2 * d + 1] * vel[f, low, at]
            total = term if total is None else total + term
        out[base + wide * f : base + wide * (f + 1)] = total
    out[base + 3 * wide : base + 3 * wide + 12] = edges[:, at]


def shares_kernel(wide, vel, tot, weight, edges, *outs):
    groups = len(outs) + 1
    part = vel.shape[2] // groups
    g = lax.axis_index("gz")
    weights = [weight[i] for i in range(10)]
    for shift, out in enumerate(outs, 1):
        begin = lax.rem(g + shift, groups) * part
        for tile in range(part // LANES):
            at = pl.ds(pl.multiple_of(begin + LANES * tile, LANES), LANES)
            store_share(out, wide, tile, at, vel, tot, weights, edges)


def add_share(rhs, wide, firsts, source, piece):
    for k, first in enumerate(firsts):

        @pl.when(source == k)
        def _(first=first):
            for tile in range(rhs.shape[2] // LANES):
                for f in range(3):
                    row = (3 * wide + 12) * tile + wide * f
                    rhs[f, first : first + wide, LANES * tile : LANES * (tile + 1)] += piece[row : row + wide]


def own_kernel(wide, firsts, vel, tot, weight, edges, inv4, fixed, rhs, values, side, started, share):
    lanes = rhs.shape[2]
    blocks = lanes // (2 * LANES)
    g = lax.axis_index("gz")
    weights = [weight[i] for i in range(10)]
    for tile in range(lanes // LANES):
        at = pl.ds(pl.multiple_of(g * lanes + LANES * tile, LANES), LANES)
        store_share(share, wide, tile, at, vel, tot, weights, edges)
        row = (3 * wide + 12) * tile + 3 * wide
        side[:, LANES * tile : LANES * (tile + 1)] = share[row : row + 12]
    rhs[...] = jnp.zeros_like(rhs)
    add_share(rhs, wide, firsts, g, share)
    for f in range(3):
        for r in range(4):
            row = (6 if r < 2 else 0) + 3 * (r % 2) + f
            values[row : row + 1] = jnp.sum(inv4[r] * rhs[f], axis=0, keepdims=True)
    started[...] = jnp.zeros_like(started)
    for b in range(blocks):
        at = FIRST * b
        started[at + STATE + 24 : at + FIRST] = fixed[(MAPS + 16) * b : (MAPS + 16) * (b + 1)]
    started[FIRST * blocks : FIRST * blocks + 16] = fixed[(MAPS + 16) * blocks : (MAPS + 16) * blocks + 16]


def store_planes(ref, at, planes):
    real, imaginary = apart(planes)
    for i in range(planes.shape[0] // 3):
        ref[at + 6 * i : at + 6 * i + 3] = real[3 * i : 3 * i + 3]
        ref[at + 6 * i + 3 : at + 6 * i + 6] = imaginary[3 * i : 3 * i + 3]


def planes_of(ref, at):
    return lambda kind, j: ref[at + 12 * kind + 6 * j : at + 12 * kind + 6 * j + 6]


def relay_kernel(groups, edges, beside_edges, *outs):
    core = lax.rem(lax.axis_index("gy"), 2)
    mine = jnp.where(lax.axis_index("gz") == 0, core == 0, core == 1)
    part = edges.shape[1] // groups
    for step, out in enumerate(outs):
        begin = (2 * step + 1 - core) * part
        for b in range(part // (2 * LANES)):
            at = pl.ds(pl.multiple_of(begin + 2 * LANES * b, 2 * LANES), 2 * LANES)
            store_planes(out, 24 * b, jnp.where(mine, edges[:, at], beside_edges[:, at]))


def prepare_kernel(inverse_ends, spike_ends, coef, inv4, fixed):
    rows, modes = inverse_ends.shape[1:]
    core = lax.rem(lax.axis_index("gy"), 2)
    gy, count = lax.axis_index("gy"), lax.axis_size("gy")
    lower, upper = side_weights(coef, False), side_weights(coef, True)
    used = jnp.where(core == 0, gy > 0, gy < count - 1)
    weights = (MAPS + 16) * (modes // LANES)
    for i in range(2):
        for j in range(2):
            for kind in range(2):
                at = weights + 4 * i + 2 * j + kind
                low, high = lower[i][j][kind], upper[i][j][kind]
                fixed[at : at + 1] = jnp.where(core == 0, high, low)
                fixed[at + 8 : at + 9] = jnp.where(used, jnp.where(core == 0, low, high), 0.0)
    for b in range(modes // LANES):
        at, lanes = (MAPS + 16) * b, pl.ds(LANES * b, LANES)
        for k in range(2):
            for j in range(2):
                row = at + 2 * k + j
                fixed[row : row + 1] = -spike_ends[0, j, 14 + k : 15 + k, lanes]
                fixed[row + 4 : row + 5] = -spike_ends[0, j, k : k + 1, lanes]
                fixed[row + 8 : row + 9] = -spike_ends[1, j, k : k + 1, lanes]
        for r in range(4):
            inv4[r, :, 2 * LANES * b : 2 * LANES * (b + 1)] = doubled(inverse_ends[r, :, lanes])
            for i in range(2):
                low, high = inverse_ends[r, i : i + 1, lanes], inverse_ends[r, rows - 2 + i : rows - 1 + i, lanes]
                to = at + MAPS + 2 * ((r + 2) % 4) + i
                fixed[to : to + 1] = jnp.where(core == 0, high, low)
                fixed[to + 8 : to + 9] = jnp.where(core == 0, low, high)


def fetch_kernel(inverse, spikes, after, inside, held, sems):
    copies = [pltpu.make_async_copy(inverse, inside, sems.at[0]), pltpu.make_async_copy(spikes, held, sems.at[1])]
    for copy in copies:
        copy.start()
    for copy in copies:
        copy.wait()


def weights_of(ref, at):
    at += ref.shape[0] - 16
    return [
        [[ref[at + 4 * i + 2 * j + kind : at + 4 * i + 2 * j + kind + 1] for kind in range(2)] for j in range(2)]
        for i in range(2)
    ]


def interface_kernel(wide, firsts, inv4, started, own_values, own_side, *refs):
    groups = len(firsts)
    *pieces, message, values, side = refs
    tiles = values.shape[1] // LANES
    g = lax.axis_index("gz")
    core = lax.rem(lax.axis_index("gy"), 2)
    message[...] = started[...]
    values[...] = own_values[...]
    side[...] = own_side[...]
    for shift, piece in enumerate(pieces, 1):
        source = lax.rem(g - shift + groups, groups)
        for k, first in enumerate(firsts):

            @pl.when(source == k)
            def _(piece=piece, first=first):
                for tile in range(tiles):
                    to = pl.ds(LANES * tile, LANES)
                    for f in range(3):
                        row = (3 * wide + 12) * tile + wide * f
                        share = piece[row : row + wide]
                        for r in range(4):
                            row = (6 if r < 2 else 0) + 3 * (r % 2) + f
                            values[row : row + 1, to] += jnp.sum(
                                inv4[r, first : first + wide, to] * share, axis=0, keepdims=True
                            )

        @pl.when(source == jnp.where(core == 0, groups - 1, 0))
        def _(piece=piece):
            for tile in range(tiles):
                row = (3 * wide + 12) * tile + 3 * wide
                side[:, LANES * tile : LANES * (tile + 1)] = piece[row : row + 12]

    for b in range(tiles // 2):
        store_planes(message, FIRST * b, values[:, 2 * LANES * b : 2 * LANES * (b + 1)])
        store_planes(message, FIRST * b + STATE, side[:, 2 * LANES * b : 2 * LANES * (b + 1)])


class Piece:
    def __init__(self, ref, at):
        self.p = [ref[at : at + 6], ref[at + 6 : at + 12]]
        self.q = [ref[at + 12 : at + 18], ref[at + 18 : at + 24]]
        self.F, self.H, self.G = (matrix_of(ref, at + STATE + 4 * i) for i in range(3))


def matrix_of(ref, at):
    return [[ref[at + 2 * k + j : at + 2 * k + j + 1] for j in range(2)] for k in range(2)]


def act(matrix, vector, plus=None):
    out = [matrix[k][0] * vector[0] + matrix[k][1] * vector[1] for k in range(2)]
    return out if plus is None else [plus[k] + out[k] for k in range(2)]


def times(a, b, plus=None):
    out = [[a[k][0] * b[0][j] + a[k][1] * b[1][j] for j in range(2)] for k in range(2)]
    return out if plus is None else [[plus[k][j] + out[k][j] for j in range(2)] for k in range(2)]


def after(state, piece):
    if state is None:
        return piece.p, piece.F
    return act(piece.F, state[0], piece.p), times(piece.F, state[1])


def before(piece, state):
    if state is None:
        return piece.q, piece.H, piece.G
    q, H, G = state
    q = act(piece.G, act(H, piece.p, q), piece.q)
    H = times(piece.G, times(H, piece.F), piece.H)
    return q, H, times(piece.G, G)


def choose(flag, new, old):
    return jax.tree.map(lambda a, b: jnp.where(flag, a, b), new, old)


def store_run(ref, at, p, q, F, H, G):
    for i, vector in enumerate((p, q)):
        for k in range(2):
            ref[at + 12 * i + 6 * k : at + 12 * i + 6 * k + 6] = vector[k]
    for i, matrix in enumerate((F, H, G)):
        for k in range(2):
            for j in range(2):
                row = at + STATE + 4 * i + 2 * k + j
                ref[row : row + 1] = matrix[k][j]


def sort_pieces(base, pieces, board):
    size = len(pieces)
    position = lax.rem(lax.div(lax.axis_index("gy"), base), size)
    for i, piece in enumerate(pieces):
        board[jnp.bitwise_xor(position, (size - i) % size)] = piece[...]
    return position


def compose_kernel(base, *refs):
    *pieces, out, board = refs
    sort_pieces(base, pieces, board)
    for at in range(0, out.shape[0], RUN):
        run = [Piece(board.at[i], at) for i in range(len(pieces))]
        up = down = None
        for piece in run:
            up = after(up, piece)
        for piece in run[::-1]:
            down = before(piece, down)
        store_run(out, at, up[0], down[0], up[1], down[1], down[2])


def ends_kernel(*refs):
    *ends, out = refs
    step = lax.div(lax.axis_index("gz"), 2)
    end = ends[0][...]
    for i in range(1, len(ends)):
        end = jnp.where(step == i, ends[i][...], end)
    out[...] = end


def pair_kernel(mine, other, end_mine, end_other, out, fixed_mine, fixed_other):
    core = lax.rem(lax.axis_index("gy"), 2)
    blocks = out.shape[0] // RUN
    for ref, across, end, target in ((mine, other, end_mine, fixed_mine), (other, mine, end_other, fixed_other)):
        inner_weights, outer_weights = weights_of(ref, 0), weights_of(ref, 8)
        for b in range(blocks):
            at, to = FIRST * b, RUN * b
            inner = beside(inner_weights, planes_of(across, at + STATE))
            outer = beside(outer_weights, planes_of(end, 24 * b))
            target[to + STATE : to + RUN] = ref[at + 48 : at + 48 + MAPS]
            for k in range(4):
                value = ref[at + 6 * k : at + 6 * k + 6]
                for i in range(2):
                    row = at + 48 + MAPS + 2 * k + i
                    value = value + ref[row : row + 1] * inner[i] + ref[row + 8 : row + 9] * outer[i]
                target[to + 6 * k : to + 6 * k + 6] = value
    low = jnp.where(core == 0, fixed_mine[...], fixed_other[...])
    high = jnp.where(core == 0, fixed_other[...], fixed_mine[...])
    for at in range(0, out.shape[0], RUN):
        first, second = Piece(low, at), Piece(high, at)
        up, down = after(after(None, first), second), before(first, before(second, None))
        store_run(out, at, up[0], down[0], up[1], down[1], down[2])


def widen_kernel(base, start, *refs):
    *pieces, out, board = refs
    known_ref = None if start else pieces.pop()
    position = sort_pieces(base, pieces, board)
    for at in range(0, out.shape[0], RUN):
        run = [Piece(board.at[i], at) for i in range(len(pieces))]
        mine = Piece(pieces[0], at)
        one, none = jnp.ones_like(mine.F[0][0]), jnp.zeros_like(mine.F[0][0])
        zero = [jnp.zeros_like(mine.p[0])] * 2
        unit, blank = [[one, none], [none, one]], [[none, none], [none, none]]
        up, down = (zero, unit), (zero, blank, unit)
        for i, piece in enumerate(run[:-1]):
            up = choose(i < position, after(up, piece), up)
        for i in range(len(run) - 1, 0, -1):
            down = choose(i > position, before(run[i], down), down)
        (t, F), (q, H, G) = up, down
        e = act(H, act(mine.F, t, mine.p), q)
        E = times(H, times(mine.F, F))
        if start:
            store_run(out, at, t, e, F, E, G)
        else:
            known = Piece(known_ref, at)
            a, A, b, B, D = known.p, known.F, known.q, known.H, known.G
            store_run(
                out, at, act(A, t, a), act(D, e, act(B, t, b)), times(A, F), times(D, E, times(B, F)), times(D, G)
            )


def block_kernel(wide, firsts, inverse, own_rhs, mine, other, end, *refs):
    *pieces, local, rhs, split = refs
    fields, rows, lanes = rhs.shape
    g = lax.axis_index("gz")
    rhs[...] = own_rhs[...]
    for shift, piece in enumerate(pieces, 1):
        add_share(rhs, wide, firsts, lax.rem(g - shift + len(firsts), len(firsts)), piece)
    core = lax.rem(lax.axis_index("gy"), 2)
    inner_weights, outer_weights = weights_of(mine, 0), weights_of(mine, 8)
    flat = rhs[...].reshape(fields * rows, lanes)
    for b in range(lanes // (2 * LANES)):
        columns = pl.ds(2 * LANES * b, 2 * LANES)
        parts = apart(flat[:, 2 * LANES * b : 2 * LANES * (b + 1)])
        inner = beside(inner_weights, planes_of(other, FIRST * b + STATE))
        outer = beside(outer_weights, planes_of(end, 24 * b))
        solved = []
        for p in range(2):
            split[...] = parts[p].reshape(fields, rows, LANES)
            for f in range(fields):
                for i in range(2):
                    one, two = inner[i][3 * p + f : 3 * p + f + 1], outer[i][3 * p + f : 3 * p + f + 1]
                    split[f, i : i + 1] += jnp.where(core == 0, two, one)
                    split[f, rows - 2 + i : rows - 1 + i] += jnp.where(core == 0, one, two)
            factors = inverse[:, :, LANES * b : LANES * (b + 1)]
            solved.append([jnp.sum(factors * split[f][None], axis=1) for f in range(fields)])
        for f in range(fields):
            local[f, :, columns] = together(solved[0][f], solved[1][f])


def last_message_kernel(base, composed, out):
    upper = lax.rem(lax.div(lax.axis_index("gy"), base), 2) == 1
    for b in range(out.shape[0] // LAST):
        at, to = RUN * b, LAST * b
        out[to : to + 12] = jnp.where(upper, composed[at + 12 : at + 24], composed[at : at + 12])
        out[to + 12 : to + 16] = composed[at + STATE + 4 : at + STATE + 8]


def ready_kernel(base, local, spikes, known, ready, lift):
    upper = lax.rem(lax.div(lax.axis_index("gy"), base), 2) == 1
    for b in range(known.shape[0] // RUN):
        columns = pl.ds(2 * LANES * b, 2 * LANES)
        factors = [[doubled(spikes[i, k, :, LANES * b : LANES * (b + 1)]) for k in range(2)] for i in range(2)]
        run = Piece(known, RUN * b)
        maps = doubled(known[RUN * b + STATE : RUN * (b + 1)])
        A, B, D = (matrix_of(maps, 4 * i) for i in range(3))
        t, s = ([together(v[k][0:3], v[k][3:6]) for k in range(2)] for v in (run.p, run.q))
        for f in range(3):
            value = local[f, :, columns]
            for k in range(2):
                value = value - factors[0][k] * t[k][f : f + 1] - factors[1][k] * s[k][f : f + 1]
            ready[f, :, columns] = value
        for j in range(2):
            value = jnp.zeros_like(factors[0][0])
            for k in range(2):
                through_t = factors[0][k] * A[k][j] + factors[1][k] * B[k][j]
                value = value - jnp.where(upper, through_t, factors[1][k] * D[k][j])
            lift[j, :, columns] = value


def final_kernel(base, ready, lift, composed, received, out, held, sems):
    upper = lax.rem(lax.div(lax.axis_index("gy"), base), 2) == 1
    states = []
    for b in range(composed.shape[0] // RUN):
        at, to = RUN * b, LAST * b
        mine = [composed[at : at + 6], composed[at + 6 : at + 12]]
        theirs = [received[to : to + 6], received[to + 6 : to + 12]]
        state = choose(upper, theirs, act(matrix_of(received, to + 12), mine, theirs))
        states.append([together(v[0:3], v[3:6]) for v in state])
    copies = []
    for f in range(3):
        for b, state in enumerate(states):
            columns = pl.ds(2 * LANES * b, 2 * LANES)
            value = ready[f, :, columns]
            for j in range(2):
                value = value + lift[j, :, columns] * state[j][f : f + 1]
            held[f, :, columns] = value
        copies.append(pltpu.make_async_copy(held.at[f], out.at[f], sems.at[f]))
        copies[-1].start()
    for copy in copies:
        copy.wait()


def end_pairs(gy, gz, step):
    at = lambda y, z: y * gz + z
    pairs = []
    for y in range(1, gy - 1, 2):
        for core in range(2):
            column = 2 * step + 1 - core
            pairs.append((at(y - 1 + core, gz - 1), at(y + 1, column)))
            pairs.append((at(y + 1 + core, 0), at(y, column)))
    sources = sorted(set(range(gy * gz)) - {s for s, _ in pairs})
    targets = sorted(set(range(gy * gz)) - {t for _, t in pairs})
    if gz == 2:
        for i in range(0, len(sources), 2):
            (a, b), (c, d) = sources[i : i + 2], targets[i : i + 2]
            pairs += [(a, d), (b, c)] if a != d and b != c else [(a, c), (b, d)]
    return pairs


def groups_of(count):
    steps, base = [(1, 2)], 2
    while 2 * base < count:
        size = 4 if base * 8 <= count else 2
        steps.append((base, size))
        base *= size
    return steps + [(base, 2)]


def per_device(velocity, explicit, bands, inverse, spikes):
    gy, gz = lax.axis_size("gy"), lax.axis_size("gz")
    own, columns = velocity.shape[1:]
    rows, modes = inverse.shape[0], inverse.shape[2]
    lanes = 2 * modes
    wide, firsts = window(rows, own, gz)
    vmem = lambda *shape: pltpu.VMEM(shape, F32)
    dma = lambda n: pltpu.SemaphoreType.DMA((n,))

    blocks = modes // LANES
    taps = jnp.transpose(bands, (1, 0, 2))
    to_core = lambda x: lax.ppermute(x, "gy", [(i, i ^ 1) for i in range(gy)])
    padded = (3, rows + 16, columns)
    edges, coef, weight, vel, tot, inverse_ends, spike_ends = vmem_call(
        functools.partial(load_kernel, wide, firsts),
        [(12, columns), (10, rows, LANES), (10, wide, LANES), padded, padded, (4, rows, modes), (2, 2, 16, modes)],
        [velocity, explicit, taps, inverse, spikes],
        scratch=[vmem(3, own, columns)] * 2 + [vmem(5, 2, rows), vmem(LANES, LANES), dma(7)],
        flops=2 * 10**10,
        name="load",
        far=5,
    )
    beside_edges = to_core(edges)
    share = ((3 * wide + 12) * 2 * blocks, LANES)
    shares = vmem_call(
        functools.partial(shares_kernel, wide),
        [share] * (gz - 1),
        [vel, tot, weight, edges],
        flops=2 * 10**10,
        name="shares",
    )
    pieces = [
        lax.ppermute(x, "gz", [(i, (i + shift) % gz) for i in range(gz)]) for shift, x in enumerate(shares, 1)
    ]
    relays = vmem_call(
        functools.partial(relay_kernel, gz), [(24 * blocks, LANES)] * (gz // 2), [edges, beside_edges], name="relay"
    )
    ends = [lax.ppermute(x, ("gy", "gz"), end_pairs(gy, gz, step)) for step, x in enumerate(relays)]
    inv4, fixed = vmem_call(
        prepare_kernel,
        [(4, rows, lanes), ((MAPS + 16) * blocks + 16, LANES)],
        [inverse_ends, spike_ends, coef],
        flops=2 * 10**10,
        name="prepare",
    )
    first = (FIRST * blocks + 16, LANES)
    rhs, values, side, started = vmem_call(
        functools.partial(own_kernel, wide, firsts),
        [(3, rows, lanes), (12, lanes), (12, lanes), first],
        [vel, tot, weight, edges, inv4, fixed],
        scratch=[vmem(*share)],
        flops=2 * 10**8,
        name="own",
    )
    (message,) = vmem_call(
        functools.partial(interface_kernel, wide, firsts),
        [first],
        [inv4, started, values, side, *pieces],
        scratch=[vmem(12, lanes), vmem(12, lanes)],
        name="interface",
    )
    other = to_core(message)
    (end,) = vmem_call(ends_kernel, [(24 * blocks, LANES)], ends, flops=2 * 10**10, name="ends")
    other_end = to_core(end)
    run = (RUN * blocks, LANES)
    composed, mine, theirs = vmem_call(pair_kernel, [run] * 3, [message, other, end, other_end], name="pair")

    inside, held = vmem_call(
        fetch_kernel,
        [(rows, rows, modes), (2, 2, rows, modes)],
        [inverse, spikes, composed],
        scratch=[dma(2)],
        flops=2 * 10**10,
        name="fetch",
        far=2,
    )
    steps = groups_of(gy)
    base, size = steps[0]
    (known,) = vmem_call(
        functools.partial(widen_kernel, base, True),
        [run],
        [mine, theirs],
        scratch=[vmem(size, *run)],
        flops=10**7,
        name="widen",
    )
    (local,) = vmem_call(
        functools.partial(block_kernel, wide, firsts),
        [(3, rows, lanes)],
        [inside, rhs, message, other, end, *pieces],
        scratch=[vmem(3, rows, lanes), vmem(3, rows, LANES)],
        flops=2 * 10**8,
        name="block",
    )
    for base, size in steps[1:-1]:
        gathered = [composed]
        for x in range(size - 1, 0, -1):
            gathered.append(lax.ppermute(composed, "gy", [(i, i ^ (x * base) ^ 1) for i in range(gy)]))
        board = [vmem(size, *run)]
        (composed,) = vmem_call(
            functools.partial(compose_kernel, base), [run], gathered, scratch=board, name="compose"
        )
        (known,) = vmem_call(
            functools.partial(widen_kernel, base, False),
            [run],
            [*gathered, known],
            scratch=board,
            flops=10**7,
            name="widen",
        )
    base, _ = steps[-1]
    (message,) = vmem_call(
        functools.partial(last_message_kernel, base), [(LAST * blocks, LANES)], [composed], name="last_message"
    )
    received = lax.ppermute(message, "gy", [(i, i ^ base ^ 1) for i in range(gy)])
    ready, lift = vmem_call(
        functools.partial(ready_kernel, base),
        [(3, rows, lanes), (2, rows, lanes)],
        [local, held, known],
        flops=10**7,
        name="ready",
    )
    (out,) = vmem_call(
        functools.partial(final_kernel, base),
        [(3, rows, lanes)],
        [ready, lift, composed, received],
        scratch=[vmem(3, rows, lanes), dma(3)],
        name="final",
        far_out=True,
    )
    return out


def solution(mesh):
    placed = (
        P(None, ("gy", "gz"), None),
        P(None, ("gy", "gz"), None),
        P(None, None, "gy"),
        P("gy", None, "gz"),
        P(None, None, "gy", "gz"),
    )
    return jax.shard_map(
        per_device, mesh=mesh, in_specs=placed, out_specs=P(None, "gy", "gz"), check_vma=False
    )
```

```python
import functools

import jax
import jax.numpy as jnp
from jax import lax
from jax.experimental import pallas as pl
from jax.experimental.pallas import tpu as pltpu
from jax.sharding import PartitionSpec as P

F32 = jnp.float32
LANES = 128
HALO = 2


def vmem_call(body, out_shapes, args, scratch=(), flops=0, name=None, far=0, far_out=False):
    near, away = pl.BlockSpec(memory_space=pltpu.VMEM), pl.BlockSpec(memory_space=pltpu.HBM)
    nbytes = sum(a.size * 4 for a in args)
    args = [pltpu.with_memory_space_constraint(a, pltpu.HBM) for a in args[:far]] + args[far:]
    return pl.pallas_call(
        body,
        out_shape=[jax.ShapeDtypeStruct(s, F32) for s in out_shapes],
        in_specs=[away] * far + [near] * (len(args) - far),
        out_specs=[away if far_out else near] * len(out_shapes),
        scratch_shapes=list(scratch),
        compiler_params=pltpu.CompilerParams(vmem_limit_bytes=16 * 2**20),
        cost_estimate=pl.CostEstimate(flops=flops, bytes_accessed=nbytes, transcendentals=0),
        name=name,
    )(*args)


def window(rows, own, groups):
    spans = [(max(g * own - HALO, 0), min(g * own + own + HALO, rows)) for g in range(groups)]
    wide = max(high - low for low, high in spans)
    return wide, [min(low, rows - wide) for low, _ in spans]


def lane_of(x):
    return lax.broadcasted_iota(jnp.int32, (x.shape[0], LANES), 1)


def take(x, lanes):
    return jnp.take_along_axis(x, lanes, axis=1, mode="promise_in_bounds")


def apart(x):
    lane = lane_of(x)
    low = lane < LANES // 2
    even = jnp.where(low, 2 * lane, 2 * lane - (LANES - 1))
    odd = jnp.where(low, 2 * lane + 1, 2 * lane - LANES)
    a, b = x[:, :LANES], x[:, LANES:]
    return jnp.where(low, take(a, even), take(b, odd)), jnp.where(low, take(a, odd), take(b, even))


def together(real, imaginary):
    lane = lane_of(real)
    half, odd = lax.shift_right_logical(lane, 1), jnp.bitwise_and(lane, 1) == 1
    parts = [
        jnp.where(odd, take(imaginary, half + at), take(real, half + at)) for at in (0, LANES // 2)
    ]
    return jnp.concatenate(parts, axis=1)


def doubled(x):
    half = lax.shift_right_logical(lane_of(x), 1)
    return jnp.concatenate([take(x, half), take(x, half + LANES // 2)], axis=1)


STATE = 24
MAPS = 12
RUN = STATE + MAPS
FIRST = STATE + 24 + MAPS + 16
LAST = 16


def side_weights(coef, upper):
    rows = coef.shape[1]
    if upper:
        taps = [[(4, rows - 2), None], [(3, rows - 1), (4, rows - 1)]]
    else:
        taps = [[(0, 0), (1, 0)], [None, (0, 1)]]
    none = jnp.zeros((1, LANES), F32)
    get = lambda tap, kind: none if tap is None else coef[2 * tap[0] + kind, tap[1] : tap[1] + 1]
    return [[[get(tap, kind) for kind in range(2)] for tap in row] for row in taps]


def beside(weights, planes):
    return [
        sum(weights[i][j][kind] * planes(kind, j) for j in range(2) for kind in range(2)) for i in range(2)
    ]


def load_kernel(wide, firsts, velocity, explicit, bands, *refs):
    edges, coef, weight, vel, tot, here, there, taps, square, sems = refs
    groups = len(firsts)
    own = velocity.shape[1]
    rows = coef.shape[1]
    g = lax.axis_index("gz")
    moves = [(bands, taps), (velocity, here), (explicit, there)]
    copies = [pltpu.make_async_copy(source, target, sems.at[i]) for i, (source, target) in enumerate(moves)]
    for copy in copies:
        copy.start()
    square[...] = jnp.zeros_like(square)
    vel[...] = jnp.zeros_like(vel)
    tot[...] = jnp.zeros_like(tot)
    copies[0].wait()
    for d in range(5):
        square[2 * d : 2 * d + 2, 0:rows] = taps[d]
    turned = jnp.transpose(square[...])
    for i in range(10):
        coef[i] = jnp.broadcast_to(turned[0:rows, i : i + 1], (rows, LANES))
    for k in range(groups):

        @pl.when(g == k)
        def _(first=firsts[k]):
            for i in range(10):
                weight[i] = coef[i, first : first + wide]

    copies[1].wait()
    copies[2].wait()
    for k in range(groups):

        @pl.when(g == k)
        def _(base=8 + k * own - firsts[k]):
            for f in range(3):
                vel[f, base : base + own] = here[f]
                tot[f, base : base + own] = here[f] + there[f]

    for f in range(3):
        for j in range(HALO):
            top, bottom = here[f, j : j + 1], here[f, own - HALO + j : own - HALO + j + 1]
            edges[6 + 3 * j + f : 7 + 3 * j + f] = jnp.where(g == 0, top, bottom)
            top += there[f, j : j + 1]
            bottom += there[f, own - HALO + j : own - HALO + j + 1]
            edges[3 * j + f : 3 * j + f + 1] = jnp.where(g == 0, top, bottom)


def stencil(vel, tot, weights, f, wide, at):
    total = None
    for d in range(5):
        low = pl.ds(8 + d - 2, wide)
        term = weights[2 * d] * tot[f, low, at] + weights[2 * d + 1] * vel[f, low, at]
        total = term if total is None else total + term
    return total


def store_share(out, wide, tile, at, vel, tot, weights, edges):
    base = (3 * wide + 12) * tile
    for f in range(3):
        total = None
        for d in range(5):
            low = pl.ds(8 + d - 2, wide)
            term = weights[2 * d] * tot[f, low, at] + weights[2 * d + 1] * vel[f, low, at]
            total = term if total is None else total + term
        out[base + wide * f : base + wide * (f + 1)] = total
    out[base + 3 * wide : base + 3 * wide + 12] = edges[:, at]


def shares_kernel(wide, vel, tot, weight, edges, *outs):
    groups = len(outs) + 1
    part = vel.shape[2] // groups
    g = lax.axis_index("gz")
    weights = [weight[i] for i in range(10)]
    for shift, out in enumerate(outs, 1):
        begin = lax.rem(g + shift, groups) * part
        for tile in range(part // LANES):
            at = pl.ds(pl.multiple_of(begin + LANES * tile, LANES), LANES)
            store_share(out, wide, tile, at, vel, tot, weights, edges)


def add_share(rhs, wide, firsts, source, piece):
    for k, first in enumerate(firsts):

        @pl.when(source == k)
        def _(first=first):
            for tile in range(rhs.shape[2] // LANES):
                for f in range(3):
                    row = (3 * wide + 12) * tile + wide * f
                    rhs[f, first : first + wide, LANES * tile : LANES * (tile + 1)] += piece[row : row + wide]


def own_kernel(wide, firsts, vel, tot, weight, edges, inv4, fixed, rhs, values, side, started, share):
    lanes = rhs.shape[2]
    blocks = lanes // (2 * LANES)
    g = lax.axis_index("gz")
    weights = [weight[i] for i in range(10)]
    for tile in range(lanes // LANES):
        at = pl.ds(pl.multiple_of(g * lanes + LANES * tile, LANES), LANES)
        store_share(share, wide, tile, at, vel, tot, weights, edges)
        row = (3 * wide + 12) * tile + 3 * wide
        side[:, LANES * tile : LANES * (tile + 1)] = share[row : row + 12]
    rhs[...] = jnp.zeros_like(rhs)
    add_share(rhs, wide, firsts, g, share)
    for f in range(3):
        for r in range(4):
            row = (6 if r < 2 else 0) + 3 * (r % 2) + f
            values[row : row + 1] = jnp.sum(inv4[r] * rhs[f], axis=0, keepdims=True)
    started[...] = jnp.zeros_like(started)
    for b in range(blocks):
        at = FIRST * b
        started[at + STATE + 24 : at + FIRST] = fixed[(MAPS + 16) * b : (MAPS + 16) * (b + 1)]
    started[FIRST * blocks : FIRST * blocks + 16] = fixed[(MAPS + 16) * blocks : (MAPS + 16) * blocks + 16]


def store_planes(ref, at, planes):
    real, imaginary = apart(planes)
    for i in range(planes.shape[0] // 3):
        ref[at + 6 * i : at + 6 * i + 3] = real[3 * i : 3 * i + 3]
        ref[at + 6 * i + 3 : at + 6 * i + 6] = imaginary[3 * i : 3 * i + 3]


def planes_of(ref, at):
    return lambda kind, j: ref[at + 12 * kind + 6 * j : at + 12 * kind + 6 * j + 6]


def relay_kernel(groups, edges, beside_edges, *outs):
    core = lax.rem(lax.axis_index("gy"), 2)
    mine = jnp.where(lax.axis_index("gz") == 0, core == 0, core == 1)
    part = edges.shape[1] // groups
    for step, out in enumerate(outs):
        begin = (2 * step + 1 - core) * part
        for b in range(part // (2 * LANES)):
            at = pl.ds(pl.multiple_of(begin + 2 * LANES * b, 2 * LANES), 2 * LANES)
            store_planes(out, 24 * b, jnp.where(mine, edges[:, at], beside_edges[:, at]))


def prepare_kernel(inverse, spikes, coef, inv4, fixed, inverse_ends, spike_ends, sems):
    rows, modes = inverse_ends.shape[1:]
    copies = []
    for i, (low, tiles) in enumerate(((0, 0), (rows - 2, rows - 8))):
        source, target = inverse.at[pl.ds(low, 2)], inverse_ends.at[pl.ds(2 * i, 2)]
        copies.append(pltpu.make_async_copy(source, target, sems.at[2 * i]))
        source, target = spikes.at[:, :, pl.ds(tiles, 8)], spike_ends.at[:, :, pl.ds(8 * i, 8)]
        copies.append(pltpu.make_async_copy(source, target, sems.at[2 * i + 1]))
    for copy in copies:
        copy.start()
    core = lax.rem(lax.axis_index("gy"), 2)
    gy, count = lax.axis_index("gy"), lax.axis_size("gy")
    lower, upper = side_weights(coef, False), side_weights(coef, True)
    used = jnp.where(core == 0, gy > 0, gy < count - 1)
    weights = (MAPS + 16) * (modes // LANES)
    for i in range(2):
        for j in range(2):
            for kind in range(2):
                at = weights + 4 * i + 2 * j + kind
                low, high = lower[i][j][kind], upper[i][j][kind]
                fixed[at : at + 1] = jnp.where(core == 0, high, low)
                fixed[at + 8 : at + 9] = jnp.where(used, jnp.where(core == 0, low, high), 0.0)
    for copy in copies:
        copy.wait()
    for b in range(modes // LANES):
        at, lanes = (MAPS + 16) * b, pl.ds(LANES * b, LANES)
        for k in range(2):
            for j in range(2):
                row = at + 2 * k + j
                fixed[row : row + 1] = -spike_ends[0, j, 14 + k : 15 + k, lanes]
                fixed[row + 4 : row + 5] = -spike_ends[0, j, k : k + 1, lanes]
                fixed[row + 8 : row + 9] = -spike_ends[1, j, k : k + 1, lanes]
        for r in range(4):
            inv4[r, :, 2 * LANES * b : 2 * LANES * (b + 1)] = doubled(inverse_ends[r, :, lanes])
            for i in range(2):
                low, high = inverse_ends[r, i : i + 1, lanes], inverse_ends[r, rows - 2 + i : rows - 1 + i, lanes]
                to = at + MAPS + 2 * ((r + 2) % 4) + i
                fixed[to : to + 1] = jnp.where(core == 0, high, low)
                fixed[to + 8 : to + 9] = jnp.where(core == 0, low, high)


def fetch_kernel(inverse, spikes, after, inside, held, sems):
    copies = [pltpu.make_async_copy(inverse, inside, sems.at[0]), pltpu.make_async_copy(spikes, held, sems.at[1])]
    for copy in copies:
        copy.start()
    for copy in copies:
        copy.wait()


def weights_of(ref, at):
    at += ref.shape[0] - 16
    return [
        [[ref[at + 4 * i + 2 * j + kind : at + 4 * i + 2 * j + kind + 1] for kind in range(2)] for j in range(2)]
        for i in range(2)
    ]


def interface_kernel(wide, firsts, inv4, started, own_values, own_side, *refs):
    groups = len(firsts)
    *pieces, message, values, side = refs
    tiles = values.shape[1] // LANES
    g = lax.axis_index("gz")
    core = lax.rem(lax.axis_index("gy"), 2)
    message[...] = started[...]
    values[...] = own_values[...]
    side[...] = own_side[...]
    for shift, piece in enumerate(pieces, 1):
        source = lax.rem(g - shift + groups, groups)
        for k, first in enumerate(firsts):

            @pl.when(source == k)
            def _(piece=piece, first=first):
                for tile in range(tiles):
                    to = pl.ds(LANES * tile, LANES)
                    for f in range(3):
                        row = (3 * wide + 12) * tile + wide * f
                        share = piece[row : row + wide]
                        for r in range(4):
                            row = (6 if r < 2 else 0) + 3 * (r % 2) + f
                            values[row : row + 1, to] += jnp.sum(
                                inv4[r, first : first + wide, to] * share, axis=0, keepdims=True
                            )

        @pl.when(source == jnp.where(core == 0, groups - 1, 0))
        def _(piece=piece):
            for tile in range(tiles):
                row = (3 * wide + 12) * tile + 3 * wide
                side[:, LANES * tile : LANES * (tile + 1)] = piece[row : row + 12]

    for b in range(tiles // 2):
        store_planes(message, FIRST * b, values[:, 2 * LANES * b : 2 * LANES * (b + 1)])
        store_planes(message, FIRST * b + STATE, side[:, 2 * LANES * b : 2 * LANES * (b + 1)])


class Piece:
    def __init__(self, ref, at):
        self.p = [ref[at : at + 6], ref[at + 6 : at + 12]]
        self.q = [ref[at + 12 : at + 18], ref[at + 18 : at + 24]]
        self.F, self.H, self.G = (matrix_of(ref, at + STATE + 4 * i) for i in range(3))


def matrix_of(ref, at):
    return [[ref[at + 2 * k + j : at + 2 * k + j + 1] for j in range(2)] for k in range(2)]


def act(matrix, vector, plus=None):
    out = [matrix[k][0] * vector[0] + matrix[k][1] * vector[1] for k in range(2)]
    return out if plus is None else [plus[k] + out[k] for k in range(2)]


def times(a, b, plus=None):
    out = [[a[k][0] * b[0][j] + a[k][1] * b[1][j] for j in range(2)] for k in range(2)]
    return out if plus is None else [[plus[k][j] + out[k][j] for j in range(2)] for k in range(2)]


def after(state, piece):
    if state is None:
        return piece.p, piece.F
    return act(piece.F, state[0], piece.p), times(piece.F, state[1])


def before(piece, state):
    if state is None:
        return piece.q, piece.H, piece.G
    q, H, G = state
    q = act(piece.G, act(H, piece.p, q), piece.q)
    H = times(piece.G, times(H, piece.F), piece.H)
    return q, H, times(piece.G, G)


def choose(flag, new, old):
    return jax.tree.map(lambda a, b: jnp.where(flag, a, b), new, old)


def store_run(ref, at, p, q, F, H, G):
    for i, vector in enumerate((p, q)):
        for k in range(2):
            ref[at + 12 * i + 6 * k : at + 12 * i + 6 * k + 6] = vector[k]
    for i, matrix in enumerate((F, H, G)):
        for k in range(2):
            for j in range(2):
                row = at + STATE + 4 * i + 2 * k + j
                ref[row : row + 1] = matrix[k][j]


def sort_pieces(base, pieces, board):
    size = len(pieces)
    position = lax.rem(lax.div(lax.axis_index("gy"), base), size)
    for i, piece in enumerate(pieces):
        board[jnp.bitwise_xor(position, (size - i) % size)] = piece[...]
    return position


def compose_kernel(base, *refs):
    *pieces, out, last, board = refs
    sort_pieces(base, pieces, board)
    upper = lax.rem(lax.div(lax.axis_index("gy"), base * len(pieces)), 2) == 1
    for b in range(out.shape[0] // RUN):
        at, to = RUN * b, LAST * b
        run = [Piece(board.at[i], at) for i in range(len(pieces))]
        up = down = None
        for piece in run:
            up = after(up, piece)
        for piece in run[::-1]:
            down = before(piece, down)
        for k in range(2):
            last[to + 6 * k : to + 6 * k + 6] = jnp.where(upper, down[0][k], up[0][k])
            for j in range(2):
                last[to + 12 + 2 * k + j : to + 13 + 2 * k + j] = down[1][k][j]
        store_run(out, at, up[0], down[0], up[1], down[1], down[2])


def ends_kernel(*refs):
    *ends, out = refs
    step = lax.div(lax.axis_index("gz"), 2)
    end = ends[0][...]
    for i in range(1, len(ends)):
        end = jnp.where(step == i, ends[i][...], end)
    out[...] = end


def pair_kernel(mine, other, end_mine, end_other, out, fixed_mine, fixed_other):
    core = lax.rem(lax.axis_index("gy"), 2)
    blocks = out.shape[0] // RUN
    for ref, across, end, target in ((mine, other, end_mine, fixed_mine), (other, mine, end_other, fixed_other)):
        inner_weights, outer_weights = weights_of(ref, 0), weights_of(ref, 8)
        for b in range(blocks):
            at, to = FIRST * b, RUN * b
            inner = beside(inner_weights, planes_of(across, at + STATE))
            outer = beside(outer_weights, planes_of(end, 24 * b))
            target[to + STATE : to + RUN] = ref[at + 48 : at + 48 + MAPS]
            for k in range(4):
                value = ref[at + 6 * k : at + 6 * k + 6]
                for i in range(2):
                    row = at + 48 + MAPS + 2 * k + i
                    value = value + ref[row : row + 1] * inner[i] + ref[row + 8 : row + 9] * outer[i]
                target[to + 6 * k : to + 6 * k + 6] = value
    low = jnp.where(core == 0, fixed_mine[...], fixed_other[...])
    high = jnp.where(core == 0, fixed_other[...], fixed_mine[...])
    for at in range(0, out.shape[0], RUN):
        first, second = Piece(low, at), Piece(high, at)
        up, down = after(after(None, first), second), before(first, before(second, None))
        store_run(out, at, up[0], down[0], up[1], down[1], down[2])


def widen_kernel(base, start, *refs):
    *pieces, out, board = refs
    known_ref = None if start else pieces.pop()
    position = sort_pieces(base, pieces, board)
    for at in range(0, out.shape[0], RUN):
        run = [Piece(board.at[i], at) for i in range(len(pieces))]
        mine = Piece(pieces[0], at)
        one, none = jnp.ones_like(mine.F[0][0]), jnp.zeros_like(mine.F[0][0])
        zero = [jnp.zeros_like(mine.p[0])] * 2
        unit, blank = [[one, none], [none, one]], [[none, none], [none, none]]
        up, down = (zero, unit), (zero, blank, unit)
        for i, piece in enumerate(run[:-1]):
            up = choose(i < position, after(up, piece), up)
        for i in range(len(run) - 1, 0, -1):
            down = choose(i > position, before(run[i], down), down)
        (t, F), (q, H, G) = up, down
        e = act(H, act(mine.F, t, mine.p), q)
        E = times(H, times(mine.F, F))
        if start:
            store_run(out, at, t, e, F, E, G)
        else:
            known = Piece(known_ref, at)
            a, A, b, B, D = known.p, known.F, known.q, known.H, known.G
            store_run(
                out, at, act(A, t, a), act(D, e, act(B, t, b)), times(A, F), times(D, E, times(B, F)), times(D, G)
            )


def block_kernel(wide, firsts, inverse, own_rhs, mine, other, end, *refs):
    *pieces, local, rhs, split = refs
    fields, rows, lanes = rhs.shape
    g = lax.axis_index("gz")
    rhs[...] = own_rhs[...]
    for shift, piece in enumerate(pieces, 1):
        add_share(rhs, wide, firsts, lax.rem(g - shift + len(firsts), len(firsts)), piece)
    core = lax.rem(lax.axis_index("gy"), 2)
    inner_weights, outer_weights = weights_of(mine, 0), weights_of(mine, 8)
    flat = rhs[...].reshape(fields * rows, lanes)
    for b in range(lanes // (2 * LANES)):
        columns = pl.ds(2 * LANES * b, 2 * LANES)
        parts = apart(flat[:, 2 * LANES * b : 2 * LANES * (b + 1)])
        inner = beside(inner_weights, planes_of(other, FIRST * b + STATE))
        outer = beside(outer_weights, planes_of(end, 24 * b))
        solved = []
        for p in range(2):
            split[...] = parts[p].reshape(fields, rows, LANES)
            for f in range(fields):
                for i in range(2):
                    one, two = inner[i][3 * p + f : 3 * p + f + 1], outer[i][3 * p + f : 3 * p + f + 1]
                    split[f, i : i + 1] += jnp.where(core == 0, two, one)
                    split[f, rows - 2 + i : rows - 1 + i] += jnp.where(core == 0, one, two)
            factors = inverse[:, :, LANES * b : LANES * (b + 1)]
            solved.append([jnp.sum(factors * split[f][None], axis=1) for f in range(fields)])
        for f in range(fields):
            local[f, :, columns] = together(solved[0][f], solved[1][f])


def ready_kernel(base, local, spikes, known, ready, lift):
    upper = lax.rem(lax.div(lax.axis_index("gy"), base), 2) == 1
    for b in range(known.shape[0] // RUN):
        columns = pl.ds(2 * LANES * b, 2 * LANES)
        factors = [[doubled(spikes[i, k, :, LANES * b : LANES * (b + 1)]) for k in range(2)] for i in range(2)]
        run = Piece(known, RUN * b)
        maps = doubled(known[RUN * b + STATE : RUN * (b + 1)])
        A, B, D = (matrix_of(maps, 4 * i) for i in range(3))
        t, s = ([together(v[k][0:3], v[k][3:6]) for k in range(2)] for v in (run.p, run.q))
        for f in range(3):
            value = local[f, :, columns]
            for k in range(2):
                value = value - factors[0][k] * t[k][f : f + 1] - factors[1][k] * s[k][f : f + 1]
            ready[f, :, columns] = value
        for j in range(2):
            value = jnp.zeros_like(factors[0][0])
            for k in range(2):
                through_t = factors[0][k] * A[k][j] + factors[1][k] * B[k][j]
                value = value - jnp.where(upper, through_t, factors[1][k] * D[k][j])
            lift[j, :, columns] = value


def final_kernel(base, ready, lift, composed, received, out, held, sems):
    upper = lax.rem(lax.div(lax.axis_index("gy"), base), 2) == 1
    states = []
    for b in range(composed.shape[0] // RUN):
        at, to = RUN * b, LAST * b
        mine = [composed[at : at + 6], composed[at + 6 : at + 12]]
        theirs = [received[to : to + 6], received[to + 6 : to + 12]]
        state = choose(upper, theirs, act(matrix_of(received, to + 12), mine, theirs))
        states.append([together(v[0:3], v[3:6]) for v in state])
    copies = []
    for f in range(3):
        for b, state in enumerate(states):
            columns = pl.ds(2 * LANES * b, 2 * LANES)
            value = ready[f, :, columns]
            for j in range(2):
                value = value + lift[j, :, columns] * state[j][f : f + 1]
            held[f, :, columns] = value
        copies.append(pltpu.make_async_copy(held.at[f], out.at[f], sems.at[f]))
        copies[-1].start()
    for copy in copies:
        copy.wait()


def end_pairs(gy, gz, step):
    at = lambda y, z: y * gz + z
    pairs = []
    for y in range(1, gy - 1, 2):
        for core in range(2):
            column = 2 * step + 1 - core
            pairs.append((at(y - 1 + core, gz - 1), at(y + 1, column)))
            pairs.append((at(y + 1 + core, 0), at(y, column)))
    sources = sorted(set(range(gy * gz)) - {s for s, _ in pairs})
    targets = sorted(set(range(gy * gz)) - {t for _, t in pairs})
    if gz == 2:
        for i in range(0, len(sources), 2):
            (a, b), (c, d) = sources[i : i + 2], targets[i : i + 2]
            pairs += [(a, d), (b, c)] if a != d and b != c else [(a, c), (b, d)]
    return pairs


def groups_of(count):
    steps, base = [(1, 2)], 2
    while 2 * base < count:
        size = 4 if base * 8 <= count else 2
        steps.append((base, size))
        base *= size
    return steps + [(base, 2)]


def per_device(velocity, explicit, bands, inverse, spikes):
    gy, gz = lax.axis_size("gy"), lax.axis_size("gz")
    own, columns = velocity.shape[1:]
    rows, modes = inverse.shape[0], inverse.shape[2]
    lanes = 2 * modes
    wide, firsts = window(rows, own, gz)
    vmem = lambda *shape: pltpu.VMEM(shape, F32)
    dma = lambda n: pltpu.SemaphoreType.DMA((n,))

    blocks = modes // LANES
    to_core = lambda x: lax.ppermute(x, "gy", [(i, i ^ 1) for i in range(gy)])
    padded = (3, rows + 16, columns)
    edges, coef, weight, vel, tot = vmem_call(
        functools.partial(load_kernel, wide, firsts),
        [(12, columns), (10, rows, LANES), (10, wide, LANES), padded, padded],
        [velocity, explicit, jnp.transpose(bands, (1, 0, 2))],
        scratch=[vmem(3, own, columns)] * 2 + [vmem(5, 2, rows), vmem(LANES, LANES), dma(3)],
        flops=2 * 10**10,
        name="load",
        far=3,
    )
    beside_edges = to_core(edges)
    share = ((3 * wide + 12) * 2 * blocks, LANES)
    shares = vmem_call(
        functools.partial(shares_kernel, wide),
        [share] * (gz - 1),
        [vel, tot, weight, edges],
        flops=2 * 10**10,
        name="shares",
    )
    pieces = [
        lax.ppermute(x, "gz", [(i, (i + shift) % gz) for i in range(gz)]) for shift, x in enumerate(shares, 1)
    ]
    relays = vmem_call(
        functools.partial(relay_kernel, gz), [(24 * blocks, LANES)] * (gz // 2), [edges, beside_edges], name="relay"
    )
    ends = [lax.ppermute(x, ("gy", "gz"), end_pairs(gy, gz, step)) for step, x in enumerate(relays)]
    inv4, fixed = vmem_call(
        prepare_kernel,
        [(4, rows, lanes), ((MAPS + 16) * blocks + 16, LANES)],
        [inverse, spikes, coef],
        scratch=[vmem(4, rows, modes), vmem(2, 2, 16, modes), dma(4)],
        flops=2 * 10**10,
        name="prepare",
        far=2,
    )
    first = (FIRST * blocks + 16, LANES)
    rhs, values, side, started = vmem_call(
        functools.partial(own_kernel, wide, firsts),
        [(3, rows, lanes), (12, lanes), (12, lanes), first],
        [vel, tot, weight, edges, inv4, fixed],
        scratch=[vmem(*share)],
        flops=2 * 10**8,
        name="own",
    )
    (message,) = vmem_call(
        functools.partial(interface_kernel, wide, firsts),
        [first],
        [inv4, started, values, side, *pieces],
        scratch=[vmem(12, lanes), vmem(12, lanes)],
        name="interface",
    )
    other = to_core(message)
    (end,) = vmem_call(ends_kernel, [(24 * blocks, LANES)], ends, flops=2 * 10**10, name="ends")
    other_end = to_core(end)
    run = (RUN * blocks, LANES)
    composed, mine, theirs = vmem_call(pair_kernel, [run] * 3, [message, other, end, other_end], name="pair")

    inside, held = vmem_call(
        fetch_kernel,
        [(rows, rows, modes), (2, 2, rows, modes)],
        [inverse, spikes, composed],
        scratch=[dma(2)],
        flops=2 * 10**10,
        name="fetch",
        far=2,
    )
    steps = groups_of(gy)
    base, size = steps[0]
    (known,) = vmem_call(
        functools.partial(widen_kernel, base, True),
        [run],
        [mine, theirs],
        scratch=[vmem(size, *run)],
        flops=10**7,
        name="widen",
    )
    (local,) = vmem_call(
        functools.partial(block_kernel, wide, firsts),
        [(3, rows, lanes)],
        [inside, rhs, message, other, end, *pieces],
        scratch=[vmem(3, rows, lanes), vmem(3, rows, LANES)],
        flops=2 * 10**8,
        name="block",
    )
    for base, size in steps[1:-1]:
        gathered = [composed]
        for x in range(size - 1, 0, -1):
            gathered.append(lax.ppermute(composed, "gy", [(i, i ^ (x * base) ^ 1) for i in range(gy)]))
        board = [vmem(size, *run)]
        composed, last = vmem_call(
            functools.partial(compose_kernel, base),
            [run, (LAST * blocks, LANES)],
            gathered,
            scratch=board,
            name="compose",
        )
        (known,) = vmem_call(
            functools.partial(widen_kernel, base, False),
            [run],
            [*gathered, known],
            scratch=board,
            flops=10**7,
            name="widen",
        )
    base, _ = steps[-1]
    received = lax.ppermute(last, "gy", [(i, i ^ base ^ 1) for i in range(gy)])
    ready, lift = vmem_call(
        functools.partial(ready_kernel, base),
        [(3, rows, lanes), (2, rows, lanes)],
        [local, held, known],
        flops=10**7,
        name="ready",
    )
    (out,) = vmem_call(
        functools.partial(final_kernel, base),
        [(3, rows, lanes)],
        [ready, lift, composed, received],
        scratch=[vmem(3, rows, lanes), dma(3)],
        name="final",
        far_out=True,
    )
    return out


def solution(mesh):
    placed = (
        P(None, ("gy", "gz"), None),
        P(None, ("gy", "gz"), None),
        P(None, None, "gy"),
        P("gy", None, "gz"),
        P(None, None, "gy", "gz"),
    )
    return jax.shard_map(
        per_device, mesh=mesh, in_specs=placed, out_specs=P(None, "gy", "gz"), check_vma=False
    )
```

```python
import functools

import jax
import jax.numpy as jnp
from jax import lax
from jax.experimental import pallas as pl
from jax.experimental.pallas import tpu as pltpu
from jax.sharding import PartitionSpec as P

F32 = jnp.float32
LANES = 128
HALO = 2


def vmem_call(body, out_shapes, args, scratch=(), flops=0, name=None, far=0, far_out=False):
    near, away = pl.BlockSpec(memory_space=pltpu.VMEM), pl.BlockSpec(memory_space=pltpu.HBM)
    nbytes = sum(a.size * 4 for a in args)
    args = [pltpu.with_memory_space_constraint(a, pltpu.HBM) for a in args[:far]] + args[far:]
    return pl.pallas_call(
        body,
        out_shape=[jax.ShapeDtypeStruct(s, F32) for s in out_shapes],
        in_specs=[away] * far + [near] * (len(args) - far),
        out_specs=[away if far_out else near] * len(out_shapes),
        scratch_shapes=list(scratch),
        compiler_params=pltpu.CompilerParams(vmem_limit_bytes=16 * 2**20),
        cost_estimate=pl.CostEstimate(flops=flops, bytes_accessed=nbytes, transcendentals=0),
        name=name,
    )(*args)


def window(rows, own, groups):
    spans = [(max(g * own - HALO, 0), min(g * own + own + HALO, rows)) for g in range(groups)]
    wide = max(high - low for low, high in spans)
    return wide, [min(low, rows - wide) for low, _ in spans]


def lane_of(x):
    return lax.broadcasted_iota(jnp.int32, (x.shape[0], LANES), 1)


def take(x, lanes):
    return jnp.take_along_axis(x, lanes, axis=1, mode="promise_in_bounds")


def apart(x):
    lane = lane_of(x)
    low = lane < LANES // 2
    even = jnp.where(low, 2 * lane, 2 * lane - (LANES - 1))
    odd = jnp.where(low, 2 * lane + 1, 2 * lane - LANES)
    a, b = x[:, :LANES], x[:, LANES:]
    return jnp.where(low, take(a, even), take(b, odd)), jnp.where(low, take(a, odd), take(b, even))


def together(real, imaginary):
    lane = lane_of(real)
    half, odd = lax.shift_right_logical(lane, 1), jnp.bitwise_and(lane, 1) == 1
    parts = [
        jnp.where(odd, take(imaginary, half + at), take(real, half + at)) for at in (0, LANES // 2)
    ]
    return jnp.concatenate(parts, axis=1)


def doubled(x):
    half = lax.shift_right_logical(lane_of(x), 1)
    return jnp.concatenate([take(x, half), take(x, half + LANES // 2)], axis=1)


STATE = 24
MAPS = 12
RUN = STATE + MAPS
FIRST = STATE + 24 + MAPS + 16
LAST = 16


def side_weights(coef, upper):
    rows = coef.shape[1]
    if upper:
        taps = [[(4, rows - 2), None], [(3, rows - 1), (4, rows - 1)]]
    else:
        taps = [[(0, 0), (1, 0)], [None, (0, 1)]]
    none = jnp.zeros((1, LANES), F32)
    get = lambda tap, kind: none if tap is None else coef[2 * tap[0] + kind, tap[1] : tap[1] + 1]
    return [[[get(tap, kind) for kind in range(2)] for tap in row] for row in taps]


def beside(weights, planes):
    return [
        sum(weights[i][j][kind] * planes(kind, j) for j in range(2) for kind in range(2)) for i in range(2)
    ]


def load_kernel(wide, firsts, velocity, explicit, bands, *refs):
    edges, coef, weight, vel, tot, here, there, taps, square, sems = refs
    groups = len(firsts)
    own = velocity.shape[1]
    rows = coef.shape[1]
    g = lax.axis_index("gz")
    moves = [(bands, taps), (velocity, here), (explicit, there)]
    copies = [pltpu.make_async_copy(source, target, sems.at[i]) for i, (source, target) in enumerate(moves)]
    for copy in copies:
        copy.start()
    square[...] = jnp.zeros_like(square)
    vel[...] = jnp.zeros_like(vel)
    tot[...] = jnp.zeros_like(tot)
    copies[0].wait()
    for d in range(5):
        square[2 * d : 2 * d + 2, 0:rows] = taps[d]
    turned = jnp.transpose(square[...])
    for i in range(10):
        coef[i] = jnp.broadcast_to(turned[0:rows, i : i + 1], (rows, LANES))
    for k in range(groups):

        @pl.when(g == k)
        def _(first=firsts[k]):
            for i in range(10):
                weight[i] = coef[i, first : first + wide]

    copies[1].wait()
    copies[2].wait()
    for k in range(groups):

        @pl.when(g == k)
        def _(base=8 + k * own - firsts[k]):
            for f in range(3):
                vel[f, base : base + own] = here[f]
                tot[f, base : base + own] = here[f] + there[f]

    for f in range(3):
        for j in range(HALO):
            top, bottom = here[f, j : j + 1], here[f, own - HALO + j : own - HALO + j + 1]
            edges[6 + 3 * j + f : 7 + 3 * j + f] = jnp.where(g == 0, top, bottom)
            top += there[f, j : j + 1]
            bottom += there[f, own - HALO + j : own - HALO + j + 1]
            edges[3 * j + f : 3 * j + f + 1] = jnp.where(g == 0, top, bottom)


def stencil(vel, tot, weights, f, wide, at):
    total = None
    for d in range(5):
        low = pl.ds(8 + d - 2, wide)
        term = weights[2 * d] * tot[f, low, at] + weights[2 * d + 1] * vel[f, low, at]
        total = term if total is None else total + term
    return total


def store_share(out, wide, tile, at, vel, tot, weights, edges):
    base = (3 * wide + 12) * tile
    for f in range(3):
        total = None
        for d in range(5):
            low = pl.ds(8 + d - 2, wide)
            term = weights[2 * d] * tot[f, low, at] + weights[2 * d + 1] * vel[f, low, at]
            total = term if total is None else total + term
        out[base + wide * f : base + wide * (f + 1)] = total
    out[base + 3 * wide : base + 3 * wide + 12] = edges[:, at]


def shares_kernel(wide, vel, tot, weight, edges, *outs):
    groups = len(outs) + 1
    part = vel.shape[2] // groups
    g = lax.axis_index("gz")
    weights = [weight[i] for i in range(10)]
    for shift, out in enumerate(outs, 1):
        begin = lax.rem(g + shift, groups) * part
        for tile in range(part // LANES):
            at = pl.ds(pl.multiple_of(begin + LANES * tile, LANES), LANES)
            store_share(out, wide, tile, at, vel, tot, weights, edges)


def add_share(rhs, wide, firsts, source, piece):
    for k, first in enumerate(firsts):

        @pl.when(source == k)
        def _(first=first):
            for tile in range(rhs.shape[2] // LANES):
                for f in range(3):
                    row = (3 * wide + 12) * tile + wide * f
                    rhs[f, first : first + wide, LANES * tile : LANES * (tile + 1)] += piece[row : row + wide]


def own_kernel(wide, firsts, vel, tot, weight, edges, inv4, fixed, rhs, values, side, started, share):
    lanes = rhs.shape[2]
    blocks = lanes // (2 * LANES)
    g = lax.axis_index("gz")
    weights = [weight[i] for i in range(10)]
    for tile in range(lanes // LANES):
        at = pl.ds(pl.multiple_of(g * lanes + LANES * tile, LANES), LANES)
        store_share(share, wide, tile, at, vel, tot, weights, edges)
        row = (3 * wide + 12) * tile + 3 * wide
        side[:, LANES * tile : LANES * (tile + 1)] = share[row : row + 12]
    rhs[...] = jnp.zeros_like(rhs)
    add_share(rhs, wide, firsts, g, share)
    for f in range(3):
        for r in range(4):
            row = (6 if r < 2 else 0) + 3 * (r % 2) + f
            values[row : row + 1] = jnp.sum(inv4[r] * rhs[f], axis=0, keepdims=True)
    started[...] = jnp.zeros_like(started)
    for b in range(blocks):
        at = FIRST * b
        started[at + STATE + 24 : at + FIRST] = fixed[(MAPS + 16) * b : (MAPS + 16) * (b + 1)]
    started[FIRST * blocks : FIRST * blocks + 16] = fixed[(MAPS + 16) * blocks : (MAPS + 16) * blocks + 16]


def store_planes(ref, at, planes):
    real, imaginary = apart(planes)
    for i in range(planes.shape[0] // 3):
        ref[at + 6 * i : at + 6 * i + 3] = real[3 * i : 3 * i + 3]
        ref[at + 6 * i + 3 : at + 6 * i + 6] = imaginary[3 * i : 3 * i + 3]


def planes_of(ref, at):
    return lambda kind, j: ref[at + 12 * kind + 6 * j : at + 12 * kind + 6 * j + 6]


def relay_kernel(groups, edges, beside_edges, *outs):
    core = lax.rem(lax.axis_index("gy"), 2)
    head = lax.axis_index("gz") == 0
    mine = jnp.where(head, core == 0, core == 1)
    part = edges.shape[1] // groups
    for step, out in enumerate(outs):
        begin = (2 * step + jnp.where(head, core, 1 - core)) * part
        for b in range(part // (2 * LANES)):
            at = pl.ds(pl.multiple_of(begin + 2 * LANES * b, 2 * LANES), 2 * LANES)
            store_planes(out, 24 * b, jnp.where(mine, edges[:, at], beside_edges[:, at]))


def prepare_kernel(inverse, spikes, coef, inv4, fixed, inverse_ends, spike_ends, sems):
    rows, modes = inverse_ends.shape[1:]
    copies = []
    for i, (low, tiles) in enumerate(((0, 0), (rows - 2, rows - 8))):
        source, target = inverse.at[pl.ds(low, 2)], inverse_ends.at[pl.ds(2 * i, 2)]
        copies.append(pltpu.make_async_copy(source, target, sems.at[2 * i]))
        source, target = spikes.at[:, :, pl.ds(tiles, 8)], spike_ends.at[:, :, pl.ds(8 * i, 8)]
        copies.append(pltpu.make_async_copy(source, target, sems.at[2 * i + 1]))
    for copy in copies:
        copy.start()
    core = lax.rem(lax.axis_index("gy"), 2)
    gy, count = lax.axis_index("gy"), lax.axis_size("gy")
    lower, upper = side_weights(coef, False), side_weights(coef, True)
    used = jnp.where(core == 0, gy > 0, gy < count - 1)
    weights = (MAPS + 16) * (modes // LANES)
    for i in range(2):
        for j in range(2):
            for kind in range(2):
                at = weights + 4 * i + 2 * j + kind
                low, high = lower[i][j][kind], upper[i][j][kind]
                fixed[at : at + 1] = jnp.where(core == 0, high, low)
                fixed[at + 8 : at + 9] = jnp.where(used, jnp.where(core == 0, low, high), 0.0)
    for copy in copies:
        copy.wait()
    for b in range(modes // LANES):
        at, lanes = (MAPS + 16) * b, pl.ds(LANES * b, LANES)
        for k in range(2):
            for j in range(2):
                row = at + 2 * k + j
                fixed[row : row + 1] = -spike_ends[0, j, 14 + k : 15 + k, lanes]
                fixed[row + 4 : row + 5] = -spike_ends[0, j, k : k + 1, lanes]
                fixed[row + 8 : row + 9] = -spike_ends[1, j, k : k + 1, lanes]
        for r in range(4):
            inv4[r, :, 2 * LANES * b : 2 * LANES * (b + 1)] = doubled(inverse_ends[r, :, lanes])
            for i in range(2):
                low, high = inverse_ends[r, i : i + 1, lanes], inverse_ends[r, rows - 2 + i : rows - 1 + i, lanes]
                to = at + MAPS + 2 * ((r + 2) % 4) + i
                fixed[to : to + 1] = jnp.where(core == 0, high, low)
                fixed[to + 8 : to + 9] = jnp.where(core == 0, low, high)


def fetch_kernel(inverse, spikes, after, inside, held, sems):
    copies = [pltpu.make_async_copy(inverse, inside, sems.at[0]), pltpu.make_async_copy(spikes, held, sems.at[1])]
    for copy in copies:
        copy.start()
    for copy in copies:
        copy.wait()


def weights_of(ref, at):
    at += ref.shape[0] - 16
    return [
        [[ref[at + 4 * i + 2 * j + kind : at + 4 * i + 2 * j + kind + 1] for kind in range(2)] for j in range(2)]
        for i in range(2)
    ]


def interface_kernel(wide, firsts, inv4, started, own_values, own_side, *refs):
    groups = len(firsts)
    *pieces, message, values, side = refs
    tiles = values.shape[1] // LANES
    g = lax.axis_index("gz")
    core = lax.rem(lax.axis_index("gy"), 2)
    message[...] = started[...]
    values[...] = own_values[...]
    side[...] = own_side[...]
    for shift, piece in enumerate(pieces, 1):
        source = lax.rem(g - shift + groups, groups)
        for k, first in enumerate(firsts):

            @pl.when(source == k)
            def _(piece=piece, first=first):
                for tile in range(tiles):
                    to = pl.ds(LANES * tile, LANES)
                    for f in range(3):
                        row = (3 * wide + 12) * tile + wide * f
                        share = piece[row : row + wide]
                        for r in range(4):
                            row = (6 if r < 2 else 0) + 3 * (r % 2) + f
                            values[row : row + 1, to] += jnp.sum(
                                inv4[r, first : first + wide, to] * share, axis=0, keepdims=True
                            )

        @pl.when(source == jnp.where(core == 0, groups - 1, 0))
        def _(piece=piece):
            for tile in range(tiles):
                row = (3 * wide + 12) * tile + 3 * wide
                side[:, LANES * tile : LANES * (tile + 1)] = piece[row : row + 12]

    for b in range(tiles // 2):
        store_planes(message, FIRST * b, values[:, 2 * LANES * b : 2 * LANES * (b + 1)])
        store_planes(message, FIRST * b + STATE, side[:, 2 * LANES * b : 2 * LANES * (b + 1)])


class Piece:
    def __init__(self, ref, at):
        self.p = [ref[at : at + 6], ref[at + 6 : at + 12]]
        self.q = [ref[at + 12 : at + 18], ref[at + 18 : at + 24]]
        self.F, self.H, self.G = (matrix_of(ref, at + STATE + 4 * i) for i in range(3))


def matrix_of(ref, at):
    return [[ref[at + 2 * k + j : at + 2 * k + j + 1] for j in range(2)] for k in range(2)]


def act(matrix, vector, plus=None):
    out = [matrix[k][0] * vector[0] + matrix[k][1] * vector[1] for k in range(2)]
    return out if plus is None else [plus[k] + out[k] for k in range(2)]


def times(a, b, plus=None):
    out = [[a[k][0] * b[0][j] + a[k][1] * b[1][j] for j in range(2)] for k in range(2)]
    return out if plus is None else [[plus[k][j] + out[k][j] for j in range(2)] for k in range(2)]


def after(state, piece):
    if state is None:
        return piece.p, piece.F
    return act(piece.F, state[0], piece.p), times(piece.F, state[1])


def before(piece, state):
    if state is None:
        return piece.q, piece.H, piece.G
    q, H, G = state
    q = act(piece.G, act(H, piece.p, q), piece.q)
    H = times(piece.G, times(H, piece.F), piece.H)
    return q, H, times(piece.G, G)


def choose(flag, new, old):
    return jax.tree.map(lambda a, b: jnp.where(flag, a, b), new, old)


def store_run(ref, at, p, q, F, H, G):
    for i, vector in enumerate((p, q)):
        for k in range(2):
            ref[at + 12 * i + 6 * k : at + 12 * i + 6 * k + 6] = vector[k]
    for i, matrix in enumerate((F, H, G)):
        for k in range(2):
            for j in range(2):
                row = at + STATE + 4 * i + 2 * k + j
                ref[row : row + 1] = matrix[k][j]


def sort_pieces(base, pieces, board):
    size = len(pieces)
    position = lax.rem(lax.div(lax.axis_index("gy"), base), size)
    for i, piece in enumerate(pieces):
        board[jnp.bitwise_xor(position, (size - i) % size)] = piece[...]
    return position


def compose_kernel(base, *refs):
    *pieces, out, last, board = refs
    sort_pieces(base, pieces, board)
    upper = lax.rem(lax.div(lax.axis_index("gy"), base * len(pieces)), 2) == 1
    for b in range(out.shape[0] // RUN):
        at, to = RUN * b, LAST * b
        run = [Piece(board.at[i], at) for i in range(len(pieces))]
        up = down = None
        for piece in run:
            up = after(up, piece)
        for piece in run[::-1]:
            down = before(piece, down)
        for k in range(2):
            last[to + 6 * k : to + 6 * k + 6] = jnp.where(upper, down[0][k], up[0][k])
            for j in range(2):
                last[to + 12 + 2 * k + j : to + 13 + 2 * k + j] = down[1][k][j]
        store_run(out, at, up[0], down[0], up[1], down[1], down[2])


def ends_kernel(*refs):
    *ends, out = refs
    step = lax.div(lax.axis_index("gz"), 2)
    end = ends[0][...]
    for i in range(1, len(ends)):
        end = jnp.where(step == i, ends[i][...], end)
    out[...] = end


def outer_share(weights, here, end, far_end, b):
    near, far = planes_of(end, 24 * b), planes_of(far_end, 24 * b)
    return beside(weights, lambda kind, j: jnp.where(here, near(kind, j), far(kind, j)))


def pair_kernel(mine, other, end_mine, end_other, out, fixed_mine, fixed_other):
    core = lax.rem(lax.axis_index("gy"), 2)
    here = lax.rem(lax.axis_index("gz"), 2) == 0
    blocks = out.shape[0] // RUN
    for ref, across, end, far_end, target in (
        (mine, other, end_mine, end_other, fixed_mine),
        (other, mine, end_other, end_mine, fixed_other),
    ):
        inner_weights, outer_weights = weights_of(ref, 0), weights_of(ref, 8)
        for b in range(blocks):
            at, to = FIRST * b, RUN * b
            inner = beside(inner_weights, planes_of(across, at + STATE))
            outer = outer_share(outer_weights, here, end, far_end, b)
            target[to + STATE : to + RUN] = ref[at + 48 : at + 48 + MAPS]
            for k in range(4):
                value = ref[at + 6 * k : at + 6 * k + 6]
                for i in range(2):
                    row = at + 48 + MAPS + 2 * k + i
                    value = value + ref[row : row + 1] * inner[i] + ref[row + 8 : row + 9] * outer[i]
                target[to + 6 * k : to + 6 * k + 6] = value
    low = jnp.where(core == 0, fixed_mine[...], fixed_other[...])
    high = jnp.where(core == 0, fixed_other[...], fixed_mine[...])
    for at in range(0, out.shape[0], RUN):
        first, second = Piece(low, at), Piece(high, at)
        up, down = after(after(None, first), second), before(first, before(second, None))
        store_run(out, at, up[0], down[0], up[1], down[1], down[2])


def widen_kernel(base, start, *refs):
    *pieces, out, board = refs
    known_ref = None if start else pieces.pop()
    position = sort_pieces(base, pieces, board)
    for at in range(0, out.shape[0], RUN):
        run = [Piece(board.at[i], at) for i in range(len(pieces))]
        mine = Piece(pieces[0], at)
        one, none = jnp.ones_like(mine.F[0][0]), jnp.zeros_like(mine.F[0][0])
        zero = [jnp.zeros_like(mine.p[0])] * 2
        unit, blank = [[one, none], [none, one]], [[none, none], [none, none]]
        up, down = (zero, unit), (zero, blank, unit)
        for i, piece in enumerate(run[:-1]):
            up = choose(i < position, after(up, piece), up)
        for i in range(len(run) - 1, 0, -1):
            down = choose(i > position, before(run[i], down), down)
        (t, F), (q, H, G) = up, down
        e = act(H, act(mine.F, t, mine.p), q)
        E = times(H, times(mine.F, F))
        if start:
            store_run(out, at, t, e, F, E, G)
        else:
            known = Piece(known_ref, at)
            a, A, b, B, D = known.p, known.F, known.q, known.H, known.G
            store_run(
                out, at, act(A, t, a), act(D, e, act(B, t, b)), times(A, F), times(D, E, times(B, F)), times(D, G)
            )


def block_kernel(wide, firsts, inverse, own_rhs, mine, other, end, far_end, *refs):
    *pieces, local, rhs, split = refs
    fields, rows, lanes = rhs.shape
    g = lax.axis_index("gz")
    rhs[...] = own_rhs[...]
    for shift, piece in enumerate(pieces, 1):
        add_share(rhs, wide, firsts, lax.rem(g - shift + len(firsts), len(firsts)), piece)
    core = lax.rem(lax.axis_index("gy"), 2)
    inner_weights, outer_weights = weights_of(mine, 0), weights_of(mine, 8)
    flat = rhs[...].reshape(fields * rows, lanes)
    for b in range(lanes // (2 * LANES)):
        columns = pl.ds(2 * LANES * b, 2 * LANES)
        parts = apart(flat[:, 2 * LANES * b : 2 * LANES * (b + 1)])
        inner = beside(inner_weights, planes_of(other, FIRST * b + STATE))
        outer = outer_share(outer_weights, lax.rem(g, 2) == 0, end, far_end, b)
        solved = []
        for p in range(2):
            split[...] = parts[p].reshape(fields, rows, LANES)
            for f in range(fields):
                for i in range(2):
                    one, two = inner[i][3 * p + f : 3 * p + f + 1], outer[i][3 * p + f : 3 * p + f + 1]
                    split[f, i : i + 1] += jnp.where(core == 0, two, one)
                    split[f, rows - 2 + i : rows - 1 + i] += jnp.where(core == 0, one, two)
            factors = inverse[:, :, LANES * b : LANES * (b + 1)]
            solved.append([jnp.sum(factors * split[f][None], axis=1) for f in range(fields)])
        for f in range(fields):
            local[f, :, columns] = together(solved[0][f], solved[1][f])


def ready_kernel(base, local, spikes, known, ready, lift):
    upper = lax.rem(lax.div(lax.axis_index("gy"), base), 2) == 1
    for b in range(known.shape[0] // RUN):
        columns = pl.ds(2 * LANES * b, 2 * LANES)
        factors = [[doubled(spikes[i, k, :, LANES * b : LANES * (b + 1)]) for k in range(2)] for i in range(2)]
        run = Piece(known, RUN * b)
        maps = doubled(known[RUN * b + STATE : RUN * (b + 1)])
        A, B, D = (matrix_of(maps, 4 * i) for i in range(3))
        t, s = ([together(v[k][0:3], v[k][3:6]) for k in range(2)] for v in (run.p, run.q))
        for f in range(3):
            value = local[f, :, columns]
            for k in range(2):
                value = value - factors[0][k] * t[k][f : f + 1] - factors[1][k] * s[k][f : f + 1]
            ready[f, :, columns] = value
        for j in range(2):
            value = jnp.zeros_like(factors[0][0])
            for k in range(2):
                through_t = factors[0][k] * A[k][j] + factors[1][k] * B[k][j]
                value = value - jnp.where(upper, through_t, factors[1][k] * D[k][j])
            lift[j, :, columns] = value


def final_kernel(base, ready, lift, composed, received, out, held, sems):
    upper = lax.rem(lax.div(lax.axis_index("gy"), base), 2) == 1
    states = []
    for b in range(composed.shape[0] // RUN):
        at, to = RUN * b, LAST * b
        mine = [composed[at : at + 6], composed[at + 6 : at + 12]]
        theirs = [received[to : to + 6], received[to + 6 : to + 12]]
        state = choose(upper, theirs, act(matrix_of(received, to + 12), mine, theirs))
        states.append([together(v[0:3], v[3:6]) for v in state])
    copies = []
    for f in range(3):
        for b, state in enumerate(states):
            columns = pl.ds(2 * LANES * b, 2 * LANES)
            value = ready[f, :, columns]
            for j in range(2):
                value = value + lift[j, :, columns] * state[j][f : f + 1]
            held[f, :, columns] = value
        copies.append(pltpu.make_async_copy(held.at[f], out.at[f], sems.at[f]))
        copies[-1].start()
    for copy in copies:
        copy.wait()


def end_pairs(gy, gz, step):
    at = lambda y, z: y * gz + z
    pairs = []
    for y in range(gy - 2):
        core = y % 2
        pairs.append((at(y, gz - 1), at((y + 2) ^ 1, 2 * step + 1 - core)))
        pairs.append((at(y + 2, 0), at(y ^ 1, 2 * step + core)))
    sources = sorted(set(range(gy * gz)) - {s for s, _ in pairs})
    targets = sorted(set(range(gy * gz)) - {t for _, t in pairs})
    if gz == 2:
        for i in range(0, len(sources), 2):
            (a, b), (c, d) = sources[i : i + 2], targets[i : i + 2]
            pairs += [(a, d), (b, c)] if a != d and b != c else [(a, c), (b, d)]
    return pairs


def groups_of(count):
    steps, base = [(1, 2)], 2
    while 2 * base < count:
        size = 4 if base * 8 <= count else 2
        steps.append((base, size))
        base *= size
    return steps + [(base, 2)]


def per_device(velocity, explicit, bands, inverse, spikes):
    gy, gz = lax.axis_size("gy"), lax.axis_size("gz")
    own, columns = velocity.shape[1:]
    rows, modes = inverse.shape[0], inverse.shape[2]
    lanes = 2 * modes
    wide, firsts = window(rows, own, gz)
    vmem = lambda *shape: pltpu.VMEM(shape, F32)
    dma = lambda n: pltpu.SemaphoreType.DMA((n,))

    blocks = modes // LANES
    to_core = lambda x: lax.ppermute(x, "gy", [(i, i ^ 1) for i in range(gy)])
    padded = (3, rows + 16, columns)
    edges, coef, weight, vel, tot = vmem_call(
        functools.partial(load_kernel, wide, firsts),
        [(12, columns), (10, rows, LANES), (10, wide, LANES), padded, padded],
        [velocity, explicit, jnp.transpose(bands, (1, 0, 2))],
        scratch=[vmem(3, own, columns)] * 2 + [vmem(5, 2, rows), vmem(LANES, LANES), dma(3)],
        flops=2 * 10**10,
        name="load",
        far=3,
    )
    beside_edges = to_core(edges)
    share = ((3 * wide + 12) * 2 * blocks, LANES)
    shares = vmem_call(
        functools.partial(shares_kernel, wide),
        [share] * (gz - 1),
        [vel, tot, weight, edges],
        flops=2 * 10**10,
        name="shares",
    )
    pieces = [
        lax.ppermute(x, "gz", [(i, (i + shift) % gz) for i in range(gz)]) for shift, x in enumerate(shares, 1)
    ]
    relays = vmem_call(
        functools.partial(relay_kernel, gz), [(24 * blocks, LANES)] * (gz // 2), [edges, beside_edges], name="relay"
    )
    ends = [lax.ppermute(x, ("gy", "gz"), end_pairs(gy, gz, step)) for step, x in enumerate(relays)]
    inv4, fixed = vmem_call(
        prepare_kernel,
        [(4, rows, lanes), ((MAPS + 16) * blocks + 16, LANES)],
        [inverse, spikes, coef],
        scratch=[vmem(4, rows, modes), vmem(2, 2, 16, modes), dma(4)],
        flops=2 * 10**10,
        name="prepare",
        far=2,
    )
    first = (FIRST * blocks + 16, LANES)
    rhs, values, side, started = vmem_call(
        functools.partial(own_kernel, wide, firsts),
        [(3, rows, lanes), (12, lanes), (12, lanes), first],
        [vel, tot, weight, edges, inv4, fixed],
        scratch=[vmem(*share)],
        flops=2 * 10**8,
        name="own",
    )
    (message,) = vmem_call(
        functools.partial(interface_kernel, wide, firsts),
        [first],
        [inv4, started, values, side, *pieces],
        scratch=[vmem(12, lanes), vmem(12, lanes)],
        name="interface",
    )
    other = to_core(message)
    (end,) = vmem_call(ends_kernel, [(24 * blocks, LANES)], ends, flops=2 * 10**10, name="ends")
    other_end = to_core(end)
    run = (RUN * blocks, LANES)
    composed, mine, theirs = vmem_call(pair_kernel, [run] * 3, [message, other, end, other_end], name="pair")

    inside, held = vmem_call(
        fetch_kernel,
        [(rows, rows, modes), (2, 2, rows, modes)],
        [inverse, spikes, composed],
        scratch=[dma(2)],
        flops=2 * 10**10,
        name="fetch",
        far=2,
    )
    steps = groups_of(gy)
    base, size = steps[0]
    (known,) = vmem_call(
        functools.partial(widen_kernel, base, True),
        [run],
        [mine, theirs],
        scratch=[vmem(size, *run)],
        flops=10**7,
        name="widen",
    )
    (local,) = vmem_call(
        functools.partial(block_kernel, wide, firsts),
        [(3, rows, lanes)],
        [inside, rhs, message, other, end, other_end, *pieces],
        scratch=[vmem(3, rows, lanes), vmem(3, rows, LANES)],
        flops=2 * 10**8,
        name="block",
    )
    for base, size in steps[1:-1]:
        gathered = [composed]
        for x in range(size - 1, 0, -1):
            gathered.append(lax.ppermute(composed, "gy", [(i, i ^ (x * base) ^ 1) for i in range(gy)]))
        board = [vmem(size, *run)]
        composed, last = vmem_call(
            functools.partial(compose_kernel, base),
            [run, (LAST * blocks, LANES)],
            gathered,
            scratch=board,
            name="compose",
        )
        (known,) = vmem_call(
            functools.partial(widen_kernel, base, False),
            [run],
            [*gathered, known],
            scratch=board,
            flops=10**7,
            name="widen",
        )
    base, _ = steps[-1]
    received = lax.ppermute(last, "gy", [(i, i ^ base ^ 1) for i in range(gy)])
    ready, lift = vmem_call(
        functools.partial(ready_kernel, base),
        [(3, rows, lanes), (2, rows, lanes)],
        [local, held, known],
        flops=10**7,
        name="ready",
    )
    (out,) = vmem_call(
        functools.partial(final_kernel, base),
        [(3, rows, lanes)],
        [ready, lift, composed, received],
        scratch=[vmem(3, rows, lanes), dma(3)],
        name="final",
        far_out=True,
    )
    return out


def solution(mesh):
    placed = (
        P(None, ("gy", "gz"), None),
        P(None, ("gy", "gz"), None),
        P(None, None, "gy"),
        P("gy", None, "gz"),
        P(None, None, "gy", "gz"),
    )
    return jax.shard_map(
        per_device, mesh=mesh, in_specs=placed, out_specs=P(None, "gy", "gz"), check_vma=False
    )
```

```python
import functools

import jax
import jax.numpy as jnp
from jax import lax
from jax.experimental import pallas as pl
from jax.experimental.pallas import tpu as pltpu
from jax.sharding import PartitionSpec as P

F32 = jnp.float32
LANES = 128
HALO = 2


def vmem_call(body, out_shapes, args, scratch=(), flops=0, name=None, far=0, far_out=False):
    near, away = pl.BlockSpec(memory_space=pltpu.VMEM), pl.BlockSpec(memory_space=pltpu.HBM)
    nbytes = sum(a.size * 4 for a in args)
    args = [pltpu.with_memory_space_constraint(a, pltpu.HBM) for a in args[:far]] + args[far:]
    return pl.pallas_call(
        body,
        out_shape=[jax.ShapeDtypeStruct(s, F32) for s in out_shapes],
        in_specs=[away] * far + [near] * (len(args) - far),
        out_specs=[away if far_out else near] * len(out_shapes),
        scratch_shapes=list(scratch),
        compiler_params=pltpu.CompilerParams(vmem_limit_bytes=16 * 2**20),
        cost_estimate=pl.CostEstimate(flops=flops, bytes_accessed=nbytes, transcendentals=0),
        name=name,
    )(*args)


def window(rows, own, groups):
    spans = [(max(g * own - HALO, 0), min(g * own + own + HALO, rows)) for g in range(groups)]
    wide = max(high - low for low, high in spans)
    return wide, [min(low, rows - wide) for low, _ in spans]


def lane_of(x):
    return lax.broadcasted_iota(jnp.int32, (x.shape[0], LANES), 1)


def take(x, lanes):
    return jnp.take_along_axis(x, lanes, axis=1, mode="promise_in_bounds")


def apart(x):
    lane = lane_of(x)
    low = lane < LANES // 2
    even = jnp.where(low, 2 * lane, 2 * lane - (LANES - 1))
    odd = jnp.where(low, 2 * lane + 1, 2 * lane - LANES)
    a, b = x[:, :LANES], x[:, LANES:]
    return jnp.where(low, take(a, even), take(b, odd)), jnp.where(low, take(a, odd), take(b, even))


def together(real, imaginary):
    lane = lane_of(real)
    half, odd = lax.shift_right_logical(lane, 1), jnp.bitwise_and(lane, 1) == 1
    parts = [
        jnp.where(odd, take(imaginary, half + at), take(real, half + at)) for at in (0, LANES // 2)
    ]
    return jnp.concatenate(parts, axis=1)


def doubled(x):
    half = lax.shift_right_logical(lane_of(x), 1)
    return jnp.concatenate([take(x, half), take(x, half + LANES // 2)], axis=1)


STATE = 24
MAPS = 12
RUN = STATE + MAPS
FIRST = STATE + 24 + MAPS + 16
LAST = 16


def side_weights(coef, upper):
    rows = coef.shape[1]
    if upper:
        taps = [[(4, rows - 2), None], [(3, rows - 1), (4, rows - 1)]]
    else:
        taps = [[(0, 0), (1, 0)], [None, (0, 1)]]
    none = jnp.zeros((1, LANES), F32)
    get = lambda tap, kind: none if tap is None else coef[2 * tap[0] + kind, tap[1] : tap[1] + 1]
    return [[[get(tap, kind) for kind in range(2)] for tap in row] for row in taps]


def beside(weights, planes):
    return [
        sum(weights[i][j][kind] * planes(kind, j) for j in range(2) for kind in range(2)) for i in range(2)
    ]


def load_kernel(wide, firsts, velocity, explicit, bands, *refs):
    edges, relayed, coef, weight, vel, tot, here, there, taps, square, sems = refs
    groups = len(firsts)
    own = velocity.shape[1]
    rows = coef.shape[1]
    g = lax.axis_index("gz")
    moves = [(bands, taps), (velocity, here), (explicit, there)]
    copies = [pltpu.make_async_copy(source, target, sems.at[i]) for i, (source, target) in enumerate(moves)]
    for copy in copies:
        copy.start()
    square[...] = jnp.zeros_like(square)
    vel[...] = jnp.zeros_like(vel)
    tot[...] = jnp.zeros_like(tot)
    copies[0].wait()
    for d in range(5):
        square[2 * d : 2 * d + 2, 0:rows] = taps[d]
    turned = jnp.transpose(square[...])
    for i in range(10):
        coef[i] = jnp.broadcast_to(turned[0:rows, i : i + 1], (rows, LANES))
    for k in range(groups):

        @pl.when(g == k)
        def _(first=firsts[k]):
            for i in range(10):
                weight[i] = coef[i, first : first + wide]

    copies[1].wait()
    copies[2].wait()
    for k in range(groups):

        @pl.when(g == k)
        def _(base=8 + k * own - firsts[k]):
            for f in range(3):
                vel[f, base : base + own] = here[f]
                tot[f, base : base + own] = here[f] + there[f]

    for f in range(3):
        for j in range(HALO):
            top, bottom = here[f, j : j + 1], here[f, own - HALO + j : own - HALO + j + 1]
            edges[6 + 3 * j + f : 7 + 3 * j + f] = jnp.where(g == 0, top, bottom)
            top += there[f, j : j + 1]
            bottom += there[f, own - HALO + j : own - HALO + j + 1]
            edges[3 * j + f : 3 * j + f + 1] = jnp.where(g == 0, top, bottom)
    core = lax.rem(lax.axis_index("gy"), 2)
    part = edges.shape[1] // groups
    for step in range(groups // 2):
        begin = (2 * step + core) * part
        for tile in range(part // LANES):
            at = pl.ds(pl.multiple_of(begin + LANES * tile, LANES), LANES)
            row = 12 * (step * (part // LANES) + tile)
            relayed[row : row + 12] = edges[:, at]


def stencil(vel, tot, weights, f, wide, at):
    total = None
    for d in range(5):
        low = pl.ds(8 + d - 2, wide)
        term = weights[2 * d] * tot[f, low, at] + weights[2 * d + 1] * vel[f, low, at]
        total = term if total is None else total + term
    return total


def store_share(out, wide, tile, at, vel, tot, weights, edges):
    base = (3 * wide + 12) * tile
    for f in range(3):
        total = None
        for d in range(5):
            low = pl.ds(8 + d - 2, wide)
            term = weights[2 * d] * tot[f, low, at] + weights[2 * d + 1] * vel[f, low, at]
            total = term if total is None else total + term
        out[base + wide * f : base + wide * (f + 1)] = total
    out[base + 3 * wide : base + 3 * wide + 12] = edges[:, at]


def shares_kernel(wide, vel, tot, weight, edges, *outs):
    groups = len(outs) + 1
    part = vel.shape[2] // groups
    g = lax.axis_index("gz")
    weights = [weight[i] for i in range(10)]
    for shift, out in enumerate(outs, 1):
        begin = lax.rem(g + shift, groups) * part
        for tile in range(part // LANES):
            at = pl.ds(pl.multiple_of(begin + LANES * tile, LANES), LANES)
            store_share(out, wide, tile, at, vel, tot, weights, edges)


def add_share(rhs, wide, firsts, source, piece):
    for k, first in enumerate(firsts):

        @pl.when(source == k)
        def _(first=first):
            for tile in range(rhs.shape[2] // LANES):
                for f in range(3):
                    row = (3 * wide + 12) * tile + wide * f
                    rhs[f, first : first + wide, LANES * tile : LANES * (tile + 1)] += piece[row : row + wide]


def own_kernel(wide, firsts, vel, tot, weight, edges, inv4, fixed, rhs, values, side, started, share):
    lanes = rhs.shape[2]
    blocks = lanes // (2 * LANES)
    g = lax.axis_index("gz")
    weights = [weight[i] for i in range(10)]
    for tile in range(lanes // LANES):
        at = pl.ds(pl.multiple_of(g * lanes + LANES * tile, LANES), LANES)
        store_share(share, wide, tile, at, vel, tot, weights, edges)
        row = (3 * wide + 12) * tile + 3 * wide
        side[:, LANES * tile : LANES * (tile + 1)] = share[row : row + 12]
    rhs[...] = jnp.zeros_like(rhs)
    add_share(rhs, wide, firsts, g, share)
    for f in range(3):
        for r in range(4):
            row = (6 if r < 2 else 0) + 3 * (r % 2) + f
            values[row : row + 1] = jnp.sum(inv4[r] * rhs[f], axis=0, keepdims=True)
    started[...] = jnp.zeros_like(started)
    for b in range(blocks):
        at = FIRST * b
        started[at + STATE + 24 : at + FIRST] = fixed[(MAPS + 16) * b : (MAPS + 16) * (b + 1)]
    started[FIRST * blocks : FIRST * blocks + 16] = fixed[(MAPS + 16) * blocks : (MAPS + 16) * blocks + 16]


def store_planes(ref, at, planes):
    real, imaginary = apart(planes)
    for i in range(planes.shape[0] // 3):
        ref[at + 6 * i : at + 6 * i + 3] = real[3 * i : 3 * i + 3]
        ref[at + 6 * i + 3 : at + 6 * i + 6] = imaginary[3 * i : 3 * i + 3]


def planes_of(ref, at):
    return lambda kind, j: ref[at + 12 * kind + 6 * j : at + 12 * kind + 6 * j + 6]


def relay_kernel(groups, edges, beside_edges, *outs):
    core = lax.rem(lax.axis_index("gy"), 2)
    mine = jnp.where(lax.axis_index("gz") == 0, core == 0, core == 1)
    part = edges.shape[1] // groups
    for step, out in enumerate(outs):
        begin = (2 * step + 1 - core) * part
        for b in range(part // (2 * LANES)):
            at = pl.ds(pl.multiple_of(begin + 2 * LANES * b, 2 * LANES), 2 * LANES)
            row = 12 * (step * (part // LANES) + 2 * b)
            beside = jnp.concatenate([beside_edges[row : row + 12], beside_edges[row + 12 : row + 24]], axis=1)
            store_planes(out, 24 * b, jnp.where(mine, edges[:, at], beside))


def prepare_kernel(inverse, spikes, coef, inv4, fixed, inverse_ends, spike_ends, sems):
    rows, modes = inverse_ends.shape[1:]
    copies = []
    for i, (low, tiles) in enumerate(((0, 0), (rows - 2, rows - 8))):
        source, target = inverse.at[pl.ds(low, 2)], inverse_ends.at[pl.ds(2 * i, 2)]
        copies.append(pltpu.make_async_copy(source, target, sems.at[2 * i]))
        source, target = spikes.at[:, :, pl.ds(tiles, 8)], spike_ends.at[:, :, pl.ds(8 * i, 8)]
        copies.append(pltpu.make_async_copy(source, target, sems.at[2 * i + 1]))
    for copy in copies:
        copy.start()
    core = lax.rem(lax.axis_index("gy"), 2)
    gy, count = lax.axis_index("gy"), lax.axis_size("gy")
    lower, upper = side_weights(coef, False), side_weights(coef, True)
    used = jnp.where(core == 0, gy > 0, gy < count - 1)
    weights = (MAPS + 16) * (modes // LANES)
    for i in range(2):
        for j in range(2):
            for kind in range(2):
                at = weights + 4 * i + 2 * j + kind
                low, high = lower[i][j][kind], upper[i][j][kind]
                fixed[at : at + 1] = jnp.where(core == 0, high, low)
                fixed[at + 8 : at + 9] = jnp.where(used, jnp.where(core == 0, low, high), 0.0)
    for copy in copies:
        copy.wait()
    for b in range(modes // LANES):
        at, lanes = (MAPS + 16) * b, pl.ds(LANES * b, LANES)
        for k in range(2):
            for j in range(2):
                row = at + 2 * k + j
                fixed[row : row + 1] = -spike_ends[0, j, 14 + k : 15 + k, lanes]
                fixed[row + 4 : row + 5] = -spike_ends[0, j, k : k + 1, lanes]
                fixed[row + 8 : row + 9] = -spike_ends[1, j, k : k + 1, lanes]
        for r in range(4):
            inv4[r, :, 2 * LANES * b : 2 * LANES * (b + 1)] = doubled(inverse_ends[r, :, lanes])
            for i in range(2):
                low, high = inverse_ends[r, i : i + 1, lanes], inverse_ends[r, rows - 2 + i : rows - 1 + i, lanes]
                to = at + MAPS + 2 * ((r + 2) % 4) + i
                fixed[to : to + 1] = jnp.where(core == 0, high, low)
                fixed[to + 8 : to + 9] = jnp.where(core == 0, low, high)


def fetch_kernel(inverse, spikes, after, inside, held, sems):
    copies = [pltpu.make_async_copy(inverse, inside, sems.at[0]), pltpu.make_async_copy(spikes, held, sems.at[1])]
    for copy in copies:
        copy.start()
    for copy in copies:
        copy.wait()


def weights_of(ref, at):
    at += ref.shape[0] - 16
    return [
        [[ref[at + 4 * i + 2 * j + kind : at + 4 * i + 2 * j + kind + 1] for kind in range(2)] for j in range(2)]
        for i in range(2)
    ]


def interface_kernel(wide, firsts, inv4, started, own_values, own_side, *refs):
    groups = len(firsts)
    *pieces, message, values, side = refs
    tiles = values.shape[1] // LANES
    g = lax.axis_index("gz")
    core = lax.rem(lax.axis_index("gy"), 2)
    message[...] = started[...]
    values[...] = own_values[...]
    side[...] = own_side[...]
    for shift, piece in enumerate(pieces, 1):
        source = lax.rem(g - shift + groups, groups)
        for k, first in enumerate(firsts):

            @pl.when(source == k)
            def _(piece=piece, first=first):
                for tile in range(tiles):
                    to = pl.ds(LANES * tile, LANES)
                    for f in range(3):
                        row = (3 * wide + 12) * tile + wide * f
                        share = piece[row : row + wide]
                        for r in range(4):
                            row = (6 if r < 2 else 0) + 3 * (r % 2) + f
                            values[row : row + 1, to] += jnp.sum(
                                inv4[r, first : first + wide, to] * share, axis=0, keepdims=True
                            )

        @pl.when(source == jnp.where(core == 0, groups - 1, 0))
        def _(piece=piece):
            for tile in range(tiles):
                row = (3 * wide + 12) * tile + 3 * wide
                side[:, LANES * tile : LANES * (tile + 1)] = piece[row : row + 12]

    for b in range(tiles // 2):
        store_planes(message, FIRST * b, values[:, 2 * LANES * b : 2 * LANES * (b + 1)])
        store_planes(message, FIRST * b + STATE, side[:, 2 * LANES * b : 2 * LANES * (b + 1)])


class Piece:
    def __init__(self, ref, at):
        self.p = [ref[at : at + 6], ref[at + 6 : at + 12]]
        self.q = [ref[at + 12 : at + 18], ref[at + 18 : at + 24]]
        self.F, self.H, self.G = (matrix_of(ref, at + STATE + 4 * i) for i in range(3))


def matrix_of(ref, at):
    return [[ref[at + 2 * k + j : at + 2 * k + j + 1] for j in range(2)] for k in range(2)]


def act(matrix, vector, plus=None):
    out = [matrix[k][0] * vector[0] + matrix[k][1] * vector[1] for k in range(2)]
    return out if plus is None else [plus[k] + out[k] for k in range(2)]


def times(a, b, plus=None):
    out = [[a[k][0] * b[0][j] + a[k][1] * b[1][j] for j in range(2)] for k in range(2)]
    return out if plus is None else [[plus[k][j] + out[k][j] for j in range(2)] for k in range(2)]


def after(state, piece):
    if state is None:
        return piece.p, piece.F
    return act(piece.F, state[0], piece.p), times(piece.F, state[1])


def before(piece, state):
    if state is None:
        return piece.q, piece.H, piece.G
    q, H, G = state
    q = act(piece.G, act(H, piece.p, q), piece.q)
    H = times(piece.G, times(H, piece.F), piece.H)
    return q, H, times(piece.G, G)


def choose(flag, new, old):
    return jax.tree.map(lambda a, b: jnp.where(flag, a, b), new, old)


def store_run(ref, at, p, q, F, H, G):
    for i, vector in enumerate((p, q)):
        for k in range(2):
            ref[at + 12 * i + 6 * k : at + 12 * i + 6 * k + 6] = vector[k]
    for i, matrix in enumerate((F, H, G)):
        for k in range(2):
            for j in range(2):
                row = at + STATE + 4 * i + 2 * k + j
                ref[row : row + 1] = matrix[k][j]


def sort_pieces(base, pieces, board):
    size = len(pieces)
    position = lax.rem(lax.div(lax.axis_index("gy"), base), size)
    for i, piece in enumerate(pieces):
        board[jnp.bitwise_xor(position, (size - i) % size)] = piece[...]
    return position


def compose_kernel(base, *refs):
    *pieces, out, last, board = refs
    sort_pieces(base, pieces, board)
    upper = lax.rem(lax.div(lax.axis_index("gy"), base * len(pieces)), 2) == 1
    for b in range(out.shape[0] // RUN):
        at, to = RUN * b, LAST * b
        run = [Piece(board.at[i], at) for i in range(len(pieces))]
        up = down = None
        for piece in run:
            up = after(up, piece)
        for piece in run[::-1]:
            down = before(piece, down)
        for k in range(2):
            last[to + 6 * k : to + 6 * k + 6] = jnp.where(upper, down[0][k], up[0][k])
            for j in range(2):
                last[to + 12 + 2 * k + j : to + 13 + 2 * k + j] = down[1][k][j]
        store_run(out, at, up[0], down[0], up[1], down[1], down[2])


def ends_kernel(*refs):
    *ends, out = refs
    step = lax.div(lax.axis_index("gz"), 2)
    end = ends[0][...]
    for i in range(1, len(ends)):
        end = jnp.where(step == i, ends[i][...], end)
    out[...] = end


def pair_kernel(mine, other, end_mine, end_other, out, fixed_mine, fixed_other):
    core = lax.rem(lax.axis_index("gy"), 2)
    blocks = out.shape[0] // RUN
    for ref, across, end, target in ((mine, other, end_mine, fixed_mine), (other, mine, end_other, fixed_other)):
        inner_weights, outer_weights = weights_of(ref, 0), weights_of(ref, 8)
        for b in range(blocks):
            at, to = FIRST * b, RUN * b
            inner = beside(inner_weights, planes_of(across, at + STATE))
            outer = beside(outer_weights, planes_of(end, 24 * b))
            target[to + STATE : to + RUN] = ref[at + 48 : at + 48 + MAPS]
            for k in range(4):
                value = ref[at + 6 * k : at + 6 * k + 6]
                for i in range(2):
                    row = at + 48 + MAPS + 2 * k + i
                    value = value + ref[row : row + 1] * inner[i] + ref[row + 8 : row + 9] * outer[i]
                target[to + 6 * k : to + 6 * k + 6] = value
    low = jnp.where(core == 0, fixed_mine[...], fixed_other[...])
    high = jnp.where(core == 0, fixed_other[...], fixed_mine[...])
    for at in range(0, out.shape[0], RUN):
        first, second = Piece(low, at), Piece(high, at)
        up, down = after(after(None, first), second), before(first, before(second, None))
        store_run(out, at, up[0], down[0], up[1], down[1], down[2])


def widen_kernel(base, start, *refs):
    *pieces, out, board = refs
    known_ref = None if start else pieces.pop()
    position = sort_pieces(base, pieces, board)
    for at in range(0, out.shape[0], RUN):
        run = [Piece(board.at[i], at) for i in range(len(pieces))]
        mine = Piece(pieces[0], at)
        one, none = jnp.ones_like(mine.F[0][0]), jnp.zeros_like(mine.F[0][0])
        zero = [jnp.zeros_like(mine.p[0])] * 2
        unit, blank = [[one, none], [none, one]], [[none, none], [none, none]]
        up, down = (zero, unit), (zero, blank, unit)
        for i, piece in enumerate(run[:-1]):
            up = choose(i < position, after(up, piece), up)
        for i in range(len(run) - 1, 0, -1):
            down = choose(i > position, before(run[i], down), down)
        (t, F), (q, H, G) = up, down
        e = act(H, act(mine.F, t, mine.p), q)
        E = times(H, times(mine.F, F))
        if start:
            store_run(out, at, t, e, F, E, G)
        else:
            known = Piece(known_ref, at)
            a, A, b, B, D = known.p, known.F, known.q, known.H, known.G
            store_run(
                out, at, act(A, t, a), act(D, e, act(B, t, b)), times(A, F), times(D, E, times(B, F)), times(D, G)
            )


def block_kernel(wide, firsts, inverse, own_rhs, mine, other, end, *refs):
    *pieces, local, rhs, split = refs
    fields, rows, lanes = rhs.shape
    g = lax.axis_index("gz")
    rhs[...] = own_rhs[...]
    for shift, piece in enumerate(pieces, 1):
        add_share(rhs, wide, firsts, lax.rem(g - shift + len(firsts), len(firsts)), piece)
    core = lax.rem(lax.axis_index("gy"), 2)
    inner_weights, outer_weights = weights_of(mine, 0), weights_of(mine, 8)
    flat = rhs[...].reshape(fields * rows, lanes)
    for b in range(lanes // (2 * LANES)):
        columns = pl.ds(2 * LANES * b, 2 * LANES)
        parts = apart(flat[:, 2 * LANES * b : 2 * LANES * (b + 1)])
        inner = beside(inner_weights, planes_of(other, FIRST * b + STATE))
        outer = beside(outer_weights, planes_of(end, 24 * b))
        solved = []
        for p in range(2):
            split[...] = parts[p].reshape(fields, rows, LANES)
            for f in range(fields):
                for i in range(2):
                    one, two = inner[i][3 * p + f : 3 * p + f + 1], outer[i][3 * p + f : 3 * p + f + 1]
                    split[f, i : i + 1] += jnp.where(core == 0, two, one)
                    split[f, rows - 2 + i : rows - 1 + i] += jnp.where(core == 0, one, two)
            factors = inverse[:, :, LANES * b : LANES * (b + 1)]
            solved.append([jnp.sum(factors * split[f][None], axis=1) for f in range(fields)])
        for f in range(fields):
            local[f, :, columns] = together(solved[0][f], solved[1][f])


def ready_kernel(base, local, spikes, known, ready, lift):
    upper = lax.rem(lax.div(lax.axis_index("gy"), base), 2) == 1
    for b in range(known.shape[0] // RUN):
        columns = pl.ds(2 * LANES * b, 2 * LANES)
        factors = [[doubled(spikes[i, k, :, LANES * b : LANES * (b + 1)]) for k in range(2)] for i in range(2)]
        run = Piece(known, RUN * b)
        maps = doubled(known[RUN * b + STATE : RUN * (b + 1)])
        A, B, D = (matrix_of(maps, 4 * i) for i in range(3))
        t, s = ([together(v[k][0:3], v[k][3:6]) for k in range(2)] for v in (run.p, run.q))
        for f in range(3):
            value = local[f, :, columns]
            for k in range(2):
                value = value - factors[0][k] * t[k][f : f + 1] - factors[1][k] * s[k][f : f + 1]
            ready[f, :, columns] = value
        for j in range(2):
            value = jnp.zeros_like(factors[0][0])
            for k in range(2):
                through_t = factors[0][k] * A[k][j] + factors[1][k] * B[k][j]
                value = value - jnp.where(upper, through_t, factors[1][k] * D[k][j])
            lift[j, :, columns] = value


def final_kernel(base, ready, lift, composed, received, out, held, sems):
    upper = lax.rem(lax.div(lax.axis_index("gy"), base), 2) == 1
    states = []
    for b in range(composed.shape[0] // RUN):
        at, to = RUN * b, LAST * b
        mine = [composed[at : at + 6], composed[at + 6 : at + 12]]
        theirs = [received[to : to + 6], received[to + 6 : to + 12]]
        state = choose(upper, theirs, act(matrix_of(received, to + 12), mine, theirs))
        states.append([together(v[0:3], v[3:6]) for v in state])
    copies = []
    for f in range(3):
        for b, state in enumerate(states):
            columns = pl.ds(2 * LANES * b, 2 * LANES)
            value = ready[f, :, columns]
            for j in range(2):
                value = value + lift[j, :, columns] * state[j][f : f + 1]
            held[f, :, columns] = value
        copies.append(pltpu.make_async_copy(held.at[f], out.at[f], sems.at[f]))
        copies[-1].start()
    for copy in copies:
        copy.wait()


def end_pairs(gy, gz, step):
    at = lambda y, z: y * gz + z
    pairs = []
    for y in range(1, gy - 1, 2):
        for core in range(2):
            column = 2 * step + 1 - core
            pairs.append((at(y - 1 + core, gz - 1), at(y + 1, column)))
            pairs.append((at(y + 1 + core, 0), at(y, column)))
    sources = sorted(set(range(gy * gz)) - {s for s, _ in pairs})
    targets = sorted(set(range(gy * gz)) - {t for _, t in pairs})
    if gz == 2:
        for i in range(0, len(sources), 2):
            (a, b), (c, d) = sources[i : i + 2], targets[i : i + 2]
            pairs += [(a, d), (b, c)] if a != d and b != c else [(a, c), (b, d)]
    return pairs


def groups_of(count):
    steps, base = [(1, 2)], 2
    while 2 * base < count:
        size = 4 if base * 8 <= count else 2
        steps.append((base, size))
        base *= size
    return steps + [(base, 2)]


def per_device(velocity, explicit, bands, inverse, spikes):
    gy, gz = lax.axis_size("gy"), lax.axis_size("gz")
    own, columns = velocity.shape[1:]
    rows, modes = inverse.shape[0], inverse.shape[2]
    lanes = 2 * modes
    wide, firsts = window(rows, own, gz)
    vmem = lambda *shape: pltpu.VMEM(shape, F32)
    dma = lambda n: pltpu.SemaphoreType.DMA((n,))

    blocks = modes // LANES
    to_core = lambda x: lax.ppermute(x, "gy", [(i, i ^ 1) for i in range(gy)])
    padded = (3, rows + 16, columns)
    edges, relayed, coef, weight, vel, tot = vmem_call(
        functools.partial(load_kernel, wide, firsts),
        [(12, columns), (24 * blocks * (gz // 2), LANES), (10, rows, LANES), (10, wide, LANES), padded, padded],
        [velocity, explicit, jnp.transpose(bands, (1, 0, 2))],
        scratch=[vmem(3, own, columns)] * 2 + [vmem(5, 2, rows), vmem(LANES, LANES), dma(3)],
        flops=2 * 10**10,
        name="load",
        far=3,
    )
    beside_edges = to_core(relayed)
    share = ((3 * wide + 12) * 2 * blocks, LANES)
    shares = vmem_call(
        functools.partial(shares_kernel, wide),
        [share] * (gz - 1),
        [vel, tot, weight, edges],
        flops=2 * 10**10,
        name="shares",
    )
    pieces = [
        lax.ppermute(x, "gz", [(i, (i + shift) % gz) for i in range(gz)]) for shift, x in enumerate(shares, 1)
    ]
    relays = vmem_call(
        functools.partial(relay_kernel, gz), [(24 * blocks, LANES)] * (gz // 2), [edges, beside_edges], name="relay"
    )
    ends = [lax.ppermute(x, ("gy", "gz"), end_pairs(gy, gz, step)) for step, x in enumerate(relays)]
    inv4, fixed = vmem_call(
        prepare_kernel,
        [(4, rows, lanes), ((MAPS + 16) * blocks + 16, LANES)],
        [inverse, spikes, coef],
        scratch=[vmem(4, rows, modes), vmem(2, 2, 16, modes), dma(4)],
        flops=2 * 10**10,
        name="prepare",
        far=2,
    )
    first = (FIRST * blocks + 16, LANES)
    rhs, values, side, started = vmem_call(
        functools.partial(own_kernel, wide, firsts),
        [(3, rows, lanes), (12, lanes), (12, lanes), first],
        [vel, tot, weight, edges, inv4, fixed],
        scratch=[vmem(*share)],
        flops=2 * 10**8,
        name="own",
    )
    (message,) = vmem_call(
        functools.partial(interface_kernel, wide, firsts),
        [first],
        [inv4, started, values, side, *pieces],
        scratch=[vmem(12, lanes), vmem(12, lanes)],
        name="interface",
    )
    other = to_core(message)
    (end,) = vmem_call(ends_kernel, [(24 * blocks, LANES)], ends, flops=2 * 10**10, name="ends")
    other_end = to_core(end)
    run = (RUN * blocks, LANES)
    composed, mine, theirs = vmem_call(pair_kernel, [run] * 3, [message, other, end, other_end], name="pair")

    inside, held = vmem_call(
        fetch_kernel,
        [(rows, rows, modes), (2, 2, rows, modes)],
        [inverse, spikes, composed],
        scratch=[dma(2)],
        flops=2 * 10**10,
        name="fetch",
        far=2,
    )
    steps = groups_of(gy)
    base, size = steps[0]
    (known,) = vmem_call(
        functools.partial(widen_kernel, base, True),
        [run],
        [mine, theirs],
        scratch=[vmem(size, *run)],
        flops=10**7,
        name="widen",
    )
    (local,) = vmem_call(
        functools.partial(block_kernel, wide, firsts),
        [(3, rows, lanes)],
        [inside, rhs, message, other, end, *pieces],
        scratch=[vmem(3, rows, lanes), vmem(3, rows, LANES)],
        flops=2 * 10**8,
        name="block",
    )
    for base, size in steps[1:-1]:
        gathered = [composed]
        for x in range(size - 1, 0, -1):
            gathered.append(lax.ppermute(composed, "gy", [(i, i ^ (x * base) ^ 1) for i in range(gy)]))
        board = [vmem(size, *run)]
        composed, last = vmem_call(
            functools.partial(compose_kernel, base),
            [run, (LAST * blocks, LANES)],
            gathered,
            scratch=board,
            name="compose",
        )
        (known,) = vmem_call(
            functools.partial(widen_kernel, base, False),
            [run],
            [*gathered, known],
            scratch=board,
            flops=10**7,
            name="widen",
        )
    base, _ = steps[-1]
    received = lax.ppermute(last, "gy", [(i, i ^ base ^ 1) for i in range(gy)])
    ready, lift = vmem_call(
        functools.partial(ready_kernel, base),
        [(3, rows, lanes), (2, rows, lanes)],
        [local, held, known],
        flops=10**7,
        name="ready",
    )
    (out,) = vmem_call(
        functools.partial(final_kernel, base),
        [(3, rows, lanes)],
        [ready, lift, composed, received],
        scratch=[vmem(3, rows, lanes), dma(3)],
        name="final",
        far_out=True,
    )
    return out


def solution(mesh):
    placed = (
        P(None, ("gy", "gz"), None),
        P(None, ("gy", "gz"), None),
        P(None, None, "gy"),
        P("gy", None, "gz"),
        P(None, None, "gy", "gz"),
    )
    return jax.shard_map(
        per_device, mesh=mesh, in_specs=placed, out_specs=P(None, "gy", "gz"), check_vma=False
    )
```

```python
import functools

import jax
import jax.numpy as jnp
from jax import lax
from jax.experimental import pallas as pl
from jax.experimental.pallas import tpu as pltpu
from jax.sharding import PartitionSpec as P

F32 = jnp.float32
LANES = 128
HALO = 2


def vmem_call(body, out_shapes, args, scratch=(), flops=0, name=None, far=0, far_out=False):
    near, away = pl.BlockSpec(memory_space=pltpu.VMEM), pl.BlockSpec(memory_space=pltpu.HBM)
    nbytes = sum(a.size * 4 for a in args)
    args = [pltpu.with_memory_space_constraint(a, pltpu.HBM) for a in args[:far]] + args[far:]
    return pl.pallas_call(
        body,
        out_shape=[jax.ShapeDtypeStruct(s, F32) for s in out_shapes],
        in_specs=[away] * far + [near] * (len(args) - far),
        out_specs=[away if far_out else near] * len(out_shapes),
        scratch_shapes=list(scratch),
        compiler_params=pltpu.CompilerParams(vmem_limit_bytes=16 * 2**20),
        cost_estimate=pl.CostEstimate(flops=flops, bytes_accessed=nbytes, transcendentals=0),
        name=name,
    )(*args)


def window(rows, own, groups):
    spans = [(max(g * own - HALO, 0), min(g * own + own + HALO, rows)) for g in range(groups)]
    wide = max(high - low for low, high in spans)
    return wide, [min(low, rows - wide) for low, _ in spans]


def lane_of(x):
    return lax.broadcasted_iota(jnp.int32, (x.shape[0], LANES), 1)


def take(x, lanes):
    return jnp.take_along_axis(x, lanes, axis=1, mode="promise_in_bounds")


def apart(x):
    lane = lane_of(x)
    low = lane < LANES // 2
    even = jnp.where(low, 2 * lane, 2 * lane - (LANES - 1))
    odd = jnp.where(low, 2 * lane + 1, 2 * lane - LANES)
    a, b = x[:, :LANES], x[:, LANES:]
    return jnp.where(low, take(a, even), take(b, odd)), jnp.where(low, take(a, odd), take(b, even))


def together(real, imaginary):
    lane = lane_of(real)
    half, odd = lax.shift_right_logical(lane, 1), jnp.bitwise_and(lane, 1) == 1
    parts = [
        jnp.where(odd, take(imaginary, half + at), take(real, half + at)) for at in (0, LANES // 2)
    ]
    return jnp.concatenate(parts, axis=1)


def doubled(x):
    half = lax.shift_right_logical(lane_of(x), 1)
    return jnp.concatenate([take(x, half), take(x, half + LANES // 2)], axis=1)


STATE = 24
MAPS = 12
RUN = STATE + MAPS
FIRST = STATE + 24 + MAPS + 16
LAST = 16


def side_weights(coef, upper):
    rows = coef.shape[1]
    if upper:
        taps = [[(4, rows - 2), None], [(3, rows - 1), (4, rows - 1)]]
    else:
        taps = [[(0, 0), (1, 0)], [None, (0, 1)]]
    none = jnp.zeros((1, LANES), F32)
    get = lambda tap, kind: none if tap is None else coef[2 * tap[0] + kind, tap[1] : tap[1] + 1]
    return [[[get(tap, kind) for kind in range(2)] for tap in row] for row in taps]


def beside(weights, planes):
    return [
        sum(weights[i][j][kind] * planes(kind, j) for j in range(2) for kind in range(2)) for i in range(2)
    ]


def load_kernel(wide, firsts, velocity, explicit, bands, *refs):
    edges, relayed, coef, weight, vel, tot, here, there, taps, square, sems = refs
    groups = len(firsts)
    own = velocity.shape[1]
    rows = coef.shape[1]
    g = lax.axis_index("gz")
    moves = [(bands, taps), (velocity, here), (explicit, there)]
    copies = [pltpu.make_async_copy(source, target, sems.at[i]) for i, (source, target) in enumerate(moves)]
    for copy in copies:
        copy.start()
    square[...] = jnp.zeros_like(square)
    vel[...] = jnp.zeros_like(vel)
    tot[...] = jnp.zeros_like(tot)
    copies[0].wait()
    for d in range(5):
        square[2 * d : 2 * d + 2, 0:rows] = taps[d]
    turned = jnp.transpose(square[...])
    for i in range(10):
        coef[i] = jnp.broadcast_to(turned[0:rows, i : i + 1], (rows, LANES))
    for k in range(groups):

        @pl.when(g == k)
        def _(first=firsts[k]):
            for i in range(10):
                weight[i] = coef[i, first : first + wide]

    copies[1].wait()
    copies[2].wait()
    for k in range(groups):

        @pl.when(g == k)
        def _(base=8 + k * own - firsts[k]):
            for f in range(3):
                vel[f, base : base + own] = here[f]
                tot[f, base : base + own] = here[f] + there[f]

    for f in range(3):
        for j in range(HALO):
            top, bottom = here[f, j : j + 1], here[f, own - HALO + j : own - HALO + j + 1]
            edges[6 + 3 * j + f : 7 + 3 * j + f] = jnp.where(g == 0, top, bottom)
            top += there[f, j : j + 1]
            bottom += there[f, own - HALO + j : own - HALO + j + 1]
            edges[3 * j + f : 3 * j + f + 1] = jnp.where(g == 0, top, bottom)
    core = lax.rem(lax.axis_index("gy"), 2)
    part = edges.shape[1] // groups
    for step in range(groups // 2):
        begin = (2 * step + jnp.where(g == 0, 1 - core, core)) * part
        for tile in range(part // LANES):
            at = pl.ds(pl.multiple_of(begin + LANES * tile, LANES), LANES)
            row = 12 * (step * (part // LANES) + tile)
            relayed[row : row + 12] = edges[:, at]


def stencil(vel, tot, weights, f, wide, at):
    total = None
    for d in range(5):
        low = pl.ds(8 + d - 2, wide)
        term = weights[2 * d] * tot[f, low, at] + weights[2 * d + 1] * vel[f, low, at]
        total = term if total is None else total + term
    return total


def store_share(out, wide, tile, at, vel, tot, weights, edges):
    base = (3 * wide + 12) * tile
    for f in range(3):
        total = None
        for d in range(5):
            low = pl.ds(8 + d - 2, wide)
            term = weights[2 * d] * tot[f, low, at] + weights[2 * d + 1] * vel[f, low, at]
            total = term if total is None else total + term
        out[base + wide * f : base + wide * (f + 1)] = total
    out[base + 3 * wide : base + 3 * wide + 12] = edges[:, at]


def shares_kernel(wide, vel, tot, weight, edges, *outs):
    groups = len(outs) + 1
    part = vel.shape[2] // groups
    g = lax.axis_index("gz")
    weights = [weight[i] for i in range(10)]
    for shift, out in enumerate(outs, 1):
        begin = lax.rem(g + shift, groups) * part
        for tile in range(part // LANES):
            at = pl.ds(pl.multiple_of(begin + LANES * tile, LANES), LANES)
            store_share(out, wide, tile, at, vel, tot, weights, edges)


def add_share(rhs, wide, firsts, source, piece):
    for k, first in enumerate(firsts):

        @pl.when(source == k)
        def _(first=first):
            for tile in range(rhs.shape[2] // LANES):
                for f in range(3):
                    row = (3 * wide + 12) * tile + wide * f
                    rhs[f, first : first + wide, LANES * tile : LANES * (tile + 1)] += piece[row : row + wide]


def own_kernel(wide, firsts, vel, tot, weight, edges, inv4, fixed, rhs, values, side, started, share):
    lanes = rhs.shape[2]
    blocks = lanes // (2 * LANES)
    g = lax.axis_index("gz")
    weights = [weight[i] for i in range(10)]
    for tile in range(lanes // LANES):
        at = pl.ds(pl.multiple_of(g * lanes + LANES * tile, LANES), LANES)
        store_share(share, wide, tile, at, vel, tot, weights, edges)
        row = (3 * wide + 12) * tile + 3 * wide
        side[:, LANES * tile : LANES * (tile + 1)] = share[row : row + 12]
    rhs[...] = jnp.zeros_like(rhs)
    add_share(rhs, wide, firsts, g, share)
    for f in range(3):
        for r in range(4):
            row = (6 if r < 2 else 0) + 3 * (r % 2) + f
            values[row : row + 1] = jnp.sum(inv4[r] * rhs[f], axis=0, keepdims=True)
    started[...] = jnp.zeros_like(started)
    for b in range(blocks):
        at = FIRST * b
        started[at + STATE + 24 : at + FIRST] = fixed[(MAPS + 16) * b : (MAPS + 16) * (b + 1)]
    started[FIRST * blocks : FIRST * blocks + 16] = fixed[(MAPS + 16) * blocks : (MAPS + 16) * blocks + 16]


def store_planes(ref, at, planes):
    real, imaginary = apart(planes)
    for i in range(planes.shape[0] // 3):
        ref[at + 6 * i : at + 6 * i + 3] = real[3 * i : 3 * i + 3]
        ref[at + 6 * i + 3 : at + 6 * i + 6] = imaginary[3 * i : 3 * i + 3]


def planes_of(ref, at):
    return lambda kind, j: ref[at + 12 * kind + 6 * j : at + 12 * kind + 6 * j + 6]


def relay_kernel(groups, edges, beside_edges, *outs):
    core = lax.rem(lax.axis_index("gy"), 2)
    head = lax.axis_index("gz") == 0
    mine = jnp.where(head, core == 0, core == 1)
    part = edges.shape[1] // groups
    for step, out in enumerate(outs):
        begin = (2 * step + jnp.where(head, core, 1 - core)) * part
        for b in range(part // (2 * LANES)):
            at = pl.ds(pl.multiple_of(begin + 2 * LANES * b, 2 * LANES), 2 * LANES)
            row = 12 * (step * (part // LANES) + 2 * b)
            beside = jnp.concatenate([beside_edges[row : row + 12], beside_edges[row + 12 : row + 24]], axis=1)
            store_planes(out, 24 * b, jnp.where(mine, edges[:, at], beside))


def prepare_kernel(inverse, spikes, coef, inv4, fixed, inverse_ends, spike_ends, sems):
    rows, modes = inverse_ends.shape[1:]
    copies = []
    for i, (low, tiles) in enumerate(((0, 0), (rows - 2, rows - 8))):
        source, target = inverse.at[pl.ds(low, 2)], inverse_ends.at[pl.ds(2 * i, 2)]
        copies.append(pltpu.make_async_copy(source, target, sems.at[2 * i]))
        source, target = spikes.at[:, :, pl.ds(tiles, 8)], spike_ends.at[:, :, pl.ds(8 * i, 8)]
        copies.append(pltpu.make_async_copy(source, target, sems.at[2 * i + 1]))
    for copy in copies:
        copy.start()
    core = lax.rem(lax.axis_index("gy"), 2)
    gy, count = lax.axis_index("gy"), lax.axis_size("gy")
    lower, upper = side_weights(coef, False), side_weights(coef, True)
    used = jnp.where(core == 0, gy > 0, gy < count - 1)
    weights = (MAPS + 16) * (modes // LANES)
    for i in range(2):
        for j in range(2):
            for kind in range(2):
                at = weights + 4 * i + 2 * j + kind
                low, high = lower[i][j][kind], upper[i][j][kind]
                fixed[at : at + 1] = jnp.where(core == 0, high, low)
                fixed[at + 8 : at + 9] = jnp.where(used, jnp.where(core == 0, low, high), 0.0)
    for copy in copies:
        copy.wait()
    for b in range(modes // LANES):
        at, lanes = (MAPS + 16) * b, pl.ds(LANES * b, LANES)
        for k in range(2):
            for j in range(2):
                row = at + 2 * k + j
                fixed[row : row + 1] = -spike_ends[0, j, 14 + k : 15 + k, lanes]
                fixed[row + 4 : row + 5] = -spike_ends[0, j, k : k + 1, lanes]
                fixed[row + 8 : row + 9] = -spike_ends[1, j, k : k + 1, lanes]
        for r in range(4):
            inv4[r, :, 2 * LANES * b : 2 * LANES * (b + 1)] = doubled(inverse_ends[r, :, lanes])
            for i in range(2):
                low, high = inverse_ends[r, i : i + 1, lanes], inverse_ends[r, rows - 2 + i : rows - 1 + i, lanes]
                to = at + MAPS + 2 * ((r + 2) % 4) + i
                fixed[to : to + 1] = jnp.where(core == 0, high, low)
                fixed[to + 8 : to + 9] = jnp.where(core == 0, low, high)


def fetch_kernel(inverse, spikes, after, inside, held, sems):
    copies = [pltpu.make_async_copy(inverse, inside, sems.at[0]), pltpu.make_async_copy(spikes, held, sems.at[1])]
    for copy in copies:
        copy.start()
    for copy in copies:
        copy.wait()


def weights_of(ref, at):
    at += ref.shape[0] - 16
    return [
        [[ref[at + 4 * i + 2 * j + kind : at + 4 * i + 2 * j + kind + 1] for kind in range(2)] for j in range(2)]
        for i in range(2)
    ]


def interface_kernel(wide, firsts, inv4, started, own_values, own_side, *refs):
    groups = len(firsts)
    *pieces, message, values, side = refs
    tiles = values.shape[1] // LANES
    g = lax.axis_index("gz")
    core = lax.rem(lax.axis_index("gy"), 2)
    message[...] = started[...]
    values[...] = own_values[...]
    side[...] = own_side[...]
    for shift, piece in enumerate(pieces, 1):
        source = lax.rem(g - shift + groups, groups)
        for k, first in enumerate(firsts):

            @pl.when(source == k)
            def _(piece=piece, first=first):
                for tile in range(tiles):
                    to = pl.ds(LANES * tile, LANES)
                    for f in range(3):
                        row = (3 * wide + 12) * tile + wide * f
                        share = piece[row : row + wide]
                        for r in range(4):
                            row = (6 if r < 2 else 0) + 3 * (r % 2) + f
                            values[row : row + 1, to] += jnp.sum(
                                inv4[r, first : first + wide, to] * share, axis=0, keepdims=True
                            )

        @pl.when(source == jnp.where(core == 0, groups - 1, 0))
        def _(piece=piece):
            for tile in range(tiles):
                row = (3 * wide + 12) * tile + 3 * wide
                side[:, LANES * tile : LANES * (tile + 1)] = piece[row : row + 12]

    for b in range(tiles // 2):
        store_planes(message, FIRST * b, values[:, 2 * LANES * b : 2 * LANES * (b + 1)])
        store_planes(message, FIRST * b + STATE, side[:, 2 * LANES * b : 2 * LANES * (b + 1)])


class Piece:
    def __init__(self, ref, at):
        self.p = [ref[at : at + 6], ref[at + 6 : at + 12]]
        self.q = [ref[at + 12 : at + 18], ref[at + 18 : at + 24]]
        self.F, self.H, self.G = (matrix_of(ref, at + STATE + 4 * i) for i in range(3))


def matrix_of(ref, at):
    return [[ref[at + 2 * k + j : at + 2 * k + j + 1] for j in range(2)] for k in range(2)]


def act(matrix, vector, plus=None):
    out = [matrix[k][0] * vector[0] + matrix[k][1] * vector[1] for k in range(2)]
    return out if plus is None else [plus[k] + out[k] for k in range(2)]


def times(a, b, plus=None):
    out = [[a[k][0] * b[0][j] + a[k][1] * b[1][j] for j in range(2)] for k in range(2)]
    return out if plus is None else [[plus[k][j] + out[k][j] for j in range(2)] for k in range(2)]


def after(state, piece):
    if state is None:
        return piece.p, piece.F
    return act(piece.F, state[0], piece.p), times(piece.F, state[1])


def before(piece, state):
    if state is None:
        return piece.q, piece.H, piece.G
    q, H, G = state
    q = act(piece.G, act(H, piece.p, q), piece.q)
    H = times(piece.G, times(H, piece.F), piece.H)
    return q, H, times(piece.G, G)


def choose(flag, new, old):
    return jax.tree.map(lambda a, b: jnp.where(flag, a, b), new, old)


def store_run(ref, at, p, q, F, H, G):
    for i, vector in enumerate((p, q)):
        for k in range(2):
            ref[at + 12 * i + 6 * k : at + 12 * i + 6 * k + 6] = vector[k]
    for i, matrix in enumerate((F, H, G)):
        for k in range(2):
            for j in range(2):
                row = at + STATE + 4 * i + 2 * k + j
                ref[row : row + 1] = matrix[k][j]


def sort_pieces(base, pieces, board):
    size = len(pieces)
    position = lax.rem(lax.div(lax.axis_index("gy"), base), size)
    for i, piece in enumerate(pieces):
        board[jnp.bitwise_xor(position, (size - i) % size)] = piece[...]
    return position


def compose_kernel(base, *refs):
    *pieces, out, last, board = refs
    sort_pieces(base, pieces, board)
    upper = lax.rem(lax.div(lax.axis_index("gy"), base * len(pieces)), 2) == 1
    for b in range(out.shape[0] // RUN):
        at, to = RUN * b, LAST * b
        run = [Piece(board.at[i], at) for i in range(len(pieces))]
        up = down = None
        for piece in run:
            up = after(up, piece)
        for piece in run[::-1]:
            down = before(piece, down)
        for k in range(2):
            last[to + 6 * k : to + 6 * k + 6] = jnp.where(upper, down[0][k], up[0][k])
            for j in range(2):
                last[to + 12 + 2 * k + j : to + 13 + 2 * k + j] = down[1][k][j]
        store_run(out, at, up[0], down[0], up[1], down[1], down[2])


def ends_kernel(*refs):
    *ends, out = refs
    step = lax.div(lax.axis_index("gz"), 2)
    end = ends[0][...]
    for i in range(1, len(ends)):
        end = jnp.where(step == i, ends[i][...], end)
    out[...] = end


def outer_share(weights, here, end, far_end, b):
    near, far = planes_of(end, 24 * b), planes_of(far_end, 24 * b)
    return beside(weights, lambda kind, j: jnp.where(here, near(kind, j), far(kind, j)))


def pair_kernel(mine, other, end_mine, end_other, out, fixed_mine, fixed_other):
    core = lax.rem(lax.axis_index("gy"), 2)
    here = lax.rem(lax.axis_index("gz"), 2) == 0
    blocks = out.shape[0] // RUN
    for ref, across, end, far_end, target in (
        (mine, other, end_mine, end_other, fixed_mine),
        (other, mine, end_other, end_mine, fixed_other),
    ):
        inner_weights, outer_weights = weights_of(ref, 0), weights_of(ref, 8)
        for b in range(blocks):
            at, to = FIRST * b, RUN * b
            inner = beside(inner_weights, planes_of(across, at + STATE))
            outer = outer_share(outer_weights, here, end, far_end, b)
            target[to + STATE : to + RUN] = ref[at + 48 : at + 48 + MAPS]
            for k in range(4):
                value = ref[at + 6 * k : at + 6 * k + 6]
                for i in range(2):
                    row = at + 48 + MAPS + 2 * k + i
                    value = value + ref[row : row + 1] * inner[i] + ref[row + 8 : row + 9] * outer[i]
                target[to + 6 * k : to + 6 * k + 6] = value
    low = jnp.where(core == 0, fixed_mine[...], fixed_other[...])
    high = jnp.where(core == 0, fixed_other[...], fixed_mine[...])
    for at in range(0, out.shape[0], RUN):
        first, second = Piece(low, at), Piece(high, at)
        up, down = after(after(None, first), second), before(first, before(second, None))
        store_run(out, at, up[0], down[0], up[1], down[1], down[2])


def widen_kernel(base, start, *refs):
    *pieces, out, board = refs
    known_ref = None if start else pieces.pop()
    position = sort_pieces(base, pieces, board)
    for at in range(0, out.shape[0], RUN):
        run = [Piece(board.at[i], at) for i in range(len(pieces))]
        mine = Piece(pieces[0], at)
        one, none = jnp.ones_like(mine.F[0][0]), jnp.zeros_like(mine.F[0][0])
        zero = [jnp.zeros_like(mine.p[0])] * 2
        unit, blank = [[one, none], [none, one]], [[none, none], [none, none]]
        up, down = (zero, unit), (zero, blank, unit)
        for i, piece in enumerate(run[:-1]):
            up = choose(i < position, after(up, piece), up)
        for i in range(len(run) - 1, 0, -1):
            down = choose(i > position, before(run[i], down), down)
        (t, F), (q, H, G) = up, down
        e = act(H, act(mine.F, t, mine.p), q)
        E = times(H, times(mine.F, F))
        if start:
            store_run(out, at, t, e, F, E, G)
        else:
            known = Piece(known_ref, at)
            a, A, b, B, D = known.p, known.F, known.q, known.H, known.G
            store_run(
                out, at, act(A, t, a), act(D, e, act(B, t, b)), times(A, F), times(D, E, times(B, F)), times(D, G)
            )


def block_kernel(wide, firsts, inverse, own_rhs, mine, other, end, far_end, *refs):
    *pieces, local, rhs, split = refs
    fields, rows, lanes = rhs.shape
    g = lax.axis_index("gz")
    rhs[...] = own_rhs[...]
    for shift, piece in enumerate(pieces, 1):
        add_share(rhs, wide, firsts, lax.rem(g - shift + len(firsts), len(firsts)), piece)
    core = lax.rem(lax.axis_index("gy"), 2)
    inner_weights, outer_weights = weights_of(mine, 0), weights_of(mine, 8)
    flat = rhs[...].reshape(fields * rows, lanes)
    for b in range(lanes // (2 * LANES)):
        columns = pl.ds(2 * LANES * b, 2 * LANES)
        parts = apart(flat[:, 2 * LANES * b : 2 * LANES * (b + 1)])
        inner = beside(inner_weights, planes_of(other, FIRST * b + STATE))
        outer = outer_share(outer_weights, lax.rem(g, 2) == 0, end, far_end, b)
        solved = []
        for p in range(2):
            split[...] = parts[p].reshape(fields, rows, LANES)
            for f in range(fields):
                for i in range(2):
                    one, two = inner[i][3 * p + f : 3 * p + f + 1], outer[i][3 * p + f : 3 * p + f + 1]
                    split[f, i : i + 1] += jnp.where(core == 0, two, one)
                    split[f, rows - 2 + i : rows - 1 + i] += jnp.where(core == 0, one, two)
            factors = inverse[:, :, LANES * b : LANES * (b + 1)]
            solved.append([jnp.sum(factors * split[f][None], axis=1) for f in range(fields)])
        for f in range(fields):
            local[f, :, columns] = together(solved[0][f], solved[1][f])


def ready_kernel(base, local, spikes, known, ready, lift):
    upper = lax.rem(lax.div(lax.axis_index("gy"), base), 2) == 1
    for b in range(known.shape[0] // RUN):
        columns = pl.ds(2 * LANES * b, 2 * LANES)
        factors = [[doubled(spikes[i, k, :, LANES * b : LANES * (b + 1)]) for k in range(2)] for i in range(2)]
        run = Piece(known, RUN * b)
        maps = doubled(known[RUN * b + STATE : RUN * (b + 1)])
        A, B, D = (matrix_of(maps, 4 * i) for i in range(3))
        t, s = ([together(v[k][0:3], v[k][3:6]) for k in range(2)] for v in (run.p, run.q))
        for f in range(3):
            value = local[f, :, columns]
            for k in range(2):
                value = value - factors[0][k] * t[k][f : f + 1] - factors[1][k] * s[k][f : f + 1]
            ready[f, :, columns] = value
        for j in range(2):
            value = jnp.zeros_like(factors[0][0])
            for k in range(2):
                through_t = factors[0][k] * A[k][j] + factors[1][k] * B[k][j]
                value = value - jnp.where(upper, through_t, factors[1][k] * D[k][j])
            lift[j, :, columns] = value


def final_kernel(base, ready, lift, composed, received, out, held, sems):
    upper = lax.rem(lax.div(lax.axis_index("gy"), base), 2) == 1
    states = []
    for b in range(composed.shape[0] // RUN):
        at, to = RUN * b, LAST * b
        mine = [composed[at : at + 6], composed[at + 6 : at + 12]]
        theirs = [received[to : to + 6], received[to + 6 : to + 12]]
        state = choose(upper, theirs, act(matrix_of(received, to + 12), mine, theirs))
        states.append([together(v[0:3], v[3:6]) for v in state])
    copies = []
    for f in range(3):
        for b, state in enumerate(states):
            columns = pl.ds(2 * LANES * b, 2 * LANES)
            value = ready[f, :, columns]
            for j in range(2):
                value = value + lift[j, :, columns] * state[j][f : f + 1]
            held[f, :, columns] = value
        copies.append(pltpu.make_async_copy(held.at[f], out.at[f], sems.at[f]))
        copies[-1].start()
    for copy in copies:
        copy.wait()


def end_pairs(gy, gz, step):
    at = lambda y, z: y * gz + z
    pairs = []
    for y in range(gy - 2):
        core = y % 2
        pairs.append((at(y, gz - 1), at((y + 2) ^ 1, 2 * step + 1 - core)))
        pairs.append((at(y + 2, 0), at(y ^ 1, 2 * step + core)))
    sources = sorted(set(range(gy * gz)) - {s for s, _ in pairs})
    targets = sorted(set(range(gy * gz)) - {t for _, t in pairs})
    if gz == 2:
        for i in range(0, len(sources), 2):
            (a, b), (c, d) = sources[i : i + 2], targets[i : i + 2]
            pairs += [(a, d), (b, c)] if a != d and b != c else [(a, c), (b, d)]
    return pairs


def groups_of(count):
    steps, base = [(1, 2)], 2
    while 2 * base < count:
        size = 4 if base * 8 <= count else 2
        steps.append((base, size))
        base *= size
    return steps + [(base, 2)]


def per_device(velocity, explicit, bands, inverse, spikes):
    gy, gz = lax.axis_size("gy"), lax.axis_size("gz")
    own, columns = velocity.shape[1:]
    rows, modes = inverse.shape[0], inverse.shape[2]
    lanes = 2 * modes
    wide, firsts = window(rows, own, gz)
    vmem = lambda *shape: pltpu.VMEM(shape, F32)
    dma = lambda n: pltpu.SemaphoreType.DMA((n,))

    blocks = modes // LANES
    to_core = lambda x: lax.ppermute(x, "gy", [(i, i ^ 1) for i in range(gy)])
    padded = (3, rows + 16, columns)
    edges, relayed, coef, weight, vel, tot = vmem_call(
        functools.partial(load_kernel, wide, firsts),
        [(12, columns), (24 * blocks * (gz // 2), LANES), (10, rows, LANES), (10, wide, LANES), padded, padded],
        [velocity, explicit, jnp.transpose(bands, (1, 0, 2))],
        scratch=[vmem(3, own, columns)] * 2 + [vmem(5, 2, rows), vmem(LANES, LANES), dma(3)],
        flops=2 * 10**10,
        name="load",
        far=3,
    )
    beside_edges = to_core(relayed)
    share = ((3 * wide + 12) * 2 * blocks, LANES)
    shares = vmem_call(
        functools.partial(shares_kernel, wide),
        [share] * (gz - 1),
        [vel, tot, weight, edges],
        flops=2 * 10**10,
        name="shares",
    )
    pieces = [
        lax.ppermute(x, "gz", [(i, (i + shift) % gz) for i in range(gz)]) for shift, x in enumerate(shares, 1)
    ]
    relays = vmem_call(
        functools.partial(relay_kernel, gz), [(24 * blocks, LANES)] * (gz // 2), [edges, beside_edges], name="relay"
    )
    ends = [lax.ppermute(x, ("gy", "gz"), end_pairs(gy, gz, step)) for step, x in enumerate(relays)]
    inv4, fixed = vmem_call(
        prepare_kernel,
        [(4, rows, lanes), ((MAPS + 16) * blocks + 16, LANES)],
        [inverse, spikes, coef],
        scratch=[vmem(4, rows, modes), vmem(2, 2, 16, modes), dma(4)],
        flops=2 * 10**10,
        name="prepare",
        far=2,
    )
    first = (FIRST * blocks + 16, LANES)
    rhs, values, side, started = vmem_call(
        functools.partial(own_kernel, wide, firsts),
        [(3, rows, lanes), (12, lanes), (12, lanes), first],
        [vel, tot, weight, edges, inv4, fixed],
        scratch=[vmem(*share)],
        flops=2 * 10**8,
        name="own",
    )
    (message,) = vmem_call(
        functools.partial(interface_kernel, wide, firsts),
        [first],
        [inv4, started, values, side, *pieces],
        scratch=[vmem(12, lanes), vmem(12, lanes)],
        name="interface",
    )
    other = to_core(message)
    (end,) = vmem_call(ends_kernel, [(24 * blocks, LANES)], ends, flops=2 * 10**10, name="ends")
    other_end = to_core(end)
    run = (RUN * blocks, LANES)
    composed, mine, theirs = vmem_call(pair_kernel, [run] * 3, [message, other, end, other_end], name="pair")

    inside, held = vmem_call(
        fetch_kernel,
        [(rows, rows, modes), (2, 2, rows, modes)],
        [inverse, spikes, composed],
        scratch=[dma(2)],
        flops=2 * 10**10,
        name="fetch",
        far=2,
    )
    steps = groups_of(gy)
    base, size = steps[0]
    (known,) = vmem_call(
        functools.partial(widen_kernel, base, True),
        [run],
        [mine, theirs],
        scratch=[vmem(size, *run)],
        flops=10**7,
        name="widen",
    )
    (local,) = vmem_call(
        functools.partial(block_kernel, wide, firsts),
        [(3, rows, lanes)],
        [inside, rhs, message, other, end, other_end, *pieces],
        scratch=[vmem(3, rows, lanes), vmem(3, rows, LANES)],
        flops=2 * 10**8,
        name="block",
    )
    for base, size in steps[1:-1]:
        gathered = [composed]
        for x in range(size - 1, 0, -1):
            gathered.append(lax.ppermute(composed, "gy", [(i, i ^ (x * base) ^ 1) for i in range(gy)]))
        board = [vmem(size, *run)]
        composed, last = vmem_call(
            functools.partial(compose_kernel, base),
            [run, (LAST * blocks, LANES)],
            gathered,
            scratch=board,
            name="compose",
        )
        (known,) = vmem_call(
            functools.partial(widen_kernel, base, False),
            [run],
            [*gathered, known],
            scratch=board,
            flops=10**7,
            name="widen",
        )
    base, _ = steps[-1]
    received = lax.ppermute(last, "gy", [(i, i ^ base ^ 1) for i in range(gy)])
    ready, lift = vmem_call(
        functools.partial(ready_kernel, base),
        [(3, rows, lanes), (2, rows, lanes)],
        [local, held, known],
        flops=10**7,
        name="ready",
    )
    (out,) = vmem_call(
        functools.partial(final_kernel, base),
        [(3, rows, lanes)],
        [ready, lift, composed, received],
        scratch=[vmem(3, rows, lanes), dma(3)],
        name="final",
        far_out=True,
    )
    return out


def solution(mesh):
    placed = (
        P(None, ("gy", "gz"), None),
        P(None, ("gy", "gz"), None),
        P(None, None, "gy"),
        P("gy", None, "gz"),
        P(None, None, "gy", "gz"),
    )
    return jax.shard_map(
        per_device, mesh=mesh, in_specs=placed, out_specs=P(None, "gy", "gz"), check_vma=False
    )
```
